32 devices in a mesh: dp: 4 (over y, x), fsdp: 8 (over z, core).
Axes of the slice: x: 2, y: 2, z: 4, core: 2. Of those that a mesh axis runs over, the one named last changes fastest.
Arguments:
- tokens: bfloat16 [65536, 512], P(('dp', 'fsdp')), may hold values from -6 to 6
- present: int32 [65536], P(('dp', 'fsdp')), may hold values 0 or 1
- lengths: int32 [32, 4], P(('dp', 'fsdp')), may hold values from 1 to 1024, 2048 in all within a row
- conv_w: bfloat16 [4608, 512], P(('dp', 'fsdp')), may hold values from -0.09375 to 0.09375
- conv_b: bfloat16 [512], P(('dp', 'fsdp')), may hold values from -3 to 3
- gain_one: bfloat16 [512], P(('dp', 'fsdp')), may hold values from 0.099609375 to 1.8984375
- shift_one: bfloat16 [512], P(('dp', 'fsdp')), may hold values from -2 to 2
- w_in: bfloat16 [512, 2048], P(('dp', 'fsdp')), may hold values from -0.25 to 0.25
- b_in: bfloat16 [2048], P(('dp', 'fsdp')), may hold values from -3 to 3
- w_out: bfloat16 [2048, 512], P(('dp', 'fsdp')), may hold values from -0.125 to 0.125
- b_out: bfloat16 [512], P(('dp', 'fsdp')), may hold values from -3 to 3
- gain_two: bfloat16 [512], P(('dp', 'fsdp')), may hold values from 0.099609375 to 1.8984375
- shift_two: bfloat16 [512], P(('dp', 'fsdp')), may hold values from -2 to 2
- cotangent: bfloat16 [65536, 512], P(('dp', 'fsdp')), may hold values from -6 to 6
Outputs:
- mixed: bfloat16 [65536, 512], P(('dp', 'fsdp'))
- d_tokens: float32 [65536, 512], P(('dp', 'fsdp'))
- d_conv_w: float32 [4608, 512], P(('dp', 'fsdp'))
- d_conv_b: float32 [512], P(('dp', 'fsdp'))
- d_gain_one: float32 [512], P(('dp', 'fsdp'))
- d_shift_one: float32 [512], P(('dp', 'fsdp'))
- d_w_in: float32 [512, 2048], P(('dp', 'fsdp'))
- d_b_in: float32 [2048], P(('dp', 'fsdp'))
- d_w_out: float32 [2048, 512], P(('dp', 'fsdp'))
- d_b_out: float32 [512], P(('dp', 'fsdp'))
- d_gain_two: float32 [512], P(('dp', 'fsdp'))
- d_shift_two: float32 [512], P(('dp', 'fsdp'))
The draws below stay inside these ranges and needn't reach their ends.
Inputs may be any that keep to these rules, and one draw needn't show every extreme that they name: Each row gives the lengths of the 4 windows that fill one device's 2048 rows end to end, in order; they sum to 2048 and one of them is 1024.
All inputs are finite; a program needn't handle non-finite values. No bound on the sum of `present` on one device may be relied on, other than what follows from the above.
Results may differ from the reference program's by a relative error of at most 0.0064.
Values may be sent and summed in bfloat16 or wider, within the bound.
No kernel may reach another device: no remote copies, remote signals or barrier semaphores. Data moves between devices by JAX's collectives and lax.ppermute only.
A program may use at most 192 MiB of HBM per device.

```python
import math
import jax
import jax.numpy as jnp
import numpy as np
from jax import lax

D = 512
FF = 2048
KERNEL_TAPS = 9
DILATION_STEP = 8
ROWS = 2048
WINS = 4
MOST = 1024
TOKENS = 65536
N_DP = 4
N_FSDP = 8


def plant(entries, key, least, largest):
    place = [jax.random.randint(jax.random.fold_in(key, axis), (), 0, length) for axis, length in enumerate(entries.shape)]
    longest = entries.shape.index(max(entries.shape))
    beside = place[:longest] + [(place[longest] + 1) % entries.shape[longest]] + place[longest + 1:]
    return entries.at[tuple(place)].set(least).at[tuple(beside)].set(largest)


def strengthened(result, stream_key, source, target, shards_of, factor):
    owner, partner = [(jnp.arange(result.shape[dim]) // (result.shape[dim] // shards_of)).reshape([-1 if axis == dim else 1 for axis in range(result.ndim)]) for dim in (source, target)]
    chosen = jax.random.permutation(stream_key, shards_of)[partner]
    strong = (owner == chosen) | (owner == (partner + shards_of // 2) % shards_of)
    return jnp.where(strong, factor * result, result)


def block_scale(own_key, shape, cuts, low, high):
    gain = 1.0
    for position, blocks in cuts:
        draws = jax.random.uniform(jax.random.fold_in(jax.random.fold_in(own_key, 6), position), (blocks,), jnp.float32, low / len(cuts), high / len(cuts))
        gain = gain * jnp.repeat(jnp.exp(draws), shape[position] // blocks).reshape((-1,) + (1,) * (len(shape) - 1 - position))
    return gain


def profile(amount, total, bound, skew):
    weights = [(1 << 20) // math.isqrt(grade ** skew) + 1 for grade in range(2, amount + 1)]
    spare, given = total - bound - (amount - 1), [1] * (amount - 1)
    while spare > 0:
        candidates = [i for i in range(amount - 1) if given[i] < bound]
        pool, budget = sum([weights[i] for i in candidates]), spare
        for i in candidates:
            extra = min(bound - given[i], max(1, budget * weights[i] // pool), spare)
            given[i] = given[i] + extra
            spare = spare - extra
    return np.array([bound] + given)


def uneven_parts(stream_key, amount, total, bound, lean):
    if amount == 2:
        one = jax.random.randint(stream_key, (), max(1, total - bound), min(bound, total - 1) + 1)
        return jnp.stack([one, total - one])
    sizes = jnp.asarray(profile(amount, total, bound, lean), jnp.int32)
    pairs = (amount - 1) // 2
    source_of, taker = sizes[1:1 + 2 * pairs:2], sizes[2:2 + 2 * pairs:2]
    room = jnp.minimum(source_of - 1, bound - taker)
    moved = jax.random.randint(jax.random.fold_in(stream_key, 1), (pairs,), 0, 1 << 20) % (room + 1)
    sizes = sizes.at[1:1 + 2 * pairs:2].set(source_of - moved).at[2:2 + 2 * pairs:2].set(taker + moved)
    return sizes[jax.random.permutation(jax.random.fold_in(stream_key, 2), amount)]


def noise(rng, dims, deviation, reach, cuts=(), kind=jnp.bfloat16):
    values = jax.random.normal(rng, dims, jnp.float32) * deviation
    if len(cuts) > 0:
        values = block_scale(rng, dims, cuts, -0.22, 0.18) * values
    return jnp.clip(values, min=-reach, max=reach).astype(kind)


def noise_with(stream_key, extent, spread, reach, split, heavy, kind=jnp.bfloat16):
    entries = spread * jax.random.normal(stream_key, extent, jnp.float32)
    if split:
        entries = entries * block_scale(stream_key, extent, split, -0.22, 0.18)
    return jnp.clip(strengthened(entries, jax.random.fold_in(stream_key, 3), *heavy), -reach, reach).astype(kind)


def setup_inputs(seed: int = 0) -> dict:
    keys = jax.random.split(jax.random.key(seed), 15)
    tokens = noise_with(keys[0], (TOKENS, D), 1.0, 6.0, ((0, 32),), (0, 1, 32, 2.75))
    present = plant((jax.random.randint(keys[1], (TOKENS,), 0, 8) < 7).astype(jnp.int32), jax.random.fold_in(keys[1], 1), 0, 1)
    lengths = jax.vmap(lambda own: uneven_parts(own, WINS, ROWS, MOST, 2))(jax.random.split(keys[2], (N_DP * N_FSDP))).reshape((N_DP * N_FSDP, WINS)).astype(jnp.int32)
    conv_w = noise(keys[3], (KERNEL_TAPS * D, D), (KERNEL_TAPS * D) ** -0.5, 0.09375, ((0, 32),))
    conv_b = noise(keys[4], (D,), 0.5, 3.0, ((0, 32),))
    gain_one = jnp.clip(1.0 + 0.18 * jax.random.normal(keys[5], (D,), jnp.float32), 0.099609375, 1.8984375).astype(jnp.bfloat16)
    shift_one = noise(keys[6], (D,), 0.3, 2.0, ((0, 32),))
    w_in = noise(keys[7], (D, FF), D ** -0.5, 0.25, ((0, 32),))
    b_in = noise(keys[8], (FF,), 0.5, 3.0, ((0, 32),))
    w_out = noise(keys[9], (FF, D), FF ** -0.5, 0.125, ((0, 32),))
    b_out = noise(keys[10], (D,), 0.5, 3.0, ((0, 32),))
    gain_two = jnp.clip(1.0 + 0.18 * jax.random.normal(keys[11], (D,), jnp.float32), 0.099609375, 1.8984375).astype(jnp.bfloat16)
    shift_two = noise(keys[12], (D,), 0.3, 2.0, ((0, 32),))
    cotangent = noise(keys[13], (TOKENS, D), 1.0, 6.0, ((0, 32),))
    return {"tokens": tokens, "present": present, "lengths": lengths, "conv_w": conv_w, "conv_b": conv_b, "gain_one": gain_one, "shift_one": shift_one, "w_in": w_in, "b_in": b_in, "w_out": w_out, "b_out": b_out, "gain_two": gain_two, "shift_two": shift_two, "cotangent": cotangent}


@jax.custom_vjp
def low(v):
    return lax.optimization_barrier(v.astype(jnp.bfloat16)).astype(jnp.float32)

@jax.custom_vjp
def low_back(v):
    return v

def low_keep(v):
    return (low(v), None)

def low_pass(kept, grad):
    return (grad,)

def back_keep(v):
    return (v, None)

def back_low(kept, grad):
    return (low(grad),)
low.defvjp(low_keep, low_pass)
low_back.defvjp(back_keep, back_low)
EPSILON = 1e-05
HIGHEST = lax.Precision.HIGHEST

def layer_norm(values, scales, offset):
    center = lax.optimization_barrier(jnp.mean(values, axis=-1, keepdims=True))
    shifted = values - center
    second = lax.optimization_barrier(jnp.mean(shifted * shifted, axis=-1, keepdims=True))
    return shifted * lax.rsqrt(second + EPSILON) * scales + offset

def tap_masks(length_row, row_count):
    window_ends = jnp.cumsum(length_row).astype(jnp.int32)
    window_starts = (window_ends - length_row).astype(jnp.int32)
    token_position = jnp.arange(row_count, dtype=jnp.int32)
    inside = (token_position[:, None] >= window_starts[None, :]) & (token_position[:, None] < window_ends[None, :])
    first_row = lax.optimization_barrier(jnp.sum(jnp.where(inside, window_starts[None, :], 0), axis=1))
    last_row = lax.optimization_barrier(jnp.sum(jnp.where(inside, window_ends[None, :], 0), axis=1))
    tap_valid = []
    for kernel_tap_index in range(KERNEL_TAPS):
        target_position = token_position + (kernel_tap_index - KERNEL_TAPS // 2) * DILATION_STEP
        tap_valid.append((target_position >= first_row) & (target_position < last_row))
    return jnp.stack(tap_valid)

def shifted_stack(values, tap_valid):
    receptive_reach = KERNEL_TAPS // 2 * DILATION_STEP
    row_count = values.shape[0]
    padded = jnp.pad(values, ((receptive_reach, receptive_reach), (0, 0)))
    pieces = []
    for kernel_tap_index in range(KERNEL_TAPS):
        window_begin = kernel_tap_index * DILATION_STEP
        window = padded[window_begin:window_begin + row_count]
        pieces.append(jnp.where(tap_valid[kernel_tap_index][:, None], window, jnp.zeros_like(window)))
    return jnp.concatenate(pieces, axis=1)

def block_forward(inputs, keep_rows, length_row, conv_w, conv_b, gain_one, shift_one, w_in, b_in, w_out, b_out, gain_two, shift_two):
    tap_valid = tap_masks(length_row, inputs.shape[0])
    masked = inputs * keep_rows[:, None]
    stacked = shifted_stack(masked, tap_valid)
    conv = low_back(jnp.dot(stacked, conv_w, precision=HIGHEST) + conv_b)
    hidden = low(inputs + layer_norm(jax.nn.gelu(conv, approximate=False), gain_one, shift_one))
    inner = low_back(jnp.dot(hidden, w_in, precision=HIGHEST) + b_in)
    active = low(jax.nn.gelu(inner, approximate=False))
    outer = low_back(jnp.dot(active, w_out, precision=HIGHEST) + b_out)
    return hidden + layer_norm(outer, gain_two, shift_two)

def reference(tokens, present, lengths, conv_w, conv_b, gain_one, shift_one, w_in, b_in, w_out, b_out, gain_two, shift_two, cotangent):
    groups = TOKENS // ROWS
    params = tuple((item.astype(jnp.float32) for item in (conv_w, conv_b, gain_one, shift_one, w_in, b_in, w_out, b_out, gain_two, shift_two)))
    inputs = tokens.astype(jnp.float32).reshape(groups, ROWS, D)
    keep_rows = present.astype(jnp.float32).reshape(groups, ROWS)
    upstream = cotangent.astype(jnp.float32).reshape(groups, ROWS, D)
    checked = jax.checkpoint(block_forward)

    def whole(all_inputs, *weights):

        def one_group(item):
            return checked(item[0], item[1], item[2], *weights)
        return lax.map(one_group, (all_inputs, keep_rows, lengths))
    output, pullback = jax.vjp(whole, inputs, *params)
    grads = pullback(upstream)
    return (output.reshape(TOKENS, D).astype(jnp.bfloat16), grads[0].reshape(TOKENS, D), grads[1], grads[2], grads[3], grads[4], grads[5], grads[6], grads[7], grads[8], grads[9], grads[10])
```

```python
import functools
import jax
import jax.numpy as jnp
from jax import lax
from jax.experimental import pallas as pl
from jax.experimental.pallas import tpu as pltpu
from jax.sharding import PartitionSpec as P

TAPS = 9
STEP = 8
REACH = (TAPS // 2) * STEP
EPSILON = 1e-05
AXES = ("dp", "fsdp")
f32 = jnp.float32
bf16 = jnp.bfloat16
ANY = pl.BlockSpec(memory_space=pl.ANY)
SMEM = pl.BlockSpec(memory_space=pltpu.SMEM)


def dot(a, b):
    return jnp.dot(a, b, preferred_element_type=f32)


def dot_t(a, b):
    return lax.dot_general(a, b, (((1,), (1,)), ((), ())), preferred_element_type=f32)


def dot_rows(a, b):
    return lax.dot_general(a, b, (((0,), (0,)), ((), ())), preferred_element_type=f32)


def gelu_pair(v):
    t = pl.reciprocal(1.0 + 0.23164190 * jnp.abs(v))
    e = jnp.exp(-0.5 * v * v)
    poly = t * (0.127414796 + t * (-0.142248368 + t * (0.7107068705 + t * (-0.7265760135 + t * 0.5307027145))))
    tail = poly * e
    phi = jnp.where(v >= 0.0, 1.0 - tail, tail)
    return v * phi, phi + v * (e * 0.3989422804014327)


def mean(v):
    return jnp.mean(v, axis=-1, keepdims=True)


def colsum(v):
    return jnp.sum(v, axis=0, keepdims=True)


def vmem(mib):
    return pltpu.CompilerParams(vmem_limit_bytes=mib << 20)


def cost(macs, nbytes):
    return pl.CostEstimate(flops=2 * macs, bytes_accessed=nbytes, transcendentals=0)


def whole(shape):
    return pl.BlockSpec(shape, lambda *_: (0,) * len(shape), pipeline_mode=pl.Buffered(1))


def rows_of(tile, width):
    return pl.BlockSpec((tile, width), lambda i: (i, 0))


def window_bounds(len_ref, position, wins, total):
    first = jnp.zeros_like(position)
    last = jnp.full_like(position, total)
    edge = jnp.int32(0)
    edges = []
    for w in range(wins - 1):
        edge = edge + len_ref[0, w]
        edges.append(edge)
    for edge in edges:
        first = jnp.where(position >= edge, edge, first)
    for edge in reversed(edges):
        last = jnp.where(position < edge, edge, last)
    return first, last


def wide(mask, width):
    return jnp.concatenate([mask] * (width // 128), axis=1)


def prep_kernel(len_ref, tokens_ref, keep_ref, stacked_ref, masked_ref, padded, *, tile, wins):
    step = pl.program_id(0)
    rows, width = tokens_ref.shape

    @pl.when(step == 0)
    def _():
        padded[:REACH] = jnp.zeros((REACH, width), f32)
        padded[rows + REACH :] = jnp.zeros((REACH, width), f32)
        for r in range(0, rows, tile):
            padded[REACH + r : REACH + r + tile] = tokens_ref[r : r + tile].astype(f32) * wide(keep_ref[r : r + tile], width)

    start = pl.multiple_of(step * tile, tile)
    masked_ref[...] = padded[pl.ds(start + REACH, tile)].astype(bf16)
    position = lax.broadcasted_iota(jnp.int32, (tile, 128), 0) + start
    first, last = window_bounds(len_ref, position, wins, rows)
    for tap in range(TAPS):
        other = position + (tap - TAPS // 2) * STEP
        valid = ((other >= first) & (other < last)).astype(f32)
        block = padded[pl.ds(pl.multiple_of(start + tap * STEP, STEP), tile)] * wide(valid, width)
        stacked_ref[:, tap * width : (tap + 1) * width] = block.astype(bf16)


def prep(lengths, tokens, keep):
    rows, width = tokens.shape
    tile = 256
    return pl.pallas_call(
        functools.partial(prep_kernel, tile=tile, wins=lengths.shape[1]),
        grid=(rows // tile,),
        in_specs=[SMEM, whole((rows, width)), whole((rows, 128))],
        out_specs=[rows_of(tile, TAPS * width), rows_of(tile, width)],
        out_shape=[
            jax.ShapeDtypeStruct((rows, TAPS * width), bf16),
            jax.ShapeDtypeStruct((rows, width), bf16),
        ],
        scratch_shapes=[pltpu.VMEM((rows + 2 * REACH, width), f32)],
        compiler_params=vmem(60),
        cost_estimate=cost(0, 24 * rows * width),
        name="prep",
    )(lengths, tokens, keep)


def place_halves(mine, other, core, blocks, body, store, sems):
    copies = []
    for source, which in ((mine, core), (other, 1 - core)):
        for block in range(blocks):
            start = pl.multiple_of((2 * block + which) * body, 16)
            copies.append(
                pltpu.make_async_copy(
                    source.at[block, pl.ds(0, body)], store.at[pl.ds(start, body)], sems.at[len(copies)]
                )
            )
    return copies


def conv_kernel(
    core_ref, mine, other, stacked_ref, tokens_ref, hidden_ref, normed_ref, slope_ref, small_ref, store, small, sems, *, blocks, body, extra
):
    core = core_ref[0]

    @pl.when(pl.program_id(0) == 0)
    def _():
        copies = place_halves(mine, other, core, blocks, body, store, sems)
        for n, source in enumerate((mine, other)):
            copies.append(
                pltpu.make_async_copy(source.at[:, pl.ds(body, extra)], small.at[n], sems.at[2 * blocks + n])
            )
        for copy in copies:
            copy.start()
        for copy in copies:
            copy.wait()
        small_ref[...] = jnp.sum(small[...].astype(f32), axis=(0, 1))

    conv = dot(stacked_ref[...], store[...]) + small_ref[0:1]
    bent, bend = gelu_pair(conv)
    center = mean(bent)
    shifted = bent - center
    root = lax.rsqrt(mean(shifted * shifted) + EPSILON)
    normed = shifted * root
    hidden_ref[...] = (tokens_ref[...].astype(f32) + normed * small_ref[1:2] + small_ref[2:3]).astype(bf16)
    normed_ref[...] = normed
    slope_ref[...] = bend * root


def conv_forward(core, mine, other, stacked, tokens, body, extra):
    rows, width = tokens.shape
    blocks = mine.shape[0]
    tile = 512
    tall = rows_of(tile, width)
    return pl.pallas_call(
        functools.partial(conv_kernel, blocks=blocks, body=body, extra=extra),
        grid=(rows // tile,),
        in_specs=[SMEM, ANY, ANY, rows_of(tile, TAPS * width), tall],
        out_specs=[tall, tall, tall, pl.BlockSpec((extra, width), lambda i: (0, 0))],
        out_shape=[
            jax.ShapeDtypeStruct((rows, width), bf16),
            jax.ShapeDtypeStruct((rows, width), f32),
            jax.ShapeDtypeStruct((rows, width), f32),
            jax.ShapeDtypeStruct((extra, width), f32),
        ],
        scratch_shapes=[
            pltpu.VMEM((TAPS * width, width), bf16),
            pltpu.VMEM((2, blocks, extra, width), bf16),
            pltpu.SemaphoreType.DMA((2 * blocks + 2,)),
        ],
        compiler_params=vmem(60),
        cost_estimate=cost(TAPS * rows * width * width, 24 * rows * width),
        name="conv_forward",
    )(core, mine, other, stacked, tokens)


def chain_kernel(
    ff, small_ref, hidden_ref, normed_ref, slope_ref, cot_ref,
    mixed_ref, active_ref, d_outer_ref, d_inner_ref, d_hidden_ref, d_conv_ref, sums_ref,
    w_in, w_out, bend, sems, *, cols, chunk,
):
    step = pl.program_id(0)
    blocks, inner_rows, _ = w_in.shape
    width = hidden_ref.shape[1]

    @pl.when(step == 0)
    def _():
        copies = [
            pltpu.make_async_copy(
                ff.at[:, pl.ds(j * inner_rows, inner_rows)], w_in.at[:, :, pl.ds(j * width, width)], sems.at[j]
            )
            for j in range(cols)
        ]
        copies.append(
            pltpu.make_async_copy(ff.at[:, pl.ds(cols * inner_rows, w_out.shape[1])], w_out, sems.at[cols])
        )
        for copy in copies:
            copy.start()
        for copy in copies:
            copy.wait()
        sums_ref[...] = jnp.zeros_like(sums_ref)

    full_in = w_in.reshape(blocks * inner_rows, w_in.shape[2])
    full_out = w_out.reshape(blocks * w_out.shape[1], width)
    hidden = hidden_ref[...]
    total = full_in.shape[1]
    for j in range(total // chunk):
        part = slice(j * chunk, (j + 1) * chunk)
        bias = small_ref[6 + j * chunk // width : 7 + j * chunk // width, j * chunk % width : j * chunk % width + chunk]
        inner = dot(hidden, full_in[:, part]) + bias
        act, slope = gelu_pair(inner)
        active_ref[:, part] = act.astype(bf16)
        bend[:, part] = slope
    outer = dot(active_ref[...], full_out[...]) + small_ref[3:4]
    center = mean(outer)
    shifted = outer - center
    root = lax.rsqrt(mean(shifted * shifted) + EPSILON)
    normal = shifted * root
    gain_two = small_ref[4:5]
    mixed_ref[...] = (hidden.astype(f32) + normal * gain_two + small_ref[5:6]).astype(bf16)
    cot = cot_ref[...].astype(f32)
    q = cot * gain_two
    d_outer = (root * (q - mean(q) - normal * mean(q * normal))).astype(bf16)
    d_outer_ref[...] = d_outer
    sums_ref[3:4] += colsum(d_outer.astype(f32))
    sums_ref[4:5] += colsum(cot * normal)
    sums_ref[5:6] += colsum(cot)
    for j in range(total // chunk):
        part = slice(j * chunk, (j + 1) * chunk)
        d_active = dot_t(d_outer, full_out[part])
        d_inner = (d_active * bend[:, part]).astype(bf16)
        d_inner_ref[:, part] = d_inner
        row, col = 6 + j * chunk // width, j * chunk % width
        sums_ref[row : row + 1, col : col + chunk] += colsum(d_inner.astype(f32))
    d_hidden = dot_t(d_inner_ref[...], full_in[...]) + cot
    d_hidden_ref[...] = d_hidden
    first = normed_ref[...]
    sums_ref[1:2] += colsum(d_hidden * first)
    sums_ref[2:3] += colsum(d_hidden)
    p = d_hidden * small_ref[1:2]
    d_conv = (slope_ref[...] * (p - mean(p) - first * mean(p * first))).astype(bf16)
    d_conv_ref[...] = d_conv
    sums_ref[0:1] += colsum(d_conv.astype(f32))


def chain(ff, small, hidden, normed, slope, cotangent, inner_rows, outer_rows, total):
    rows, width = hidden.shape
    blocks = ff.shape[0]
    tile = 512
    tall = rows_of(tile, width)
    broad = rows_of(tile, total)
    return pl.pallas_call(
        functools.partial(chain_kernel, cols=total // width, chunk=512),
        grid=(rows // tile,),
        in_specs=[ANY, whole(small.shape), tall, tall, tall, tall],
        out_specs=[tall, broad, tall, broad, tall, tall, pl.BlockSpec((16, width), lambda i: (0, 0))],
        out_shape=[
            jax.ShapeDtypeStruct((rows, width), bf16),
            jax.ShapeDtypeStruct((rows, total), bf16),
            jax.ShapeDtypeStruct((rows, width), bf16),
            jax.ShapeDtypeStruct((rows, total), bf16),
            jax.ShapeDtypeStruct((rows, width), f32),
            jax.ShapeDtypeStruct((rows, width), bf16),
            jax.ShapeDtypeStruct((16, width), f32),
        ],
        scratch_shapes=[
            pltpu.VMEM((blocks, inner_rows, total), bf16),
            pltpu.VMEM((blocks, outer_rows, width), bf16),
            pltpu.VMEM((tile, total), f32),
            pltpu.SemaphoreType.DMA((total // width + 1,)),
        ],
        compiler_params=vmem(60),
        cost_estimate=cost(4 * rows * width * total, 40 * rows * width),
        name="chain",
    )(ff, small, hidden, normed, slope, cotangent)


def ff_grads_kernel(core_ref, hidden_ref, d_outer_ref, active_ref, d_inner_ref, keep_ref, send_ref, store, sems, *, blocks, inner_rows, outer_rows):
    step = pl.program_id(0)
    width = hidden_ref.shape[1]
    cols = pl.num_programs(0)
    d_in = dot_rows(hidden_ref[...], d_inner_ref[...]).astype(bf16)
    store[:, pl.ds(pl.multiple_of(step * inner_rows, inner_rows), inner_rows)] = d_in.reshape(2 * blocks, inner_rows, width)
    d_out = dot_rows(active_ref[...], d_outer_ref[...]).astype(bf16)
    first = store.shape[1] - outer_rows
    if outer_rows <= width:
        many = width // outer_rows
        store[pl.ds(step * many, many), pl.ds(first, outer_rows)] = d_out.reshape(many, outer_rows, width)
    else:
        per = outer_rows // width
        start = pl.multiple_of(first + (step % per) * width, 16)
        store[pl.ds(step // per, 1), pl.ds(start, width)] = d_out.reshape(1, width, width)

    @pl.when(step == cols - 1)
    def _():
        core = core_ref[0]
        copies = []
        for block in range(blocks):
            copies.append(pltpu.make_async_copy(store.at[2 * block + core], keep_ref.at[block], sems.at[0, block]))
            copies.append(pltpu.make_async_copy(store.at[2 * block + 1 - core], send_ref.at[block], sems.at[1, block]))
        for copy in copies:
            copy.start()
        for copy in copies:
            copy.wait()


def ff_grads(core, hidden, d_outer, active, d_inner, blocks, inner_rows, outer_rows):
    rows, width = hidden.shape
    total = active.shape[1]
    cols = total // width
    share = cols * inner_rows + outer_rows
    part = pl.BlockSpec((rows, width), lambda j: (0, j))
    return pl.pallas_call(
        functools.partial(ff_grads_kernel, blocks=blocks, inner_rows=inner_rows, outer_rows=outer_rows),
        grid=(cols,),
        in_specs=[SMEM, whole((rows, width)), whole((rows, width)), part, part],
        out_specs=[ANY, ANY],
        out_shape=[jax.ShapeDtypeStruct((blocks, share, width), bf16)] * 2,
        scratch_shapes=[pltpu.VMEM((2 * blocks, share, width), bf16), pltpu.SemaphoreType.DMA((2, blocks))],
        compiler_params=vmem(60),
        cost_estimate=cost(2 * rows * width * total, 20 * rows * width),
        name="ff_grads",
    )(core, hidden, d_outer, active, d_inner)


def lay_shifted(values_ref, even, odd, tile):
    rows, width = values_ref.shape
    zeros = jnp.zeros((REACH, width), bf16)
    even[:REACH] = zeros
    even[rows + REACH :] = zeros
    odd[: REACH] = zeros
    odd[rows :] = jnp.zeros((2 * REACH, width), bf16)
    for r in range(0, rows, tile):
        block = values_ref[r : r + tile]
        even[REACH + r : REACH + r + tile] = block
        odd[REACH - STEP + r : REACH - STEP + r + tile] = block


def conv_grad_kernel(len_ref, core_ref, masked_ref, d_conv_ref, keep_ref, send_ref, even, odd, store, sems, *, wins, blocks, body):
    rows, width = d_conv_ref.shape
    channels = masked_ref.shape[1]
    lay_shifted(d_conv_ref, even, odd, 256)
    position = lax.broadcasted_iota(jnp.int32, (rows, 128), 0)
    first, last = window_bounds(len_ref, position, wins, rows)
    for tap in range(TAPS):
        mirror = TAPS - 1 - tap
        other = position + (mirror - TAPS // 2) * STEP
        valid = ((other >= first) & (other < last)).astype(bf16)
        source = (odd if mirror % 2 else even)[mirror // 2 * 2 * STEP : mirror // 2 * 2 * STEP + rows]
        block = source * wide(valid, width)
        store[tap * channels : (tap + 1) * channels] = dot_rows(masked_ref[...], block).astype(bf16)
    core = core_ref[0]
    copies = []
    for block in range(blocks):
        for n, (target, which) in enumerate(((keep_ref, core), (send_ref, 1 - core))):
            start = pl.multiple_of((2 * block + which) * body, 16)
            copies.append(pltpu.make_async_copy(store.at[pl.ds(start, body)], target.at[block], sems.at[n, block]))
    for copy in copies:
        copy.start()
    for copy in copies:
        copy.wait()


def conv_grad(lengths, core, masked, d_conv, part, parts, blocks, body):
    rows, channels = masked.shape
    width = d_conv.shape[1] // parts
    return pl.pallas_call(
        functools.partial(conv_grad_kernel, wins=lengths.shape[1], blocks=blocks, body=body),
        grid=(1,),
        in_specs=[SMEM, SMEM, whole((rows, channels)), pl.BlockSpec((rows, width), lambda i: (0, part))],
        out_specs=[ANY, ANY],
        out_shape=[jax.ShapeDtypeStruct((blocks, body, width), bf16)] * 2,
        scratch_shapes=[
            pltpu.VMEM((rows + 2 * REACH, width), bf16),
            pltpu.VMEM((rows + 2 * REACH, width), bf16),
            pltpu.VMEM((TAPS * channels, width), bf16),
            pltpu.SemaphoreType.DMA((2, blocks)),
        ],
        compiler_params=vmem(60),
        cost_estimate=cost(TAPS * rows * width * channels, 12 * rows * width),
        name="conv_grad",
    )(lengths, core, masked, d_conv)


def token_grad_kernel(
    len_ref, core_ref, mine, other, d_conv_ref, d_hidden_ref, keep_ref, d_tokens_ref, even, odd, store, sems, *, wins, blocks, body, tile
):
    step = pl.program_id(0)
    rows, width = d_conv_ref.shape

    @pl.when(step == 0)
    def _():
        copies = place_halves(mine, other, core_ref[0], blocks, body, store, sems)
        for copy in copies:
            copy.start()
        lay_shifted(d_conv_ref, even, odd, 256)
        for copy in copies:
            copy.wait()

    start = pl.multiple_of(step * tile, tile)
    position = lax.broadcasted_iota(jnp.int32, (tile, 128), 0) + start
    first, last = window_bounds(len_ref, position, wins, rows)
    total = None
    for tap in range(TAPS):
        mirror = TAPS - 1 - tap
        other_row = position + (mirror - TAPS // 2) * STEP
        valid = ((other_row >= first) & (other_row < last)).astype(bf16)
        offset = pl.multiple_of(start + mirror // 2 * 2 * STEP, 2 * STEP)
        block = (odd if mirror % 2 else even)[pl.ds(offset, tile)] * wide(valid, width)
        term = dot_t(block, store[tap * width : (tap + 1) * width])
        total = term if total is None else total + term
    d_tokens_ref[...] = d_hidden_ref[...] + total * wide(keep_ref[...], width)


def token_grad(lengths, core, mine, other, d_conv, d_hidden, keep, body):
    rows, width = d_conv.shape
    blocks = mine.shape[0]
    tile = 512
    return pl.pallas_call(
        functools.partial(token_grad_kernel, wins=lengths.shape[1], blocks=blocks, body=body, tile=tile),
        grid=(rows // tile,),
        in_specs=[SMEM, SMEM, ANY, ANY, whole((rows, width)), rows_of(tile, width), rows_of(tile, 128)],
        out_specs=rows_of(tile, width),
        out_shape=jax.ShapeDtypeStruct((rows, width), f32),
        scratch_shapes=[
            pltpu.VMEM((rows + 2 * REACH, width), bf16),
            pltpu.VMEM((rows + 2 * REACH, width), bf16),
            pltpu.VMEM((TAPS * width, width), bf16),
            pltpu.SemaphoreType.DMA((2 * blocks,)),
        ],
        compiler_params=vmem(60),
        cost_estimate=cost(TAPS * rows * width * width, 12 * rows * width),
        name="token_grad",
    )(lengths, core, mine, other, d_conv, d_hidden, keep)


def on_device(
    n_dp, n_fsdp, tokens, present, lengths, conv_w, conv_b, gain_one, shift_one, w_in, b_in, w_out, b_out, gain_two, shift_two, cotangent
):
    rows, width = tokens.shape
    total = w_in.shape[1]
    cols = total // width
    devices = n_dp * n_fsdp
    place = lax.axis_index("dp") * n_fsdp + lax.axis_index("fsdp")
    fast = conv_w.shape[0] % 16 == 0 and w_in.shape[0] % 16 == 0
    extra = 16
    keep = jnp.broadcast_to((present > 0).astype(f32)[:, None], (rows, 128))
    swap = [(i, i ^ 1) for i in range(n_fsdp)]
    columns = [list(range(c, n_fsdp, 2)) for c in range(2)]
    n_z = n_fsdp // 2
    vectors = (conv_b, gain_one, shift_one, b_out, gain_two, shift_two)
    if fast:
        core = lax.rem(lax.axis_index("fsdp"), 2).astype(jnp.int32).reshape(1)
        body = conv_w.shape[0]
        inner_rows, outer_rows = w_in.shape[0], w_out.shape[0]
        blocks = devices // 2
        lane = jnp.arange(width)
        lines = []
        for vector in vectors:
            n = vector.shape[0]
            lines.append(jnp.where(lane // n == place, jnp.tile(vector, width // n), 0))
        n = b_in.shape[0]
        for j in range(cols):
            lines.append(jnp.where((lane + j * width) // n == place, jnp.tile(b_in, width // n), 0))
        lines += [jnp.zeros_like(lines[0])] * (extra - len(lines))
        pack = jnp.concatenate([conv_w, jnp.stack(lines)], axis=0)
        mine = lax.all_to_all(
            jnp.broadcast_to(pack, (n_z,) + pack.shape), "fsdp", 0, 0, tiled=True, axis_index_groups=columns
        )
        mine = lax.all_to_all(jnp.broadcast_to(mine, (n_dp,) + mine.shape), "dp", 0, 0, tiled=True)
        mine = mine.reshape((blocks,) + pack.shape)
        other = lax.ppermute(mine, "fsdp", swap)
        ff_own = jnp.concatenate([w_in[:, j * width : (j + 1) * width] for j in range(cols)] + [w_out], axis=0)
        ff = lax.all_gather(ff_own, AXES, axis=0, tiled=False)
    else:
        core = jnp.zeros((1,), jnp.int32)
        gather = functools.partial(lax.all_gather, axis_name=AXES, axis=0, tiled=True)
        full = gather(conv_w).reshape(2, 1, -1, width)
        body = full.shape[2]
        lines = [gather(vector) for vector in vectors] + list(gather(b_in).reshape(cols, width))
        lines += [jnp.zeros_like(lines[0])] * (extra - len(lines))
        tails = jnp.stack([jnp.stack(lines), jnp.zeros((extra, width), bf16)])[:, None]
        halves = jnp.concatenate([full, tails], axis=2)
        mine, other = halves[0], halves[1]
        full_in, full_out = gather(w_in), gather(w_out)
        inner_rows, outer_rows = full_in.shape[0] // 2, full_out.shape[0] // 2
        blocks = 1
        ff = jnp.concatenate(
            [full_in[:, j * width : (j + 1) * width].reshape(2, inner_rows, width) for j in range(cols)]
            + [full_out.reshape(2, outer_rows, width)],
            axis=1,
        )

    stacked, masked = prep(lengths, tokens, keep)
    hidden, normed, slope, small = conv_forward(core, mine, other, stacked, tokens, body, extra)
    mixed, active, d_outer, d_inner, d_hidden, d_conv, sums = chain(
        ff, small, hidden, normed, slope, cotangent, inner_rows, outer_rows, total
    )
    ff_pair = ff_grads(core, hidden, d_outer, active, d_inner, blocks, inner_rows, outer_rows)
    parts = 2
    conv_pairs = [conv_grad(lengths, core, masked, d_conv, part, parts, blocks, body) for part in range(parts)]
    d_conv_late, conv_pairs[-1] = lax.optimization_barrier((d_conv, conv_pairs[-1]))
    d_tokens = token_grad(lengths, core, mine, other, d_conv_late, d_hidden, keep, body)

    shares = sums[:6].reshape(6, devices, -1).transpose(1, 0, 2).reshape(devices, -1)
    shares = jnp.concatenate([shares, sums[6 : 6 + cols].reshape(devices, -1)], axis=1)
    shares = jnp.sum(lax.all_to_all(shares, AXES, 0, 0, tiled=True), axis=0)
    n = width // devices
    vector_grads = [shares[i * n : (i + 1) * n] for i in range(6)] + [shares[6 * n :]]

    def reduced(pair):
        kept, sent = pair
        if not fast:
            both = jnp.concatenate([kept, sent], axis=0)
            return both
        came = lax.ppermute(sent, "fsdp", swap)
        chip = (kept.astype(f32) + came.astype(f32)).astype(bf16)
        chip = chip.reshape((n_dp, n_z) + chip.shape[1:])
        chip = lax.all_to_all(chip, "dp", 0, 0, tiled=True)
        chip = jnp.sum(chip.astype(f32), axis=0).astype(bf16)
        chip = lax.all_to_all(chip, "fsdp", 0, 0, tiled=True, axis_index_groups=columns)
        return jnp.sum(chip.astype(f32), axis=0)

    ff_share = reduced(ff_pair)
    conv_shares = [reduced(pair) for pair in conv_pairs]
    if fast:
        d_w_in = jnp.concatenate([ff_share[j * inner_rows : (j + 1) * inner_rows] for j in range(cols)], axis=1)
        d_w_out = ff_share[cols * inner_rows :]
        d_conv_w = jnp.concatenate(conv_shares, axis=1)
    else:
        scatter = functools.partial(lax.psum_scatter, axis_name=AXES, scatter_dimension=0, tiled=True)
        d_in_full = jnp.concatenate(
            [ff_share[:, j * inner_rows : (j + 1) * inner_rows].reshape(-1, width) for j in range(cols)], axis=1
        )
        d_w_in = scatter(d_in_full.astype(f32))
        d_w_out = scatter(ff_share[:, cols * inner_rows :].reshape(-1, width).astype(f32))
        conv_full = jnp.concatenate([share.reshape(-1, width // parts) for share in conv_shares], axis=1)
        d_conv_w = scatter(conv_full.astype(f32))
    d_conv_b, d_gain_one, d_shift_one, d_b_out, d_gain_two, d_shift_two, d_b_in = vector_grads
    return (
        mixed, d_tokens, d_conv_w, d_conv_b, d_gain_one, d_shift_one, d_w_in, d_b_in, d_w_out, d_b_out, d_gain_two, d_shift_two
    )


def solution(mesh):
    both = P(AXES)
    flat = P(AXES, None)
    in_specs = (flat, both, flat, flat, both, both, both, flat, both, flat, both, both, both, flat)
    out_specs = (flat, flat, flat, both, both, both, flat, both, flat, both, both, both)
    return jax.shard_map(
        functools.partial(on_device, mesh.shape["dp"], mesh.shape["fsdp"]),
        mesh=mesh,
        in_specs=in_specs,
        out_specs=out_specs,
        check_vma=False,
    )
```

```python
import functools
import jax
import jax.numpy as jnp
from jax import lax
from jax.experimental import pallas as pl
from jax.experimental.pallas import tpu as pltpu
from jax.sharding import PartitionSpec as P

TAPS = 9
STEP = 8
REACH = (TAPS // 2) * STEP
EPSILON = 1e-05
SPLIT = 80
SLAB = 512
QUARTERS = 4
AXES = ("dp", "fsdp")
f32 = jnp.float32
bf16 = jnp.bfloat16
ANY = pl.BlockSpec(memory_space=pl.ANY)
SMEM = pl.BlockSpec(memory_space=pltpu.SMEM)


def dot(a, b):
    return jnp.dot(a, b, preferred_element_type=f32)


def dot_t(a, b):
    return lax.dot_general(a, b, (((1,), (1,)), ((), ())), preferred_element_type=f32)


def dot_rows(a, b):
    return lax.dot_general(a, b, (((0,), (0,)), ((), ())), preferred_element_type=f32)


def gelu_pair(v):
    phi = 0.5 + 0.5 * lax.erf(v * 0.7071067811865476)
    return v * phi, phi + v * (0.3989422804014327 * jnp.exp2(v * v * -0.7213475204444817))


def mean(v):
    return jnp.sum(v, axis=-1, keepdims=True) * (1.0 / v.shape[-1])


def fold(v):
    return sum(v[r : r + 8] for r in range(0, v.shape[0], 8))


def slabs(total, size):
    return [pl.ds(r, size) for r in range(0, total, size)]


def colsum(v):
    return jnp.sum(v, axis=0, keepdims=True)


def vmem(mib):
    return pltpu.CompilerParams(vmem_limit_bytes=mib << 20)


def cost(macs, nbytes):
    return pl.CostEstimate(flops=macs // 32, bytes_accessed=nbytes // 32, transcendentals=0)


def whole(shape):
    return pl.BlockSpec(shape, lambda *_: (0,) * len(shape), pipeline_mode=pl.Buffered(1))


def rows_of(tile, width):
    return pl.BlockSpec((tile, width), lambda i: (i, 0))


def window_bounds(len_ref, position, wins, total):
    first = jnp.zeros_like(position)
    last = jnp.full_like(position, total)
    edge = jnp.int32(0)
    edges = []
    for w in range(wins - 1):
        edge = edge + len_ref[0, w]
        edges.append(edge)
    for edge in edges:
        first = jnp.where(position >= edge, edge, first)
    for edge in reversed(edges):
        last = jnp.where(position < edge, edge, last)
    return first, last


def wide(mask, width):
    return jnp.concatenate([mask] * (width // 128), axis=1)


def prep_kernel(len_ref, place_ref, tokens_ref, present_ref, stacked_ref, masked_ref, keep_ref, even, odd, *, tile, wins):
    step = pl.program_id(0)
    rows, width = tokens_ref.shape
    start = pl.multiple_of(step * tile, tile)

    @pl.when(step == 0)
    def _():
        edge = jnp.zeros((REACH, width), bf16)
        even[:REACH] = edge
        even[rows + REACH :] = edge
        odd[:REACH] = edge
        odd[rows : rows + REACH] = edge
        odd[rows + REACH :] = edge
        for r in range(0, rows, 128):
            line = jnp.broadcast_to((present_ref[r // 128 : r // 128 + 1] > 0).astype(f32), (128, 128))
            kept = line.T
            keep_ref[r : r + 128] = kept
            block = tokens_ref[r : r + 128] * wide(kept.astype(bf16), width)
            even[REACH + r : REACH + r + 128] = block
            odd[REACH - STEP + r : REACH - STEP + r + 128] = block

    masked_ref[...] = even[pl.ds(start + REACH, tile)].T
    position = lax.broadcasted_iota(jnp.int32, (tile, 128), 0) + start
    first, last = window_bounds(len_ref, position, wins, rows)
    per = TAPS * width // 128 // QUARTERS
    for tap in range(TAPS):
        other = position + (tap - TAPS // 2) * STEP
        valid = ((other >= first) & (other < last)).astype(bf16)
        offset = pl.multiple_of(start + tap // 2 * 2 * STEP, 2 * STEP)
        block = (odd if tap % 2 else even)[pl.ds(offset, tile)] * wide(valid, width)
        for lane in range(0, width, 128):
            chunk = (tap * width + lane) // 128
            seat = ((chunk // per) ^ place_ref[2]) * per + chunk % per
            stacked_ref[:, pl.ds(pl.multiple_of(seat * 128, 128), 128)] = block[:, lane : lane + 128]


def prep(lengths, place, tokens, present):
    rows, width = tokens.shape
    tile = 256
    return pl.pallas_call(
        functools.partial(prep_kernel, tile=tile, wins=lengths.shape[1]),
        grid=(rows // tile,),
        in_specs=[SMEM, SMEM, whole((rows, width)), whole((rows // 128, 128))],
        out_specs=[
            rows_of(tile, TAPS * width), pl.BlockSpec((width, tile), lambda i: (0, i)), pl.BlockSpec((rows, 128), lambda i: (0, 0))
        ],
        out_shape=[
            jax.ShapeDtypeStruct((rows, TAPS * width), bf16),
            jax.ShapeDtypeStruct((width, rows), bf16),
            jax.ShapeDtypeStruct((rows, 128), f32),
        ],
        scratch_shapes=[pltpu.VMEM((rows + 2 * REACH, width), bf16), pltpu.VMEM((rows + 2 * REACH, width), bf16)],
        compiler_params=vmem(60),
        cost_estimate=cost(0, 24 * rows * width),
        name="prep",
    )(lengths, place, tokens, present.reshape(rows // 128, 128))


def conv_sites(pieces, first, place, fast, body):
    if not fast:
        return [(piece.at[0], first, 0) for piece in pieces]
    core, z, _ = place
    sites = []
    per = len(pieces) // 2
    for n, piece in enumerate(pieces):
        which = core if n < per else 1 - core
        kind = first + n % per
        for hop in range(piece.shape[0]):
            row = (((z - hop) & 3) * 2 + which) * body + (SPLIT if kind == 4 else 0)
            sites.append((piece.at[hop], min(kind, 3), row))
    return sites


def conv_copies(sites, base, store, sems):
    copies = []
    for n, (source, kind, row) in enumerate(sites):
        start = pl.multiple_of(base(kind) + row, 16)
        copies.append(pltpu.make_async_copy(source, store.at[pl.ds(start, source.shape[0])], sems.at[n]))
    return copies


def conv_kernel(place_ref, *refs, fast, body):
    *pieces, stacked_ref, conv_ref, near_ref, store, sems, out_sem = refs
    depth = store.shape[0] // (QUARTERS - 1)
    back = pltpu.make_async_copy(store, near_ref, out_sem)

    @pl.when(pl.program_id(0) == 0)
    def _():
        sites = conv_sites(pieces, 0, tuple(place_ref[i] for i in range(3)), fast, body)
        copies = conv_copies(sites, lambda kind: kind * depth, store, sems)
        for copy in copies:
            copy.start()
        for copy in copies:
            copy.wait()
        back.start()

    conv_ref[...] = dot(stacked_ref[...], store[...])

    @pl.when(pl.program_id(0) == pl.num_programs(0) - 1)
    def _():
        back.wait()


def conv_forward(place, pieces, stacked, fast, body):
    rows, depth = stacked.shape
    width = pieces[0].shape[2]
    depth = depth // QUARTERS * (QUARTERS - 1)
    tile = 512
    return pl.pallas_call(
        functools.partial(conv_kernel, fast=fast, body=body),
        grid=(rows // tile,),
        in_specs=[SMEM] + [ANY] * len(pieces) + [rows_of(tile, depth)],
        out_specs=[rows_of(tile, width), ANY],
        out_shape=[jax.ShapeDtypeStruct((rows, width), f32), jax.ShapeDtypeStruct((depth, width), bf16)],
        scratch_shapes=[
            pltpu.VMEM((depth, width), bf16),
            pltpu.SemaphoreType.DMA((sum(piece.shape[0] for piece in pieces),)),
            pltpu.SemaphoreType.DMA,
        ],
        compiler_params=vmem(60),
        cost_estimate=cost(depth * rows * width, 24 * rows * width),
        name="conv_forward",
    )(place, *pieces, stacked)


def ff_copies(pieces, place, fast, store, sems):
    if not fast:
        return [pltpu.make_async_copy(pieces[0], store, sems.at[0])]
    core, z, _ = place
    copies = []
    for piece, which in zip(pieces, (core, 1 - core)):
        for seat in range(piece.shape[0]):
            block = (seat // 4 * 4 + ((z - seat) & 3)) * 2 + which
            copies.append(pltpu.make_async_copy(piece.at[seat], store.at[block], sems.at[len(copies)]))
    return copies


def feed_kernel(place_ref, *refs, far, count, tiles, chunk, inner_rows, outer_rows, extra, fast, body):
    far_pieces, ff_pieces = refs[:far], refs[far : far + count]
    refs = refs[far + count :]
    stacked_ref, partial_ref, tokens_ref, cot_ref = refs[:4]
    mixed_ref, d_hidden_ref, d_conv_ref, keep_ref, send_ref, sums_ref, far_ref = refs[4:11]
    packed, w_in, w_far, small_ref, bend, slope_ref, normed_ref, hiddens, actives, d_outers, d_inners = refs[11:22]
    tallies, ff_sems, far_sems, grad_sems, last_sems, out_sem = refs[22:]
    slab = SLAB
    store = packed
    step = pl.program_id(0)
    tile, width = tokens_ref.shape
    total = w_in.shape[1]
    blocks = packed.shape[0]
    cols = total // width
    place = tuple(place_ref[i] for i in range(3))
    core = place[0]
    depth = w_far.shape[0]
    top = cols * inner_rows
    back = pltpu.make_async_copy(w_far, far_ref, out_sem)

    @pl.when(step == 0)
    def _():
        copies = ff_copies(ff_pieces, place, fast, packed, ff_sems)
        far_sites = conv_sites(far_pieces, QUARTERS - 1, place, fast, body)
        copies += conv_copies(far_sites, lambda kind: 0, w_far, far_sems)
        for copy in copies:
            copy.start()
        tallies[...] = jnp.zeros_like(tallies)
        for copy in copies:
            copy.wait()
        back.start()
        for j in range(cols):
            part = packed[:, j * inner_rows : (j + 1) * inner_rows].reshape(blocks * inner_rows, width)
            w_in[:, j * width : (j + 1) * width] = part
        small_ref[...] = jnp.sum(packed[:, top : top + extra].astype(f32), axis=0)

    base = pl.multiple_of(jnp.minimum(step, tiles - 1) * tile, tile)

    def at(part):
        return pl.ds(pl.multiple_of(base + part.start, part.size), part.size)

    def add_tally(row, col, term):
        tallies[8 * row : 8 * row + 8, col : col + term.shape[1]] += fold(term)

    def out_rows(j):
        if outer_rows > chunk:
            per = outer_rows // chunk
            first = top + extra + j % per * chunk
            return packed[j // per, first : first + chunk]
        count = chunk // outer_rows
        return packed[j * count : (j + 1) * count, top + extra :].reshape(chunk, width)

    in_rows = step < tiles

    @pl.when(in_rows)
    def _():
        for part in slabs(tile, slab):
            conv = partial_ref[part] + dot(stacked_ref[part], w_far[...]) + small_ref[0:1]
            bent, slope = gelu_pair(conv)
            shifted = bent - mean(bent)
            root = lax.rsqrt(mean(shifted * shifted) + EPSILON)
            normed = shifted * root
            normed_ref[part] = normed
            slope_ref[part] = slope * root
            hiddens[at(part)] = (
                tokens_ref[part].astype(f32) + normed * small_ref[1:2] + small_ref[2:3]
            ).astype(bf16)

    for j in range(total // chunk):
        cut = slice(j * chunk, (j + 1) * chunk)

        @pl.when(in_rows)
        def _(j=j, cut=cut):
            for part in slabs(tile, slab):
                inner = dot(hiddens[at(part)], w_in[:, cut]) + small_ref[6 + j : 7 + j]
                act, slope = gelu_pair(inner)
                actives[at(part), cut] = act.astype(bf16)
                bend[part, cut] = slope

    @pl.when(in_rows)
    def _():
        gain_two = small_ref[4:5]
        for part in slabs(tile, slab):
            full = packed[:, top + extra :].reshape(blocks * outer_rows, width)
            outer = dot(actives[at(part)], full) + small_ref[3:4]
            shifted = outer - mean(outer)
            root = lax.rsqrt(mean(shifted * shifted) + EPSILON)
            normal = shifted * root
            mixed_ref[part] = (hiddens[at(part)].astype(f32) + normal * gain_two + small_ref[5:6]).astype(bf16)
            cot = cot_ref[part].astype(f32)
            q = cot * gain_two
            d_outer = (root * (q - mean(q) - normal * mean(q * normal))).astype(bf16)
            d_outers[at(part)] = d_outer
            add_tally(3, 0, d_outer.astype(f32))
            add_tally(4, 0, cot * normal)
            add_tally(5, 0, cot)

    for j in range(total // chunk):
        cut = slice(j * chunk, (j + 1) * chunk)

        @pl.when(in_rows)
        def _(j=j, cut=cut):
            for part in slabs(tile, slab):
                d_inner = (dot_t(d_outers[at(part)], out_rows(j)) * bend[part, cut]).astype(bf16)
                d_inners[at(part), cut] = d_inner
                add_tally(6 + j, 0, d_inner.astype(f32))

    @pl.when(in_rows)
    def _():
        for part in slabs(tile, slab):
            d_hidden = dot_t(d_inners[at(part)], w_in[...]) + cot_ref[part].astype(f32)
            d_hidden_ref[part] = d_hidden
            first = normed_ref[part]
            p = d_hidden * small_ref[1:2]
            d_conv = (slope_ref[part] * (p - mean(p) - first * mean(p * first))).astype(bf16)
            d_conv_ref[part] = d_conv
            add_tally(0, 0, d_conv.astype(f32))
            add_tally(1, 0, d_hidden * first)
            add_tally(2, 0, d_hidden)

    def grad_copies(j):
        copies = []
        if fast:
            z = place[1]
            below = pl.ds(top + extra, outer_rows)
            for n, (target, which) in enumerate(((keep_ref, core), (send_ref, 1 - core))):
                for k in range(4):
                    seat = j * 4 + ((k - z) & 3)
                    copies.append(
                        pltpu.make_async_copy(
                            store.at[2 * (4 * j + k) + which, below], target.at[seat, below], grad_sems.at[j, 4 * n + k]
                        )
                    )
        return copies

    def last_copies():
        copies = []
        if fast:
            z = place[1]
            above = pl.ds(0, top + extra)
            for block in range(blocks // 2):
                seat = block // 4 * 4 + ((block % 4 - z) & 3)
                for n, (target, which) in enumerate(((keep_ref, core), (send_ref, 1 - core))):
                    copies.append(
                        pltpu.make_async_copy(
                            store.at[2 * block + which, above], target.at[seat, above], last_sems.at[n, block]
                        )
                    )
        return copies

    @pl.when(step >= tiles)
    def _():
        j = step - tiles
        part = pl.ds(pl.multiple_of(j * width, width), width)
        d_out = dot_rows(actives[:, part], d_outers[...]).astype(bf16)
        first = top + extra
        if fast:
            many = width // outer_rows
            store[pl.ds(j * many, many), first : first + outer_rows] = d_out.reshape(many, outer_rows, width)
        else:
            per = outer_rows // width
            start = pl.multiple_of(first + (j % per) * width, 16)
            store[pl.ds(j // per, 1), pl.ds(start, width)] = d_out.reshape(1, width, width)
        d_in = dot_rows(hiddens[...], d_inners[:, part]).astype(bf16)
        above = pl.ds(pl.multiple_of(j * inner_rows, inner_rows), inner_rows)
        store[:, above] = d_in.reshape(blocks, inner_rows, width)
        for copy in grad_copies(j):
            copy.start()

    @pl.when(step == pl.num_programs(0) - 1)
    def _():
        back.wait()
        for row in range(sums_ref.shape[0]):
            sums_ref[row : row + 1] = colsum(tallies[8 * row : 8 * row + 8])
        if fast:
            head = sums_ref[:6].astype(bf16)
            rest = jnp.zeros((extra - 7, width), bf16)
            for dp in range(blocks // 8):
                line = jnp.concatenate([head, sums_ref[6 + dp : 7 + dp].astype(bf16), rest])
                store[8 * dp : 8 * dp + 8, top : top + extra] = jnp.broadcast_to(line, (8, extra, width))
            copies = last_copies()
            for copy in copies:
                copy.start()
            for j in range(cols):
                copies += grad_copies(j)
            for copy in copies:
                copy.wait()
        else:
            for n, target in enumerate((keep_ref, send_ref)):
                copy = pltpu.make_async_copy(store.at[pl.ds(n, 1)], target, grad_sems.at[0, n])
                copy.start()
                copy.wait()


def feed(place, far, pieces, stacked, partial, tokens, cotangent, inner_rows, outer_rows, extra, total, fast, body):
    rows, width = tokens.shape
    blocks = width // inner_rows
    tile = 512
    tiles, cols = rows // tile, total // width
    share = cols * inner_rows + extra + outer_rows
    depth = stacked.shape[1] // QUARTERS
    tall = pl.BlockSpec((tile, width), lambda i: (jnp.minimum(i, tiles - 1), 0))
    last = pl.BlockSpec((tile, depth), lambda i: (jnp.minimum(i, tiles - 1), QUARTERS - 1))
    return pl.pallas_call(
        functools.partial(
            feed_kernel, far=len(far), count=len(pieces), tiles=tiles, chunk=512, inner_rows=inner_rows,
            outer_rows=outer_rows, extra=extra, fast=fast, body=body,
        ),
        grid=(tiles + cols,),
        in_specs=[SMEM] + [ANY] * (len(far) + len(pieces)) + [last, tall, tall, tall],
        out_specs=[tall, tall, tall, ANY, ANY, pl.BlockSpec((16, width), lambda i: (0, 0)), ANY],
        out_shape=[
            jax.ShapeDtypeStruct((rows, width), bf16),
            jax.ShapeDtypeStruct((rows, width), f32),
            jax.ShapeDtypeStruct((rows, width), bf16),
            jax.ShapeDtypeStruct((blocks // 2, share, width), bf16),
            jax.ShapeDtypeStruct((blocks // 2, share, width), bf16),
            jax.ShapeDtypeStruct((16, width), f32),
            jax.ShapeDtypeStruct((depth, width), bf16),
        ],
        scratch_shapes=[
            pltpu.VMEM((blocks, share, width), bf16),
            pltpu.VMEM((width, total), bf16),
            pltpu.VMEM((depth, width), bf16),
            pltpu.VMEM((extra, width), f32),
            pltpu.VMEM((tile, total), f32),
            pltpu.VMEM((tile, width), f32),
            pltpu.VMEM((tile, width), f32),
            pltpu.VMEM((rows, width), bf16),
            pltpu.VMEM((rows, total), bf16),
            pltpu.VMEM((rows, width), bf16),
            pltpu.VMEM((rows, total), bf16),
            pltpu.VMEM((8 * extra, width), f32),
            pltpu.SemaphoreType.DMA((blocks,)),
            pltpu.SemaphoreType.DMA((sum(piece.shape[0] for piece in far),)),
            pltpu.SemaphoreType.DMA((cols, 8)),
            pltpu.SemaphoreType.DMA((2, max(blocks // 2, 1))),
            pltpu.SemaphoreType.DMA,
        ],
        compiler_params=vmem(60),
        cost_estimate=cost(6 * rows * width * total, 40 * rows * width),
        name="feed",
    )(place, *far, *pieces, stacked, partial, tokens, cotangent)


def lay_shifted(values_ref, even, odd, tile):
    rows, width = values_ref.shape
    zeros = jnp.zeros((REACH, width), bf16)
    even[:REACH] = zeros
    even[rows + REACH :] = zeros
    odd[:REACH] = zeros
    odd[rows:] = jnp.zeros((2 * REACH, width), bf16)
    for r in range(0, rows, tile):
        block = values_ref[r : r + tile]
        even[REACH + r : REACH + r + tile] = block
        odd[REACH - STEP + r : REACH - STEP + r + tile] = block


def tap_products(len_ref, place, masked_ref, even, odd, part, targets, store, sems, *, wins, blocks, body, turn):
    channels, rows = masked_ref.shape
    width = part.stop - part.start
    core = place[0]
    position = lax.broadcasted_iota(jnp.int32, (rows, 128), 0)
    first, last = window_bounds(len_ref, position, wins, rows)
    copies = []
    for tap in range(TAPS):
        mirror = TAPS - 1 - tap
        other = position + (mirror - TAPS // 2) * STEP
        valid = ((other >= first) & (other < last)).astype(bf16)
        source = (odd if mirror % 2 else even)[mirror // 2 * 2 * STEP : mirror // 2 * 2 * STEP + rows, part]
        store[tap * channels : (tap + 1) * channels] = dot(masked_ref[...], source * wide(valid, width)).astype(bf16)
        while len(copies) // 2 < blocks and (len(copies) // 2 + 1) * 2 * body <= (tap + 1) * channels:
            block = len(copies) // 2
            seat = ((block // 4) ^ turn) * 4 + ((block % 4 - place[1]) & 3) if blocks == 16 else block
            for n, (target, which) in enumerate(zip(targets, (core, 1 - core))):
                start = pl.multiple_of((2 * block + which) * body, 16)
                copies.append(pltpu.make_async_copy(store.at[pl.ds(start, body)], target.at[seat], sems.at[n, block]))
                copies[-1].start()
    for copy in copies:
        copy.wait()


def conv_grad_kernel(len_ref, place_ref, masked_ref, d_conv_ref, keep_ref, send_ref, even, odd, store, sems, *, wins, blocks, body):
    lay_shifted(d_conv_ref, even, odd, 256)
    tap_products(
        len_ref, tuple(place_ref[i] for i in range(3)), masked_ref, even, odd, slice(0, d_conv_ref.shape[1]),
        (keep_ref, send_ref), store, sems, wins=wins, blocks=blocks, body=body, turn=0,
    )


def conv_grad(lengths, place, masked, d_conv, blocks, body):
    channels, rows = masked.shape
    width = d_conv.shape[1]
    return pl.pallas_call(
        functools.partial(conv_grad_kernel, wins=lengths.shape[1], blocks=blocks, body=body),
        grid=(1,),
        in_specs=[SMEM, SMEM, whole(masked.shape), whole((rows, width))],
        out_specs=[ANY, ANY],
        out_shape=[jax.ShapeDtypeStruct((blocks, body, width), bf16)] * 2,
        scratch_shapes=[
            pltpu.VMEM((rows + 2 * REACH, width), bf16),
            pltpu.VMEM((rows + 2 * REACH, width), bf16),
            pltpu.VMEM((TAPS * channels, width), bf16),
            pltpu.SemaphoreType.DMA((2, blocks)),
        ],
        compiler_params=vmem(60),
        cost_estimate=cost(TAPS * rows * width * channels, 12 * rows * width),
        name="conv_grad",
    )(lengths, place, masked, d_conv)


def token_grad_kernel(
    len_ref, place_ref, near_ref, far_ref, d_conv_ref, d_hidden_ref, keep_ref, d_tokens_ref, even, odd, store, sems, *, wins, tile
):
    step = pl.program_id(0)
    rows, width = d_conv_ref.shape
    depth = far_ref.shape[0]

    @pl.when(step == 0)
    def _():
        copies = []
        for kind in range(QUARTERS):
            source = far_ref if kind == QUARTERS - 1 else near_ref.at[pl.ds(kind * depth, depth)]
            start = pl.multiple_of((place_ref[2] ^ kind) * depth, 128)
            copies.append(pltpu.make_async_copy(source, store.at[pl.ds(start, depth)], sems.at[kind]))
        for copy in copies:
            copy.start()
        lay_shifted(d_conv_ref, even, odd, 256)
        for copy in copies:
            copy.wait()

    start = pl.multiple_of(step * tile, tile)
    position = lax.broadcasted_iota(jnp.int32, (tile, 128), 0) + start
    first, last = window_bounds(len_ref, position, wins, rows)
    total = None
    for tap in range(TAPS):
        mirror = TAPS - 1 - tap
        other_row = position + (mirror - TAPS // 2) * STEP
        valid = ((other_row >= first) & (other_row < last)).astype(bf16)
        offset = pl.multiple_of(start + mirror // 2 * 2 * STEP, 2 * STEP)
        block = (odd if mirror % 2 else even)[pl.ds(offset, tile)] * wide(valid, width)
        term = dot_t(block, store[tap * width : (tap + 1) * width])
        total = term if total is None else total + term
    d_tokens_ref[...] = d_hidden_ref[...] + total * wide(keep_ref[...], width)


def token_grad(lengths, place, near, far, d_conv, d_hidden, keep):
    rows, width = d_conv.shape
    tile = 512
    return pl.pallas_call(
        functools.partial(token_grad_kernel, wins=lengths.shape[1], tile=tile),
        grid=(rows // tile,),
        in_specs=[SMEM, SMEM, ANY, ANY, whole((rows, width)), rows_of(tile, width), rows_of(tile, 128)],
        out_specs=rows_of(tile, width),
        out_shape=jax.ShapeDtypeStruct((rows, width), f32),
        scratch_shapes=[
            pltpu.VMEM((rows + 2 * REACH, width), bf16),
            pltpu.VMEM((rows + 2 * REACH, width), bf16),
            pltpu.VMEM((TAPS * width, width), bf16),
            pltpu.SemaphoreType.DMA((QUARTERS,)),
        ],
        compiler_params=vmem(60),
        cost_estimate=cost(TAPS * rows * width * width, 12 * rows * width),
        name="token_grad",
    )(lengths, place, near, far, d_conv, d_hidden, keep)


def on_device(
    n_dp, n_fsdp, tokens, present, lengths, conv_w, conv_b, gain_one, shift_one, w_in, b_in, w_out, b_out, gain_two, shift_two, cotangent
):
    rows, width = tokens.shape
    total = w_in.shape[1]
    cols = total // width
    devices = n_dp * n_fsdp
    fast = n_dp == 4 and n_fsdp == 8 and conv_w.shape[0] % 16 == 0 and w_in.shape[0] % 16 == 0
    bar = lax.optimization_barrier
    extra = 16
    n = width // devices
    swap = [(i, i ^ 1) for i in range(n_fsdp)]
    across = {r: [(i, i ^ r) for i in range(n_dp)] for r in (1, 2, 3)}
    along = {k: [(i, (i + 2 * k) % n_fsdp) for i in range(n_fsdp)] for k in (1, 2, 3)}
    vectors = (conv_b, gain_one, shift_one, b_out, gain_two, shift_two)
    if fast:
        fsdp = lax.axis_index("fsdp").astype(jnp.int32)
        dp = lax.axis_index("dp").astype(jnp.int32)
        place = jnp.stack([fsdp & 1, fsdp >> 1, dp])
        body = conv_w.shape[0]
        inner_rows, outer_rows = w_in.shape[0], w_out.shape[0]
        blocks = devices // 2

        def from_column(shard):
            return [shard] + [lax.ppermute(shard, "fsdp", along[k]) for k in (1, 2, 3)]

        column = jnp.stack(from_column(conv_w))
        seat = dp * n_fsdp + fsdp
        lane = jnp.arange(width, dtype=jnp.int32)
        line = jnp.arange(extra, dtype=jnp.int32)[:, None]
        lines = jnp.concatenate(
            [jnp.tile(jnp.stack(vectors), (1, devices))]
            + [jnp.tile(b_in, width // b_in.shape[0])[None]] * cols
            + [jnp.zeros((extra - 6 - cols, width), bf16)]
        )
        few = b_in.shape[0]
        own_line = ((line < 6) & (lane // n == seat)) | ((line == 6 + dp) & (lane // few == fsdp))
        lines = jnp.where(own_line, lines, 0)
        ff_own = jnp.concatenate([w_in[:, j * width : (j + 1) * width] for j in range(cols)] + [lines, w_out], axis=0)
        stacked, masked, keep = prep(lengths, place, tokens, present)
        column, ff_own, stacked, masked, keep = bar((column, ff_own, stacked, masked, keep))
        beside_x = lax.ppermute(column, "dp", across[1])
        beside_y = lax.ppermute(column, "dp", across[2])
        ff_column = jnp.stack(from_column(ff_own))
        column, beside_x, beside_y, ff_column = bar((column, beside_x, beside_y, ff_column))
        ff = lax.all_to_all(jnp.broadcast_to(ff_column, (n_dp,) + ff_column.shape), "dp", 0, 0, tiled=True)
        ff = (ff.reshape((blocks,) + ff_own.shape),)
        near = (column, beside_x, beside_y)
        near = near + tuple(lax.ppermute(piece, "fsdp", swap) for piece in near)
        far = (
            lax.ppermute(beside_x[:, :SPLIT], "dp", across[2]),
            lax.ppermute(beside_y[:, SPLIT:], "dp", across[1]),
        )
    else:
        place = jnp.zeros((3,), jnp.int32)
        gather = functools.partial(lax.all_gather, axis_name=AXES, axis=0, tiled=True)
        full = gather(conv_w)
        body = full.shape[0] // 2
        depth = full.shape[0] // QUARTERS * (QUARTERS - 1)
        near, far = (full[None, :depth],), (full[None, depth:],)
        lines = [gather(vector) for vector in vectors] + list(gather(b_in).reshape(cols, width))
        lines = jnp.stack(lines + [jnp.zeros_like(lines[0])] * (extra - len(lines)))
        full_in, full_out = gather(w_in), gather(w_out)
        inner_rows, outer_rows = full_in.shape[0] // 2, full_out.shape[0] // 2
        blocks = 1
        ff = [full_in[:, j * width : (j + 1) * width].reshape(2, inner_rows, width) for j in range(cols)]
        ff.append(jnp.stack([lines, jnp.zeros_like(lines)]))
        ff = (jnp.concatenate(ff + [full_out.reshape(2, outer_rows, width)], axis=1),)
        stacked, masked, keep = prep(lengths, place, tokens, present)

    partial, w_near = conv_forward(place, near, stacked, fast, body)
    if fast:
        far, ff, partial = lax.optimization_barrier((far, ff, partial))
        far = far + tuple(lax.ppermute(piece, "fsdp", swap) for piece in far)
        ff = ff + tuple(lax.ppermute(piece, "fsdp", swap) for piece in ff)
    mixed, d_hidden, d_conv, ff_keep, ff_send, sums, w_far = feed(
        place, far, ff, stacked, partial, tokens, cotangent, inner_rows, outer_rows, extra, total, fast, body
    )
    def added(terms):
        return sum(term.astype(f32) for term in terms)

    def chip_sum(kept, came):
        chip = added((kept, came)).astype(bf16)
        return chip.reshape((n_dp, blocks // n_dp) + chip.shape[1:])

    def plane_swap(chip):
        plane = lax.all_to_all(chip, "dp", 0, 0, tiled=True)
        return [plane[r] for r in range(n_dp)]

    def line_swap(plane):
        line = [added(part[k] for part in plane).astype(bf16) for k in range(4)]
        return [line[0]] + [lax.ppermute(line[k], "fsdp", along[k]) for k in (1, 2, 3)]

    if fast:
        ff_came = lax.ppermute(ff_send, "fsdp", swap)
        ff_plane = plane_swap(chip_sum(ff_keep, ff_came))
        conv_keep, conv_send = conv_grad(lengths, place, masked, d_conv, blocks, body)
        conv_came = lax.ppermute(conv_send, "fsdp", swap)
        conv_chip, ff_plane, d_conv = bar((chip_sum(conv_keep, conv_came), ff_plane, d_conv))
        conv_plane = plane_swap(conv_chip)
        ff_line = line_swap(ff_plane)
        d_tokens = token_grad(lengths, place, w_near, w_far, d_conv, d_hidden, keep)
        d_tokens, ff_line, conv_plane = bar((d_tokens, ff_line, conv_plane))
        conv_line = line_swap(conv_plane)
        ff_share = added(ff_line)
        d_conv_w = added(conv_line)
        top = cols * inner_rows
        d_w_in = jnp.concatenate([ff_share[j * inner_rows : (j + 1) * inner_rows] for j in range(cols)], axis=1)
        d_w_out = ff_share[top + extra :]
        seat = dp * n_fsdp + fsdp
        own = lax.dynamic_slice(ff_share[top : top + 6], (0, seat * n), (6, n))
        vector_grads = list(own)
        vector_grads.append(lax.dynamic_slice(ff_share[top + 6], (fsdp * few,), (few,)))
    else:
        conv_pair = conv_grad(lengths, place, masked, d_conv, blocks, body)
        d_tokens = token_grad(lengths, place, w_near, w_far, d_conv, d_hidden, keep)
        ff_share = jnp.concatenate((ff_keep, ff_send), axis=0)
        scatter = functools.partial(lax.psum_scatter, axis_name=AXES, scatter_dimension=0, tiled=True)
        d_in_full = jnp.concatenate(
            [ff_share[:, j * inner_rows : (j + 1) * inner_rows].reshape(-1, width) for j in range(cols)], axis=1
        )
        d_w_in = scatter(d_in_full.astype(f32))
        d_w_out = scatter(ff_share[:, cols * inner_rows + extra :].reshape(-1, width).astype(f32))
        d_conv_w = scatter(jnp.concatenate(conv_pair, axis=0).reshape(-1, width).astype(f32))
        vector_grads = [scatter(line) for line in sums[:6]] + [scatter(sums[6 : 6 + cols].reshape(-1))]
    d_conv_b, d_gain_one, d_shift_one, d_b_out, d_gain_two, d_shift_two, d_b_in = vector_grads
    return (
        mixed, d_tokens, d_conv_w, d_conv_b, d_gain_one, d_shift_one, d_w_in, d_b_in, d_w_out, d_b_out, d_gain_two, d_shift_two
    )


def solution(mesh):
    both = P(AXES)
    flat = P(AXES, None)
    in_specs = (flat, both, flat, flat, both, both, both, flat, both, flat, both, both, both, flat)
    out_specs = (flat, flat, flat, both, both, both, flat, both, flat, both, both, both)
    return jax.shard_map(
        functools.partial(on_device, mesh.shape["dp"], mesh.shape["fsdp"]),
        mesh=mesh,
        in_specs=in_specs,
        out_specs=out_specs,
        check_vma=False,
    )
```

```python
import functools
import jax
import jax.numpy as jnp
from jax import lax
from jax.experimental import pallas as pl
from jax.experimental.pallas import tpu as pltpu
from jax.sharding import PartitionSpec as P

TAPS = 9
STEP = 8
REACH = (TAPS // 2) * STEP
EPSILON = 1e-05
SLAB = 512
QUARTERS = 4
AXES = ("dp", "fsdp")
f32 = jnp.float32
bf16 = jnp.bfloat16
ANY = pl.BlockSpec(memory_space=pl.ANY)
SMEM = pl.BlockSpec(memory_space=pltpu.SMEM)


def dot(a, b):
    return jnp.dot(a, b, preferred_element_type=f32)


def dot_t(a, b):
    return lax.dot_general(a, b, (((1,), (1,)), ((), ())), preferred_element_type=f32)


def dot_rows(a, b):
    return lax.dot_general(a, b, (((0,), (0,)), ((), ())), preferred_element_type=f32)


def gelu_pair(v):
    phi = 0.5 + 0.5 * lax.erf(v * 0.7071067811865476)
    return v * phi, phi + v * (0.3989422804014327 * jnp.exp2(v * v * -0.7213475204444817))


def mean(v):
    return jnp.sum(v, axis=-1, keepdims=True) * (1.0 / v.shape[-1])


def fold(v):
    return sum(v[r : r + 8] for r in range(0, v.shape[0], 8))


def slabs(total, size):
    return [pl.ds(r, size) for r in range(0, total, size)]


def colsum(v):
    return jnp.sum(v, axis=0, keepdims=True)


def vmem(mib):
    return pltpu.CompilerParams(vmem_limit_bytes=mib << 20)


def cost(macs, nbytes):
    return pl.CostEstimate(flops=macs // 32, bytes_accessed=nbytes // 32, transcendentals=0)


def whole(shape):
    return pl.BlockSpec(shape, lambda *_: (0,) * len(shape), pipeline_mode=pl.Buffered(1))


def rows_of(tile, width):
    return pl.BlockSpec((tile, width), lambda i: (i, 0))


def window_bounds(len_ref, position, wins, total):
    first = jnp.zeros_like(position)
    last = jnp.full_like(position, total)
    edge = jnp.int32(0)
    edges = []
    for w in range(wins - 1):
        edge = edge + len_ref[0, w]
        edges.append(edge)
    for edge in edges:
        first = jnp.where(position >= edge, edge, first)
    for edge in reversed(edges):
        last = jnp.where(position < edge, edge, last)
    return first, last


def wide(mask, width):
    return jnp.concatenate([mask] * (width // 128), axis=1)


def prep_kernel(len_ref, place_ref, tokens_ref, present_ref, stacked_ref, masked_ref, keep_ref, even, odd, *, tile, wins):
    step = pl.program_id(0)
    rows, width = tokens_ref.shape
    start = pl.multiple_of(step * tile, tile)

    @pl.when(step == 0)
    def _():
        edge = jnp.zeros((REACH, width), bf16)
        even[:REACH] = edge
        even[rows + REACH :] = edge
        odd[:REACH] = edge
        odd[rows : rows + REACH] = edge
        odd[rows + REACH :] = edge
        for r in range(0, rows, 128):
            line = jnp.broadcast_to((present_ref[r // 128 : r // 128 + 1] > 0).astype(f32), (128, 128))
            kept = line.T
            keep_ref[r : r + 128] = kept
            block = tokens_ref[r : r + 128] * wide(kept.astype(bf16), width)
            even[REACH + r : REACH + r + 128] = block
            odd[REACH - STEP + r : REACH - STEP + r + 128] = block

    masked_ref[...] = even[pl.ds(start + REACH, tile)].T
    position = lax.broadcasted_iota(jnp.int32, (tile, 128), 0) + start
    first, last = window_bounds(len_ref, position, wins, rows)
    per = TAPS * width // 128 // QUARTERS
    for tap in range(TAPS):
        other = position + (tap - TAPS // 2) * STEP
        valid = ((other >= first) & (other < last)).astype(bf16)
        offset = pl.multiple_of(start + tap // 2 * 2 * STEP, 2 * STEP)
        block = (odd if tap % 2 else even)[pl.ds(offset, tile)] * wide(valid, width)
        for lane in range(0, width, 128):
            chunk = (tap * width + lane) // 128
            seat = ((chunk // per) ^ place_ref[2]) * per + chunk % per
            stacked_ref[:, pl.ds(pl.multiple_of(seat * 128, 128), 128)] = block[:, lane : lane + 128]


def prep(lengths, place, tokens, present):
    rows, width = tokens.shape
    tile = 256
    return pl.pallas_call(
        functools.partial(prep_kernel, tile=tile, wins=lengths.shape[1]),
        grid=(rows // tile,),
        in_specs=[SMEM, SMEM, whole((rows, width)), whole((rows // 128, 128))],
        out_specs=[
            rows_of(tile, TAPS * width), pl.BlockSpec((width, tile), lambda i: (0, i)), pl.BlockSpec((rows, 128), lambda i: (0, 0))
        ],
        out_shape=[
            jax.ShapeDtypeStruct((rows, TAPS * width), bf16),
            jax.ShapeDtypeStruct((width, rows), bf16),
            jax.ShapeDtypeStruct((rows, 128), f32),
        ],
        scratch_shapes=[pltpu.VMEM((rows + 2 * REACH, width), bf16), pltpu.VMEM((rows + 2 * REACH, width), bf16)],
        compiler_params=vmem(63),
        cost_estimate=cost(0, 24 * rows * width),
        name="prep",
    )(lengths, place, tokens, present.reshape(rows // 128, 128))


def conv_sites(pieces, first, place, fast, body):
    if not fast:
        return [(piece.at[0], first, 0) for piece in pieces]
    core, z, _ = place
    sites = []
    per = len(pieces) // 2
    for n, piece in enumerate(pieces):
        which = core if n < per else 1 - core
        kind = first + n % per
        for hop in range(piece.shape[0]):
            row = (((z - hop - (2 if kind == 4 else 0)) & 3) * 2 + which) * body
            sites.append((piece.at[hop], min(kind, 3), row))
    return sites


def conv_copies(sites, base, store, sems):
    copies = []
    for n, (source, kind, row) in enumerate(sites):
        start = pl.multiple_of(base(kind) + row, 16)
        copies.append(pltpu.make_async_copy(source, store.at[pl.ds(start, source.shape[0])], sems.at[n]))
    return copies


def conv_kernel(place_ref, *refs, fast, body):
    *pieces, stacked_ref, conv_ref, near_ref, store, sems, out_sem = refs
    depth = store.shape[0] // (QUARTERS - 1)
    back = pltpu.make_async_copy(store, near_ref, out_sem)

    @pl.when(pl.program_id(0) == 0)
    def _():
        sites = conv_sites(pieces, 0, tuple(place_ref[i] for i in range(3)), fast, body)
        copies = conv_copies(sites, lambda kind: kind * depth, store, sems)
        for copy in copies:
            copy.start()
        for copy in copies:
            copy.wait()
        back.start()

    conv_ref[...] = dot(stacked_ref[...], store[...])

    @pl.when(pl.program_id(0) == pl.num_programs(0) - 1)
    def _():
        back.wait()


def conv_forward(place, pieces, stacked, fast, body):
    rows, depth = stacked.shape
    width = pieces[0].shape[2]
    depth = depth // QUARTERS * (QUARTERS - 1)
    tile = 512
    return pl.pallas_call(
        functools.partial(conv_kernel, fast=fast, body=body),
        grid=(rows // tile,),
        in_specs=[SMEM] + [ANY] * len(pieces) + [rows_of(tile, depth)],
        out_specs=[rows_of(tile, width), ANY],
        out_shape=[jax.ShapeDtypeStruct((rows, width), f32), jax.ShapeDtypeStruct((depth, width), bf16)],
        scratch_shapes=[
            pltpu.VMEM((depth, width), bf16),
            pltpu.SemaphoreType.DMA((sum(piece.shape[0] for piece in pieces),)),
            pltpu.SemaphoreType.DMA,
        ],
        compiler_params=vmem(63),
        cost_estimate=cost(depth * rows * width, 24 * rows * width),
        name="conv_forward",
    )(place, *pieces, stacked)


def ff_copies(pieces, place, fast, store, sems):
    if not fast:
        return [pltpu.make_async_copy(pieces[0], store, sems.at[0])]
    core, own_z, dp = place
    per = len(pieces) // 2
    copies = []
    for n, piece in enumerate(pieces):
        which = core if n < per else 1 - core
        kind = n % per
        for hop in range(piece.shape[0]):
            z = (own_z - hop - (2 if kind == 4 else 0)) & 3
            block = ((dp ^ min(kind, 3)) * 4 + z) * 2 + which
            copies.append(pltpu.make_async_copy(piece.at[hop], store.at[block], sems.at[len(copies)]))
    return copies


def relay_seat(r, k):
    if k < 2:
        return (1, r // 2 * 2 + k) if r % 2 else (0, r // 2 * 2 + k)
    return (2, r % 2 * 2 + k - 2) if r // 2 else (0, 4 + r * 2 + k - 2)


def feed_kernel(place_ref, *refs, far, count, outs, tiles, chunk, inner_rows, outer_rows, extra, fast, body):
    far_pieces, ff_pieces = refs[:far], refs[far : far + count]
    refs = refs[far + count :]
    stacked_ref, partial_ref, tokens_ref, cot_ref = refs[:4]
    mixed_ref, d_hidden_ref, d_conv_ref, sums_ref, far_ref = refs[4:9]
    targets = refs[9 : 9 + outs]
    refs = refs[9 + outs :]
    packed, w_in, w_far, small_ref, bend, slope_ref, normed_ref, hiddens, actives, d_outers, d_inners = refs[:11]
    tallies, ff_sems, far_sems, grad_sems, out_sem = refs[11:]
    slab = SLAB
    store = packed
    step = pl.program_id(0)
    tile, width = tokens_ref.shape
    total = w_in.shape[1]
    blocks = packed.shape[0]
    cols = total // width
    place = tuple(place_ref[i] for i in range(3))
    core = place[0]
    depth = w_far.shape[0]
    top = cols * inner_rows
    back = pltpu.make_async_copy(w_far, far_ref, out_sem)

    @pl.when(step == 0)
    def _():
        copies = ff_copies(ff_pieces, place, fast, packed, ff_sems)
        far_sites = conv_sites(far_pieces, QUARTERS - 1, place, fast, body)
        copies += conv_copies(far_sites, lambda kind: 0, w_far, far_sems)
        for copy in copies:
            copy.start()
        tallies[...] = jnp.zeros_like(tallies)
        for copy in copies:
            copy.wait()
        back.start()
        for j in range(cols):
            part = packed[:, j * inner_rows : (j + 1) * inner_rows].reshape(blocks * inner_rows, width)
            w_in[:, j * width : (j + 1) * width] = part
        small_ref[...] = jnp.sum(packed[:, top : top + extra].astype(f32), axis=0)

    base = pl.multiple_of(jnp.minimum(step, tiles - 1) * tile, tile)

    def at(part):
        return pl.ds(pl.multiple_of(base + part.start, part.size), part.size)

    def add_tally(row, col, term):
        tallies[8 * row : 8 * row + 8, col : col + term.shape[1]] += fold(term)

    def out_rows(j):
        if outer_rows > chunk:
            per = outer_rows // chunk
            first = top + extra + j % per * chunk
            return packed[j // per, first : first + chunk]
        count = chunk // outer_rows
        return packed[j * count : (j + 1) * count, top + extra :].reshape(chunk, width)

    in_rows = step < tiles

    @pl.when(in_rows)
    def _():
        for part in slabs(tile, slab):
            conv = partial_ref[part] + dot(stacked_ref[part], w_far[...]) + small_ref[0:1]
            bent, slope = gelu_pair(conv)
            shifted = bent - mean(bent)
            root = lax.rsqrt(mean(shifted * shifted) + EPSILON)
            normed = shifted * root
            normed_ref[part] = normed
            slope_ref[part] = slope * root
            hiddens[at(part)] = (
                tokens_ref[part].astype(f32) + normed * small_ref[1:2] + small_ref[2:3]
            ).astype(bf16)

    for j in range(total // chunk):
        cut = slice(j * chunk, (j + 1) * chunk)

        @pl.when(in_rows)
        def _(j=j, cut=cut):
            for part in slabs(tile, slab):
                inner = dot(hiddens[at(part)], w_in[:, cut]) + small_ref[6 + j : 7 + j]
                act, slope = gelu_pair(inner)
                actives[at(part), cut] = act.astype(bf16)
                bend[part, cut] = slope

    @pl.when(in_rows)
    def _():
        gain_two = small_ref[4:5]
        for part in slabs(tile, slab):
            full = packed[:, top + extra :].reshape(blocks * outer_rows, width)
            outer = dot(actives[at(part)], full) + small_ref[3:4]
            shifted = outer - mean(outer)
            root = lax.rsqrt(mean(shifted * shifted) + EPSILON)
            normal = shifted * root
            mixed_ref[part] = (hiddens[at(part)].astype(f32) + normal * gain_two + small_ref[5:6]).astype(bf16)
            cot = cot_ref[part].astype(f32)
            q = cot * gain_two
            d_outer = (root * (q - mean(q) - normal * mean(q * normal))).astype(bf16)
            d_outers[at(part)] = d_outer
            add_tally(3, 0, d_outer.astype(f32))
            add_tally(4, 0, cot * normal)
            add_tally(5, 0, cot)

    for j in range(total // chunk):
        cut = slice(j * chunk, (j + 1) * chunk)

        @pl.when(in_rows)
        def _(j=j, cut=cut):
            for part in slabs(tile, slab):
                d_inner = (dot_t(d_outers[at(part)], out_rows(j)) * bend[part, cut]).astype(bf16)
                d_inners[at(part), cut] = d_inner
                add_tally(6 + j, 0, d_inner.astype(f32))

    @pl.when(in_rows)
    def _():
        for part in slabs(tile, slab):
            d_hidden = dot_t(d_inners[at(part)], w_in[...]) + cot_ref[part].astype(f32)
            d_hidden_ref[part] = d_hidden
            first = normed_ref[part]
            p = d_hidden * small_ref[1:2]
            d_conv = (slope_ref[part] * (p - mean(p) - first * mean(p * first))).astype(bf16)
            d_conv_ref[part] = d_conv
            add_tally(0, 0, d_conv.astype(f32))
            add_tally(1, 0, d_hidden * first)
            add_tally(2, 0, d_hidden)

    def grad_copies():
        copies = []
        if not fast:
            for n, target in enumerate(targets):
                copies.append(pltpu.make_async_copy(store.at[pl.ds(n, 1)], target, grad_sems.at[n]))
            return copies
        for n, which in enumerate((core, 1 - core)):
            for r in range(4):
                for k in range(4):
                    array, seat = relay_seat(r, k)
                    block = ((place[2] ^ r) * 4 + ((place[1] + k) & 3)) * 2 + which
                    copies.append(
                        pltpu.make_async_copy(store.at[block], targets[3 * n + array].at[seat], grad_sems.at[len(copies)])
                    )
        return copies

    @pl.when(step >= tiles)
    def _():
        j = step - tiles
        part = pl.ds(pl.multiple_of(j * width, width), width)
        d_out = dot_rows(actives[:, part], d_outers[...]).astype(bf16)
        first = top + extra
        if fast:
            many = width // outer_rows
            store[pl.ds(j * many, many), first : first + outer_rows] = d_out.reshape(many, outer_rows, width)
        else:
            per = outer_rows // width
            start = pl.multiple_of(first + (j % per) * width, 16)
            store[pl.ds(j // per, 1), pl.ds(start, width)] = d_out.reshape(1, width, width)
        d_in = dot_rows(hiddens[...], d_inners[:, part]).astype(bf16)
        above = pl.ds(pl.multiple_of(j * inner_rows, inner_rows), inner_rows)
        store[:, above] = d_in.reshape(blocks, inner_rows, width)

    @pl.when(step == pl.num_programs(0) - 1)
    def _():
        back.wait()
        for row in range(sums_ref.shape[0]):
            sums_ref[row : row + 1] = colsum(tallies[8 * row : 8 * row + 8])
        if fast:
            head = sums_ref[:6].astype(bf16)
            rest = jnp.zeros((extra - 7, width), bf16)
            for dp in range(blocks // 8):
                line = jnp.concatenate([head, sums_ref[6 + dp : 7 + dp].astype(bf16), rest])
                store[8 * dp : 8 * dp + 8, top : top + extra] = jnp.broadcast_to(line, (8, extra, width))
        copies = grad_copies()
        for copy in copies:
            copy.start()
        for copy in copies:
            copy.wait()


def feed(place, far, pieces, stacked, partial, tokens, cotangent, inner_rows, outer_rows, extra, total, fast, body):
    rows, width = tokens.shape
    blocks = width // inner_rows
    tile = 512
    tiles, cols = rows // tile, total // width
    share = cols * inner_rows + extra + outer_rows
    depth = stacked.shape[1] // QUARTERS
    seats = (8, 4, 4) * 2 if fast else (1, 1)
    tall = pl.BlockSpec((tile, width), lambda i: (jnp.minimum(i, tiles - 1), 0))
    last = pl.BlockSpec((tile, depth), lambda i: (jnp.minimum(i, tiles - 1), QUARTERS - 1))
    return pl.pallas_call(
        functools.partial(
            feed_kernel, far=len(far), count=len(pieces), outs=len(seats), tiles=tiles, chunk=512, inner_rows=inner_rows,
            outer_rows=outer_rows, extra=extra, fast=fast, body=body,
        ),
        grid=(tiles + cols,),
        in_specs=[SMEM] + [ANY] * (len(far) + len(pieces)) + [last, tall, tall, tall],
        out_specs=[tall, tall, tall, pl.BlockSpec((16, width), lambda i: (0, 0)), ANY] + [ANY] * len(seats),
        out_shape=[
            jax.ShapeDtypeStruct((rows, width), bf16),
            jax.ShapeDtypeStruct((rows, width), f32),
            jax.ShapeDtypeStruct((rows, width), bf16),
            jax.ShapeDtypeStruct((16, width), f32),
            jax.ShapeDtypeStruct((depth, width), bf16),
        ] + [jax.ShapeDtypeStruct((count, share, width), bf16) for count in seats],
        scratch_shapes=[
            pltpu.VMEM((blocks, share, width), bf16),
            pltpu.VMEM((width, total), bf16),
            pltpu.VMEM((depth, width), bf16),
            pltpu.VMEM((extra, width), f32),
            pltpu.VMEM((tile, total), f32),
            pltpu.VMEM((tile, width), f32),
            pltpu.VMEM((tile, width), f32),
            pltpu.VMEM((rows, width), bf16),
            pltpu.VMEM((rows, total), bf16),
            pltpu.VMEM((rows, width), bf16),
            pltpu.VMEM((rows, total), bf16),
            pltpu.VMEM((8 * extra, width), f32),
            pltpu.SemaphoreType.DMA((sum(piece.shape[0] for piece in pieces),)),
            pltpu.SemaphoreType.DMA((sum(piece.shape[0] for piece in far),)),
            pltpu.SemaphoreType.DMA((blocks,)),
            pltpu.SemaphoreType.DMA,
        ],
        compiler_params=vmem(63),
        cost_estimate=cost(6 * rows * width * total, 40 * rows * width),
        name="feed",
    )(place, *far, *pieces, stacked, partial, tokens, cotangent)


def lay_shifted(values_ref, even, odd, tile):
    rows, width = values_ref.shape
    zeros = jnp.zeros((REACH, width), bf16)
    even[:REACH] = zeros
    even[rows + REACH :] = zeros
    odd[:REACH] = zeros
    odd[rows:] = jnp.zeros((2 * REACH, width), bf16)
    for r in range(0, rows, tile):
        block = values_ref[r : r + tile]
        even[REACH + r : REACH + r + tile] = block
        odd[REACH - STEP + r : REACH - STEP + r + tile] = block


def tap_products(len_ref, place, masked_ref, even, odd, part, targets, store, sems, *, wins, blocks, body, turn):
    channels, rows = masked_ref.shape
    width = part.stop - part.start
    core = place[0]
    position = lax.broadcasted_iota(jnp.int32, (rows, 128), 0)
    first, last = window_bounds(len_ref, position, wins, rows)
    copies = []
    for tap in range(TAPS):
        mirror = TAPS - 1 - tap
        other = position + (mirror - TAPS // 2) * STEP
        valid = ((other >= first) & (other < last)).astype(bf16)
        source = (odd if mirror % 2 else even)[mirror // 2 * 2 * STEP : mirror // 2 * 2 * STEP + rows, part]
        store[tap * channels : (tap + 1) * channels] = dot(masked_ref[...], source * wide(valid, width)).astype(bf16)
        while len(copies) // 2 < blocks and (len(copies) // 2 + 1) * 2 * body <= (tap + 1) * channels:
            block = len(copies) // 2
            seat = ((block // 4) ^ turn) * 4 + ((block % 4 - place[1]) & 3) if blocks == 16 else block
            for n, (target, which) in enumerate(zip(targets, (core, 1 - core))):
                start = pl.multiple_of((2 * block + which) * body, 16)
                copies.append(pltpu.make_async_copy(store.at[pl.ds(start, body)], target.at[seat], sems.at[n, block]))
                copies[-1].start()
    for copy in copies:
        copy.wait()


def conv_grad_kernel(len_ref, place_ref, masked_ref, d_conv_ref, keep_ref, send_ref, even, odd, store, sems, *, wins, blocks, body):
    lay_shifted(d_conv_ref, even, odd, 256)
    tap_products(
        len_ref, tuple(place_ref[i] for i in range(3)), masked_ref, even, odd, slice(0, d_conv_ref.shape[1]),
        (keep_ref, send_ref), store, sems, wins=wins, blocks=blocks, body=body, turn=0,
    )


def conv_grad(lengths, place, masked, d_conv, blocks, body):
    channels, rows = masked.shape
    width = d_conv.shape[1]
    return pl.pallas_call(
        functools.partial(conv_grad_kernel, wins=lengths.shape[1], blocks=blocks, body=body),
        grid=(1,),
        in_specs=[SMEM, SMEM, whole(masked.shape), whole((rows, width))],
        out_specs=[ANY, ANY],
        out_shape=[jax.ShapeDtypeStruct((blocks, body, width), bf16)] * 2,
        scratch_shapes=[
            pltpu.VMEM((rows + 2 * REACH, width), bf16),
            pltpu.VMEM((rows + 2 * REACH, width), bf16),
            pltpu.VMEM((TAPS * channels, width), bf16),
            pltpu.SemaphoreType.DMA((2, blocks)),
        ],
        compiler_params=vmem(63),
        cost_estimate=cost(TAPS * rows * width * channels, 12 * rows * width),
        name="conv_grad",
    )(lengths, place, masked, d_conv)


def token_grad_kernel(
    len_ref, place_ref, near_ref, far_ref, d_conv_ref, d_hidden_ref, keep_ref, d_tokens_ref, even, odd, store, sems, *, wins, tile
):
    step = pl.program_id(0)
    rows, width = d_conv_ref.shape
    depth = far_ref.shape[0]

    @pl.when(step == 0)
    def _():
        copies = []
        for kind in range(QUARTERS):
            source = far_ref if kind == QUARTERS - 1 else near_ref.at[pl.ds(kind * depth, depth)]
            start = pl.multiple_of((place_ref[2] ^ kind) * depth, 128)
            copies.append(pltpu.make_async_copy(source, store.at[pl.ds(start, depth)], sems.at[kind]))
        for copy in copies:
            copy.start()
        lay_shifted(d_conv_ref, even, odd, 256)
        for copy in copies:
            copy.wait()

    start = pl.multiple_of(step * tile, tile)
    position = lax.broadcasted_iota(jnp.int32, (tile, 128), 0) + start
    first, last = window_bounds(len_ref, position, wins, rows)
    total = None
    for tap in range(TAPS):
        mirror = TAPS - 1 - tap
        other_row = position + (mirror - TAPS // 2) * STEP
        valid = ((other_row >= first) & (other_row < last)).astype(bf16)
        offset = pl.multiple_of(start + mirror // 2 * 2 * STEP, 2 * STEP)
        block = (odd if mirror % 2 else even)[pl.ds(offset, tile)] * wide(valid, width)
        term = dot_t(block, store[tap * width : (tap + 1) * width])
        total = term if total is None else total + term
    d_tokens_ref[...] = d_hidden_ref[...] + total * wide(keep_ref[...], width)


def token_grad(lengths, place, near, far, d_conv, d_hidden, keep):
    rows, width = d_conv.shape
    tile = 512
    return pl.pallas_call(
        functools.partial(token_grad_kernel, wins=lengths.shape[1], tile=tile),
        grid=(rows // tile,),
        in_specs=[SMEM, SMEM, ANY, ANY, whole((rows, width)), rows_of(tile, width), rows_of(tile, 128)],
        out_specs=rows_of(tile, width),
        out_shape=jax.ShapeDtypeStruct((rows, width), f32),
        scratch_shapes=[
            pltpu.VMEM((rows + 2 * REACH, width), bf16),
            pltpu.VMEM((rows + 2 * REACH, width), bf16),
            pltpu.VMEM((TAPS * width, width), bf16),
            pltpu.SemaphoreType.DMA((QUARTERS,)),
        ],
        compiler_params=vmem(63),
        cost_estimate=cost(TAPS * rows * width * width, 12 * rows * width),
        name="token_grad",
    )(lengths, place, near, far, d_conv, d_hidden, keep)


def on_device(
    n_dp, n_fsdp, tokens, present, lengths, conv_w, conv_b, gain_one, shift_one, w_in, b_in, w_out, b_out, gain_two, shift_two, cotangent
):
    rows, width = tokens.shape
    total = w_in.shape[1]
    cols = total // width
    devices = n_dp * n_fsdp
    fast = n_dp == 4 and n_fsdp == 8 and conv_w.shape[0] % 16 == 0 and w_in.shape[0] % 16 == 0
    bar = lax.optimization_barrier
    extra = 16
    n = width // devices
    swap = [(i, i ^ 1) for i in range(n_fsdp)]
    across = {r: [(i, i ^ r) for i in range(n_dp)] for r in (1, 2, 3)}
    along = {k: [(i, (i + 2 * k) % n_fsdp) for i in range(n_fsdp)] for k in (1, 2, 3)}
    vectors = (conv_b, gain_one, shift_one, b_out, gain_two, shift_two)
    if fast:
        fsdp = lax.axis_index("fsdp").astype(jnp.int32)
        dp = lax.axis_index("dp").astype(jnp.int32)
        place = jnp.stack([fsdp & 1, fsdp >> 1, dp])
        body = conv_w.shape[0]
        inner_rows, outer_rows = w_in.shape[0], w_out.shape[0]
        blocks = devices // 2

        def from_column(shard):
            return [shard] + [lax.ppermute(shard, "fsdp", along[k]) for k in (1, 2, 3)]

        column = jnp.stack(from_column(conv_w))
        seat = dp * n_fsdp + fsdp
        lane = jnp.arange(width, dtype=jnp.int32)
        line = jnp.arange(extra, dtype=jnp.int32)[:, None]
        lines = jnp.concatenate(
            [jnp.tile(jnp.stack(vectors), (1, devices))]
            + [jnp.tile(b_in, width // b_in.shape[0])[None]] * cols
            + [jnp.zeros((extra - 6 - cols, width), bf16)]
        )
        few = b_in.shape[0]
        own_line = ((line < 6) & (lane // n == seat)) | ((line == 6 + dp) & (lane // few == fsdp))
        lines = jnp.where(own_line, lines, 0)
        ff_own = jnp.concatenate([w_in[:, j * width : (j + 1) * width] for j in range(cols)] + [lines, w_out], axis=0)
        column, ff_own, late_tokens = bar((column, ff_own, tokens))
        beside_x = lax.ppermute(column, "dp", across[1])
        beside_y = lax.ppermute(column, "dp", across[2])
        ff_rest = from_column(ff_own)
        stacked, masked, keep = prep(lengths, place, late_tokens, present)
        column, beside_x, beside_y, ff_rest, stacked, masked, keep = bar(
            (column, beside_x, beside_y, ff_rest, stacked, masked, keep)
        )
        ff_column = jnp.stack(ff_rest)
        near = (column, beside_x, beside_y)
        near = near + tuple(lax.ppermute(piece, "fsdp", swap) for piece in near)
        far = (
            lax.ppermute(beside_x[:2], "dp", across[2]),
            lax.ppermute(beside_y[2:], "dp", across[1]),
        )
        ff = (ff_column, lax.ppermute(ff_column, "dp", across[1]), lax.ppermute(ff_column, "dp", across[2]))
    else:
        place = jnp.zeros((3,), jnp.int32)
        gather = functools.partial(lax.all_gather, axis_name=AXES, axis=0, tiled=True)
        full = gather(conv_w)
        body = full.shape[0] // 2
        depth = full.shape[0] // QUARTERS * (QUARTERS - 1)
        near, far = (full[None, :depth],), (full[None, depth:],)
        lines = [gather(vector) for vector in vectors] + list(gather(b_in).reshape(cols, width))
        lines = jnp.stack(lines + [jnp.zeros_like(lines[0])] * (extra - len(lines)))
        full_in, full_out = gather(w_in), gather(w_out)
        inner_rows, outer_rows = full_in.shape[0] // 2, full_out.shape[0] // 2
        blocks = 1
        ff = [full_in[:, j * width : (j + 1) * width].reshape(2, inner_rows, width) for j in range(cols)]
        ff.append(jnp.stack([lines, jnp.zeros_like(lines)]))
        ff = (jnp.concatenate(ff + [full_out.reshape(2, outer_rows, width)], axis=1),)
        stacked, masked, keep = prep(lengths, place, tokens, present)

    partial, w_near = conv_forward(place, near, stacked, fast, body)
    if fast:
        far, ff, partial = bar((far, ff, partial))
        ff = ff + (
            lax.ppermute(ff[1][:2], "dp", across[2]),
            lax.ppermute(ff[2][2:], "dp", across[1]),
        )
        far = far + tuple(lax.ppermute(piece, "fsdp", swap) for piece in far)
        ff = ff + tuple(lax.ppermute(piece, "fsdp", swap) for piece in ff)
    mixed, d_hidden, d_conv, sums, w_far, *ff_grads = feed(
        place, far, ff, stacked, partial, tokens, cotangent, inner_rows, outer_rows, extra, total, fast, body
    )
    def added(terms):
        return sum(term.astype(f32) for term in terms)

    def line_swap(line):
        return [line[0]] + [lax.ppermute(line[k], "fsdp", along[k]) for k in (1, 2, 3)]

    def rounded(*terms):
        return added(terms).astype(bf16)

    if fast:
        ff_near, ff_far_a, ff_far_b = ff_grads[:3]
        came_a, came_b, came = (lax.ppermute(ff_grads[3 + n], "fsdp", swap) for n in (1, 2, 0))
        a_far, b_far, d_conv = bar((ff_far_a + came_a, ff_far_b + came_b, d_conv))
        a_came = lax.ppermute(a_far, "dp", across[1])
        b_came = lax.ppermute(b_far, "dp", across[2])
        conv_keep, conv_send = conv_grad(lengths, place, masked, d_conv, blocks, body)
        a_came, b_came, came, conv_keep, conv_send, d_conv = bar((a_came, b_came, came, conv_keep, conv_send, d_conv))
        conv_came = lax.ppermute(conv_send, "fsdp", swap)
        a_last = lax.ppermute(rounded(ff_near[2:4], came[2:4], a_came[2:]), "dp", across[2])
        b_last = lax.ppermute(rounded(ff_near[6:], came[6:], b_came[2:]), "dp", across[1])
        conv_chip = conv_keep + conv_came
        conv_chip, a_last, b_last, d_conv = bar((conv_chip, a_last, b_last, d_conv))
        conv_plane = lax.all_to_all(conv_chip.reshape(4, 4, body, width), "dp", 0, 0, tiled=True)
        line = [rounded(ff_near[k], came[k], a_came[k], a_last[k]) for k in (0, 1)]
        line += [rounded(ff_near[4 + k], came[4 + k], b_came[k], b_last[k]) for k in (0, 1)]
        ff_line = line_swap(line)
        d_tokens = token_grad(lengths, place, w_near, w_far, d_conv, d_hidden, keep)
        d_tokens, ff_line, conv_plane = bar((d_tokens, ff_line, conv_plane))
        conv_line = line_swap([added(conv_plane[r, k] for r in range(4)).astype(bf16) for k in range(4)])
        ff_share = added(ff_line)
        d_conv_w = added(conv_line)
        top = cols * inner_rows
        d_w_in = jnp.concatenate([ff_share[j * inner_rows : (j + 1) * inner_rows] for j in range(cols)], axis=1)
        d_w_out = ff_share[top + extra :]
        seat = dp * n_fsdp + fsdp
        own = lax.dynamic_slice(ff_share[top : top + 6], (0, seat * n), (6, n))
        vector_grads = list(own)
        vector_grads.append(lax.dynamic_slice(ff_share[top + 6], (fsdp * few,), (few,)))
    else:
        conv_pair = conv_grad(lengths, place, masked, d_conv, blocks, body)
        d_tokens = token_grad(lengths, place, w_near, w_far, d_conv, d_hidden, keep)
        ff_share = jnp.concatenate(ff_grads, axis=0)
        scatter = functools.partial(lax.psum_scatter, axis_name=AXES, scatter_dimension=0, tiled=True)
        d_in_full = jnp.concatenate(
            [ff_share[:, j * inner_rows : (j + 1) * inner_rows].reshape(-1, width) for j in range(cols)], axis=1
        )
        d_w_in = scatter(d_in_full.astype(f32))
        d_w_out = scatter(ff_share[:, cols * inner_rows + extra :].reshape(-1, width).astype(f32))
        d_conv_w = scatter(jnp.concatenate(conv_pair, axis=0).reshape(-1, width).astype(f32))
        vector_grads = [scatter(line) for line in sums[:6]] + [scatter(sums[6 : 6 + cols].reshape(-1))]
    d_conv_b, d_gain_one, d_shift_one, d_b_out, d_gain_two, d_shift_two, d_b_in = vector_grads
    return (
        mixed, d_tokens, d_conv_w, d_conv_b, d_gain_one, d_shift_one, d_w_in, d_b_in, d_w_out, d_b_out, d_gain_two, d_shift_two
    )


def solution(mesh):
    both = P(AXES)
    flat = P(AXES, None)
    in_specs = (flat, both, flat, flat, both, both, both, flat, both, flat, both, both, both, flat)
    out_specs = (flat, flat, flat, both, both, both, flat, both, flat, both, both, both)
    return jax.shard_map(
        functools.partial(on_device, mesh.shape["dp"], mesh.shape["fsdp"]),
        mesh=mesh,
        in_specs=in_specs,
        out_specs=out_specs,
        check_vma=False,
    )
```

```python
import functools
import jax
import jax.numpy as jnp
from jax import lax
from jax.experimental import pallas as pl
from jax.experimental.pallas import tpu as pltpu
from jax.sharding import PartitionSpec as P

TAPS = 9
STEP = 8
REACH = (TAPS // 2) * STEP
EPSILON = 1e-05
SLAB = 512
QUARTERS = 4
AXES = ("dp", "fsdp")
f32 = jnp.float32
bf16 = jnp.bfloat16
ANY = pl.BlockSpec(memory_space=pl.ANY)
SMEM = pl.BlockSpec(memory_space=pltpu.SMEM)


def dot(a, b):
    return jnp.dot(a, b, preferred_element_type=f32)


def dot_t(a, b):
    return lax.dot_general(a, b, (((1,), (1,)), ((), ())), preferred_element_type=f32)


def dot_rows(a, b):
    return lax.dot_general(a, b, (((0,), (0,)), ((), ())), preferred_element_type=f32)


def gelu_pair(v):
    phi = 0.5 + 0.5 * lax.erf(v * 0.7071067811865476)
    return v * phi, phi + v * (0.3989422804014327 * jnp.exp2(v * v * -0.7213475204444817))


def mean(v):
    return jnp.sum(v, axis=-1, keepdims=True) * (1.0 / v.shape[-1])


def fold(v):
    return sum(v[r : r + 8] for r in range(0, v.shape[0], 8))


def slabs(total, size):
    return [pl.ds(r, size) for r in range(0, total, size)]


def colsum(v):
    return jnp.sum(v, axis=0, keepdims=True)


def vmem(mib):
    return pltpu.CompilerParams(vmem_limit_bytes=mib << 20)


def cost(macs, nbytes):
    return pl.CostEstimate(flops=macs // 32, bytes_accessed=nbytes // 32, transcendentals=0)


def whole(shape):
    return pl.BlockSpec(shape, lambda *_: (0,) * len(shape), pipeline_mode=pl.Buffered(1))


def rows_of(tile, width):
    return pl.BlockSpec((tile, width), lambda i: (i, 0))


def window_bounds(len_ref, position, wins, total):
    first = jnp.zeros_like(position)
    last = jnp.full_like(position, total)
    edge = jnp.int32(0)
    edges = []
    for w in range(wins - 1):
        edge = edge + len_ref[0, w]
        edges.append(edge)
    for edge in edges:
        first = jnp.where(position >= edge, edge, first)
    for edge in reversed(edges):
        last = jnp.where(position < edge, edge, last)
    return first, last


def wide(mask, width):
    return jnp.concatenate([mask] * (width // 128), axis=1)


def prep_kernel(tokens_ref, present_ref, masked_ref, across_ref, keep_ref):
    tile, width = tokens_ref.shape
    for r in range(0, tile, 128):
        line = jnp.broadcast_to((present_ref[0, r // 128 : r // 128 + 1] > 0).astype(f32), (128, 128))
        kept = line.T
        keep_ref[r : r + 128] = kept
        masked_ref[r : r + 128] = tokens_ref[r : r + 128] * wide(kept.astype(bf16), width)
    across_ref[...] = masked_ref[...].T


def prep(tokens, present):
    rows, width = tokens.shape
    tile = 512
    return pl.pallas_call(
        prep_kernel,
        grid=(rows // tile,),
        in_specs=[rows_of(tile, width), pl.BlockSpec((1, tile // 128, 128), lambda i: (i, 0, 0))],
        out_specs=[rows_of(tile, width), pl.BlockSpec((width, tile), lambda i: (0, i)), rows_of(tile, 128)],
        out_shape=[
            jax.ShapeDtypeStruct((rows, width), bf16),
            jax.ShapeDtypeStruct((width, rows), bf16),
            jax.ShapeDtypeStruct((rows, 128), f32),
        ],
        compiler_params=vmem(63),
        cost_estimate=cost(0, 24 * rows * width),
        name="prep",
    )(tokens, present.reshape(rows // tile, tile // 128, 128))


def conv_sites(pieces, first, place, fast, body):
    if not fast:
        return [(piece.at[0], first, 0) for piece in pieces]
    core, z, _ = place
    sites = []
    per = len(pieces) // 2
    for n, piece in enumerate(pieces):
        which = core if n < per else 1 - core
        kind = first + n % per
        for hop in range(piece.shape[0]):
            row = (((z - hop - (2 if kind == 4 else 0)) & 3) * 2 + which) * body
            sites.append((piece.at[hop], min(kind, 3), row))
    return sites


def conv_copies(sites, base, store, sems):
    copies = []
    for n, (source, kind, row) in enumerate(sites):
        start = pl.multiple_of(base(kind) + row, 16)
        copies.append(pltpu.make_async_copy(source, store.at[pl.ds(start, source.shape[0])], sems.at[n]))
    return copies


def conv_kernel(len_ref, place_ref, *refs, count, fast, body, wins):
    pieces = refs[:count]
    masked_ref, conv_ref, far_ref, near_ref, store, stack, even, odd, sems, out_sem = refs[count:]
    step = pl.program_id(0)
    rows, width = masked_ref.shape
    tile = conv_ref.shape[0]
    depth = store.shape[0] // (QUARTERS - 1)
    back = pltpu.make_async_copy(store, near_ref, out_sem)
    sites = conv_sites(pieces, 0, tuple(place_ref[i] for i in range(3)), fast, body)
    copies = conv_copies(sites, lambda kind: kind * depth, store, sems)

    @pl.when(step == 0)
    def _():
        for copy in copies:
            copy.start()
        lay_shifted(masked_ref, even, odd, 256)

    start = pl.multiple_of(step * tile, tile)
    position = lax.broadcasted_iota(jnp.int32, (tile, 128), 0) + start
    first, last = window_bounds(len_ref, position, wins, rows)
    per = depth // 128
    for tap in range(TAPS):
        other = position + (tap - TAPS // 2) * STEP
        valid = ((other >= first) & (other < last)).astype(bf16)
        offset = pl.multiple_of(start + tap // 2 * 2 * STEP, 2 * STEP)
        block = (odd if tap % 2 else even)[pl.ds(offset, tile)] * wide(valid, width)
        for lane in range(0, width, 128):
            chunk = (tap * width + lane) // 128
            seat = ((chunk // per) ^ place_ref[2]) * per + chunk % per
            stack[:, pl.ds(pl.multiple_of(seat * 128, 128), 128)] = block[:, lane : lane + 128]

    @pl.when(step == 0)
    def _():
        for copy in copies:
            copy.wait()
        back.start()

    far_ref[...] = stack[:, store.shape[0] :]
    conv_ref[...] = dot(stack[:, : store.shape[0]], store[...])

    @pl.when(step == pl.num_programs(0) - 1)
    def _():
        back.wait()


def conv_forward(lengths, place, pieces, masked, fast, body):
    rows, width = masked.shape
    depth = TAPS * width // QUARTERS
    tile = 512
    return pl.pallas_call(
        functools.partial(conv_kernel, count=len(pieces), fast=fast, body=body, wins=lengths.shape[1]),
        grid=(rows // tile,),
        in_specs=[SMEM, SMEM] + [ANY] * len(pieces) + [whole((rows, width))],
        out_specs=[rows_of(tile, width), rows_of(tile, depth), ANY],
        out_shape=[
            jax.ShapeDtypeStruct((rows, width), f32),
            jax.ShapeDtypeStruct((rows, depth), bf16),
            jax.ShapeDtypeStruct(((QUARTERS - 1) * depth, width), bf16),
        ],
        scratch_shapes=[
            pltpu.VMEM(((QUARTERS - 1) * depth, width), bf16),
            pltpu.VMEM((tile, QUARTERS * depth), bf16),
            pltpu.VMEM((rows + 2 * REACH, width), bf16),
            pltpu.VMEM((rows + 2 * REACH, width), bf16),
            pltpu.SemaphoreType.DMA((sum(piece.shape[0] for piece in pieces),)),
            pltpu.SemaphoreType.DMA,
        ],
        compiler_params=vmem(63),
        cost_estimate=cost(3 * depth * rows * width, 24 * rows * width),
        name="conv_forward",
    )(lengths, place, *pieces, masked)


def ff_copies(pieces, place, fast, store, sems):
    if not fast:
        return [pltpu.make_async_copy(pieces[0], store, sems.at[0])]
    core, own_z, dp = place
    per = len(pieces) // 2
    copies = []
    for n, piece in enumerate(pieces):
        which = core if n < per else 1 - core
        kind = n % per
        for hop in range(piece.shape[0]):
            z = (own_z - hop - (2 if kind == 4 else 0)) & 3
            block = ((dp ^ min(kind, 3)) * 4 + z) * 2 + which
            copies.append(pltpu.make_async_copy(piece.at[hop], store.at[block], sems.at[len(copies)]))
    return copies


def relay_seat(r, k):
    if k < 2:
        return (1, r // 2 * 2 + k) if r % 2 else (0, r // 2 * 2 + k)
    return (2, r % 2 * 2 + k - 2) if r // 2 else (0, 4 + r * 2 + k - 2)


def feed_kernel(place_ref, *refs, far, count, outs, tiles, chunk, inner_rows, outer_rows, extra, fast, body):
    far_pieces, ff_pieces = refs[:far], refs[far : far + count]
    refs = refs[far + count :]
    stacked_ref, partial_ref, tokens_ref, cot_ref = refs[:4]
    mixed_ref, d_hidden_ref, d_conv_ref, sums_ref, far_ref = refs[4:9]
    targets = refs[9 : 9 + outs]
    refs = refs[9 + outs :]
    packed, w_in, w_far, small_ref, bend, slope_ref, normed_ref, hiddens, actives, d_outers, d_inners = refs[:11]
    tallies, ff_sems, far_sems, grad_sems, out_sem = refs[11:]
    slab = SLAB
    store = packed
    step = pl.program_id(0)
    tile, width = tokens_ref.shape
    total = w_in.shape[1]
    blocks = packed.shape[0]
    cols = total // width
    place = tuple(place_ref[i] for i in range(3))
    core = place[0]
    depth = w_far.shape[0]
    top = cols * inner_rows
    back = pltpu.make_async_copy(w_far, far_ref, out_sem)

    @pl.when(step == 0)
    def _():
        copies = ff_copies(ff_pieces, place, fast, packed, ff_sems)
        far_sites = conv_sites(far_pieces, QUARTERS - 1, place, fast, body)
        copies += conv_copies(far_sites, lambda kind: 0, w_far, far_sems)
        for copy in copies:
            copy.start()
        tallies[...] = jnp.zeros_like(tallies)
        for copy in copies:
            copy.wait()
        back.start()
        for j in range(cols):
            part = packed[:, j * inner_rows : (j + 1) * inner_rows].reshape(blocks * inner_rows, width)
            w_in[:, j * width : (j + 1) * width] = part
        small_ref[...] = jnp.sum(packed[:, top : top + extra].astype(f32), axis=0)

    base = pl.multiple_of(jnp.minimum(step, tiles - 1) * tile, tile)

    def at(part):
        return pl.ds(pl.multiple_of(base + part.start, part.size), part.size)

    def add_tally(row, col, term):
        tallies[8 * row : 8 * row + 8, col : col + term.shape[1]] += fold(term)

    def out_rows(j):
        if outer_rows > chunk:
            per = outer_rows // chunk
            first = top + extra + j % per * chunk
            return packed[j // per, first : first + chunk]
        count = chunk // outer_rows
        return packed[j * count : (j + 1) * count, top + extra :].reshape(chunk, width)

    in_rows = step < tiles

    @pl.when(in_rows)
    def _():
        for part in slabs(tile, slab):
            conv = partial_ref[part] + dot(stacked_ref[part], w_far[...]) + small_ref[0:1]
            bent, slope = gelu_pair(conv)
            shifted = bent - mean(bent)
            root = lax.rsqrt(mean(shifted * shifted) + EPSILON)
            normed = shifted * root
            normed_ref[part] = normed
            slope_ref[part] = slope * root
            hiddens[at(part)] = (
                tokens_ref[part].astype(f32) + normed * small_ref[1:2] + small_ref[2:3]
            ).astype(bf16)

    for j in range(total // chunk):
        cut = slice(j * chunk, (j + 1) * chunk)

        @pl.when(in_rows)
        def _(j=j, cut=cut):
            for part in slabs(tile, slab):
                inner = dot(hiddens[at(part)], w_in[:, cut]) + small_ref[6 + j : 7 + j]
                act, slope = gelu_pair(inner)
                actives[at(part), cut] = act.astype(bf16)
                bend[part, cut] = slope

    @pl.when(in_rows)
    def _():
        gain_two = small_ref[4:5]
        for part in slabs(tile, slab):
            full = packed[:, top + extra :].reshape(blocks * outer_rows, width)
            outer = dot(actives[at(part)], full) + small_ref[3:4]
            shifted = outer - mean(outer)
            root = lax.rsqrt(mean(shifted * shifted) + EPSILON)
            normal = shifted * root
            mixed_ref[part] = (hiddens[at(part)].astype(f32) + normal * gain_two + small_ref[5:6]).astype(bf16)
            cot = cot_ref[part].astype(f32)
            q = cot * gain_two
            d_outer = (root * (q - mean(q) - normal * mean(q * normal))).astype(bf16)
            d_outers[at(part)] = d_outer
            add_tally(3, 0, d_outer.astype(f32))
            add_tally(4, 0, cot * normal)
            add_tally(5, 0, cot)

    for j in range(total // chunk):
        cut = slice(j * chunk, (j + 1) * chunk)

        @pl.when(in_rows)
        def _(j=j, cut=cut):
            for part in slabs(tile, slab):
                d_inner = (dot_t(d_outers[at(part)], out_rows(j)) * bend[part, cut]).astype(bf16)
                d_inners[at(part), cut] = d_inner
                add_tally(6 + j, 0, d_inner.astype(f32))

    @pl.when(in_rows)
    def _():
        for part in slabs(tile, slab):
            d_hidden = dot_t(d_inners[at(part)], w_in[...]) + cot_ref[part].astype(f32)
            d_hidden_ref[part] = d_hidden
            first = normed_ref[part]
            p = d_hidden * small_ref[1:2]
            d_conv = (slope_ref[part] * (p - mean(p) - first * mean(p * first))).astype(bf16)
            d_conv_ref[part] = d_conv
            add_tally(0, 0, d_conv.astype(f32))
            add_tally(1, 0, d_hidden * first)
            add_tally(2, 0, d_hidden)

    def grad_copies():
        copies = []
        if not fast:
            for n, target in enumerate(targets):
                copies.append(pltpu.make_async_copy(store.at[pl.ds(n, 1)], target, grad_sems.at[n]))
            return copies
        for n, which in enumerate((core, 1 - core)):
            for r in range(4):
                for k in range(4):
                    array, seat = relay_seat(r, k)
                    block = ((place[2] ^ r) * 4 + ((place[1] + k) & 3)) * 2 + which
                    copies.append(
                        pltpu.make_async_copy(store.at[block], targets[3 * n + array].at[seat], grad_sems.at[len(copies)])
                    )
        return copies

    @pl.when(step >= tiles)
    def _():
        j = step - tiles
        part = pl.ds(pl.multiple_of(j * width, width), width)
        d_out = dot_rows(actives[:, part], d_outers[...]).astype(bf16)
        first = top + extra
        if fast:
            many = width // outer_rows
            store[pl.ds(j * many, many), first : first + outer_rows] = d_out.reshape(many, outer_rows, width)
        else:
            per = outer_rows // width
            start = pl.multiple_of(first + (j % per) * width, 16)
            store[pl.ds(j // per, 1), pl.ds(start, width)] = d_out.reshape(1, width, width)
        d_in = dot_rows(hiddens[...], d_inners[:, part]).astype(bf16)
        above = pl.ds(pl.multiple_of(j * inner_rows, inner_rows), inner_rows)
        store[:, above] = d_in.reshape(blocks, inner_rows, width)

    @pl.when(step == pl.num_programs(0) - 1)
    def _():
        back.wait()
        for row in range(sums_ref.shape[0]):
            sums_ref[row : row + 1] = colsum(tallies[8 * row : 8 * row + 8])
        if fast:
            head = sums_ref[:6].astype(bf16)
            rest = jnp.zeros((extra - 7, width), bf16)
            for dp in range(blocks // 8):
                line = jnp.concatenate([head, sums_ref[6 + dp : 7 + dp].astype(bf16), rest])
                store[8 * dp : 8 * dp + 8, top : top + extra] = jnp.broadcast_to(line, (8, extra, width))
        copies = grad_copies()
        for copy in copies:
            copy.start()
        for copy in copies:
            copy.wait()


def feed(place, far, pieces, stacked, partial, tokens, cotangent, inner_rows, outer_rows, extra, total, fast, body):
    rows, width = tokens.shape
    blocks = width // inner_rows
    tile = 512
    tiles, cols = rows // tile, total // width
    share = cols * inner_rows + extra + outer_rows
    depth = stacked.shape[1]
    seats = (8, 4, 4) * 2 if fast else (1, 1)
    tall = pl.BlockSpec((tile, width), lambda i: (jnp.minimum(i, tiles - 1), 0))
    last = pl.BlockSpec((tile, depth), lambda i: (jnp.minimum(i, tiles - 1), 0))
    return pl.pallas_call(
        functools.partial(
            feed_kernel, far=len(far), count=len(pieces), outs=len(seats), tiles=tiles, chunk=512, inner_rows=inner_rows,
            outer_rows=outer_rows, extra=extra, fast=fast, body=body,
        ),
        grid=(tiles + cols,),
        in_specs=[SMEM] + [ANY] * (len(far) + len(pieces)) + [last, tall, tall, tall],
        out_specs=[tall, tall, tall, pl.BlockSpec((16, width), lambda i: (0, 0)), ANY] + [ANY] * len(seats),
        out_shape=[
            jax.ShapeDtypeStruct((rows, width), bf16),
            jax.ShapeDtypeStruct((rows, width), f32),
            jax.ShapeDtypeStruct((rows, width), bf16),
            jax.ShapeDtypeStruct((16, width), f32),
            jax.ShapeDtypeStruct((depth, width), bf16),
        ] + [jax.ShapeDtypeStruct((count, share, width), bf16) for count in seats],
        scratch_shapes=[
            pltpu.VMEM((blocks, share, width), bf16),
            pltpu.VMEM((width, total), bf16),
            pltpu.VMEM((depth, width), bf16),
            pltpu.VMEM((extra, width), f32),
            pltpu.VMEM((tile, total), f32),
            pltpu.VMEM((tile, width), f32),
            pltpu.VMEM((tile, width), f32),
            pltpu.VMEM((rows, width), bf16),
            pltpu.VMEM((rows, total), bf16),
            pltpu.VMEM((rows, width), bf16),
            pltpu.VMEM((rows, total), bf16),
            pltpu.VMEM((8 * extra, width), f32),
            pltpu.SemaphoreType.DMA((sum(piece.shape[0] for piece in pieces),)),
            pltpu.SemaphoreType.DMA((sum(piece.shape[0] for piece in far),)),
            pltpu.SemaphoreType.DMA((blocks,)),
            pltpu.SemaphoreType.DMA,
        ],
        compiler_params=vmem(63),
        cost_estimate=cost(6 * rows * width * total, 40 * rows * width),
        name="feed",
    )(place, *far, *pieces, stacked, partial, tokens, cotangent)


def lay_shifted(values_ref, even, odd, tile):
    rows, width = values_ref.shape
    zeros = jnp.zeros((REACH, width), bf16)
    even[:REACH] = zeros
    even[rows + REACH :] = zeros
    odd[:REACH] = zeros
    odd[rows:] = jnp.zeros((2 * REACH, width), bf16)
    for r in range(0, rows, tile):
        block = values_ref[r : r + tile]
        even[REACH + r : REACH + r + tile] = block
        odd[REACH - STEP + r : REACH - STEP + r + tile] = block


def tap_products(len_ref, place, masked_ref, even, odd, part, targets, store, sems, *, wins, blocks, body, turn):
    channels, rows = masked_ref.shape
    width = part.stop - part.start
    core = place[0]
    position = lax.broadcasted_iota(jnp.int32, (rows, 128), 0)
    first, last = window_bounds(len_ref, position, wins, rows)
    copies = []
    for tap in range(TAPS):
        mirror = TAPS - 1 - tap
        other = position + (mirror - TAPS // 2) * STEP
        valid = ((other >= first) & (other < last)).astype(bf16)
        source = (odd if mirror % 2 else even)[mirror // 2 * 2 * STEP : mirror // 2 * 2 * STEP + rows, part]
        store[tap * channels : (tap + 1) * channels] = dot(masked_ref[...], source * wide(valid, width)).astype(bf16)
        while len(copies) // 2 < blocks and (len(copies) // 2 + 1) * 2 * body <= (tap + 1) * channels:
            block = len(copies) // 2
            seat = ((block // 4) ^ turn) * 4 + ((block % 4 - place[1]) & 3) if blocks == 16 else block
            for n, (target, which) in enumerate(zip(targets, (core, 1 - core))):
                start = pl.multiple_of((2 * block + which) * body, 16)
                copies.append(pltpu.make_async_copy(store.at[pl.ds(start, body)], target.at[seat], sems.at[n, block]))
                copies[-1].start()
    for copy in copies:
        copy.wait()


def conv_grad_kernel(len_ref, place_ref, masked_ref, d_conv_ref, keep_ref, send_ref, even, odd, store, sems, *, wins, blocks, body):
    lay_shifted(d_conv_ref, even, odd, 256)
    tap_products(
        len_ref, tuple(place_ref[i] for i in range(3)), masked_ref, even, odd, slice(0, d_conv_ref.shape[1]),
        (keep_ref, send_ref), store, sems, wins=wins, blocks=blocks, body=body, turn=0,
    )


def conv_grad(lengths, place, masked, d_conv, blocks, body):
    channels, rows = masked.shape
    width = d_conv.shape[1]
    return pl.pallas_call(
        functools.partial(conv_grad_kernel, wins=lengths.shape[1], blocks=blocks, body=body),
        grid=(1,),
        in_specs=[SMEM, SMEM, whole(masked.shape), whole((rows, width))],
        out_specs=[ANY, ANY],
        out_shape=[jax.ShapeDtypeStruct((blocks, body, width), bf16)] * 2,
        scratch_shapes=[
            pltpu.VMEM((rows + 2 * REACH, width), bf16),
            pltpu.VMEM((rows + 2 * REACH, width), bf16),
            pltpu.VMEM((TAPS * channels, width), bf16),
            pltpu.SemaphoreType.DMA((2, blocks)),
        ],
        compiler_params=vmem(63),
        cost_estimate=cost(TAPS * rows * width * channels, 12 * rows * width),
        name="conv_grad",
    )(lengths, place, masked, d_conv)


def token_grad_kernel(
    len_ref, place_ref, near_ref, far_ref, d_conv_ref, d_hidden_ref, keep_ref, d_tokens_ref, even, odd, store, sems, *, wins, tile
):
    step = pl.program_id(0)
    rows, width = d_conv_ref.shape
    depth = far_ref.shape[0]

    @pl.when(step == 0)
    def _():
        copies = []
        for kind in range(QUARTERS):
            source = far_ref if kind == QUARTERS - 1 else near_ref.at[pl.ds(kind * depth, depth)]
            start = pl.multiple_of((place_ref[2] ^ kind) * depth, 128)
            copies.append(pltpu.make_async_copy(source, store.at[pl.ds(start, depth)], sems.at[kind]))
        for copy in copies:
            copy.start()
        lay_shifted(d_conv_ref, even, odd, 256)
        for copy in copies:
            copy.wait()

    start = pl.multiple_of(step * tile, tile)
    position = lax.broadcasted_iota(jnp.int32, (tile, 128), 0) + start
    first, last = window_bounds(len_ref, position, wins, rows)
    total = None
    for tap in range(TAPS):
        mirror = TAPS - 1 - tap
        other_row = position + (mirror - TAPS // 2) * STEP
        valid = ((other_row >= first) & (other_row < last)).astype(bf16)
        offset = pl.multiple_of(start + mirror // 2 * 2 * STEP, 2 * STEP)
        block = (odd if mirror % 2 else even)[pl.ds(offset, tile)] * wide(valid, width)
        term = dot_t(block, store[tap * width : (tap + 1) * width])
        total = term if total is None else total + term
    d_tokens_ref[...] = d_hidden_ref[...] + total * wide(keep_ref[...], width)


def token_grad(lengths, place, near, far, d_conv, d_hidden, keep):
    rows, width = d_conv.shape
    tile = 512
    return pl.pallas_call(
        functools.partial(token_grad_kernel, wins=lengths.shape[1], tile=tile),
        grid=(rows // tile,),
        in_specs=[SMEM, SMEM, ANY, ANY, whole((rows, width)), rows_of(tile, width), rows_of(tile, 128)],
        out_specs=rows_of(tile, width),
        out_shape=jax.ShapeDtypeStruct((rows, width), f32),
        scratch_shapes=[
            pltpu.VMEM((rows + 2 * REACH, width), bf16),
            pltpu.VMEM((rows + 2 * REACH, width), bf16),
            pltpu.VMEM((TAPS * width, width), bf16),
            pltpu.SemaphoreType.DMA((QUARTERS,)),
        ],
        compiler_params=vmem(63),
        cost_estimate=cost(TAPS * rows * width * width, 12 * rows * width),
        name="token_grad",
    )(lengths, place, near, far, d_conv, d_hidden, keep)


def on_device(
    n_dp, n_fsdp, tokens, present, lengths, conv_w, conv_b, gain_one, shift_one, w_in, b_in, w_out, b_out, gain_two, shift_two, cotangent
):
    rows, width = tokens.shape
    total = w_in.shape[1]
    cols = total // width
    devices = n_dp * n_fsdp
    fast = n_dp == 4 and n_fsdp == 8 and conv_w.shape[0] % 16 == 0 and w_in.shape[0] % 16 == 0
    bar = lax.optimization_barrier
    extra = 16
    n = width // devices
    swap = [(i, i ^ 1) for i in range(n_fsdp)]
    across = {r: [(i, i ^ r) for i in range(n_dp)] for r in (1, 2, 3)}
    along = {k: [(i, (i + 2 * k) % n_fsdp) for i in range(n_fsdp)] for k in (1, 2, 3)}
    vectors = (conv_b, gain_one, shift_one, b_out, gain_two, shift_two)
    if fast:
        fsdp = lax.axis_index("fsdp").astype(jnp.int32)
        dp = lax.axis_index("dp").astype(jnp.int32)
        place = jnp.stack([fsdp & 1, fsdp >> 1, dp])
        body = conv_w.shape[0]
        inner_rows, outer_rows = w_in.shape[0], w_out.shape[0]
        blocks = devices // 2

        def from_column(shard):
            return [shard] + [lax.ppermute(shard, "fsdp", along[k]) for k in (1, 2, 3)]

        column = jnp.stack(from_column(conv_w))
        seat = dp * n_fsdp + fsdp
        lane = jnp.arange(width, dtype=jnp.int32)
        line = jnp.arange(extra, dtype=jnp.int32)[:, None]
        lines = jnp.concatenate(
            [jnp.tile(jnp.stack(vectors), (1, devices))]
            + [jnp.tile(b_in, width // b_in.shape[0])[None]] * cols
            + [jnp.zeros((extra - 6 - cols, width), bf16)]
        )
        few = b_in.shape[0]
        own_line = ((line < 6) & (lane // n == seat)) | ((line == 6 + dp) & (lane // few == fsdp))
        lines = jnp.where(own_line, lines, 0)
        ff_own = jnp.concatenate([w_in[:, j * width : (j + 1) * width] for j in range(cols)] + [lines, w_out], axis=0)
        masked, masked_across, keep = prep(tokens, present)
        column, ff_own, masked, masked_across, keep = bar((column, ff_own, masked, masked_across, keep))
        beside_x = lax.ppermute(column, "dp", across[1])
        beside_y = lax.ppermute(column, "dp", across[2])
        ff_rest = from_column(ff_own)
        column, beside_x, beside_y, ff_rest = bar((column, beside_x, beside_y, ff_rest))
        ff_column = jnp.stack(ff_rest)
        near = (column, beside_x, beside_y)
        near = near + tuple(lax.ppermute(piece, "fsdp", swap) for piece in near)
        far = (
            lax.ppermute(beside_x[:2], "dp", across[2]),
            lax.ppermute(beside_y[2:], "dp", across[1]),
        )
        ff = (ff_column, lax.ppermute(ff_column, "dp", across[1]), lax.ppermute(ff_column, "dp", across[2]))
    else:
        place = jnp.zeros((3,), jnp.int32)
        gather = functools.partial(lax.all_gather, axis_name=AXES, axis=0, tiled=True)
        full = gather(conv_w)
        body = full.shape[0] // 2
        depth = full.shape[0] // QUARTERS * (QUARTERS - 1)
        near, far = (full[None, :depth],), (full[None, depth:],)
        lines = [gather(vector) for vector in vectors] + list(gather(b_in).reshape(cols, width))
        lines = jnp.stack(lines + [jnp.zeros_like(lines[0])] * (extra - len(lines)))
        full_in, full_out = gather(w_in), gather(w_out)
        inner_rows, outer_rows = full_in.shape[0] // 2, full_out.shape[0] // 2
        blocks = 1
        ff = [full_in[:, j * width : (j + 1) * width].reshape(2, inner_rows, width) for j in range(cols)]
        ff.append(jnp.stack([lines, jnp.zeros_like(lines)]))
        ff = (jnp.concatenate(ff + [full_out.reshape(2, outer_rows, width)], axis=1),)
        masked, masked_across, keep = prep(tokens, present)

    partial, stacked, w_near = conv_forward(lengths, place, near, masked, fast, body)
    if fast:
        far, ff, partial = bar((far, ff, partial))
        ff = ff + (
            lax.ppermute(ff[1][:2], "dp", across[2]),
            lax.ppermute(ff[2][2:], "dp", across[1]),
        )
        far = far + tuple(lax.ppermute(piece, "fsdp", swap) for piece in far)
        ff = ff + tuple(lax.ppermute(piece, "fsdp", swap) for piece in ff)
    mixed, d_hidden, d_conv, sums, w_far, *ff_grads = feed(
        place, far, ff, stacked, partial, tokens, cotangent, inner_rows, outer_rows, extra, total, fast, body
    )
    def added(terms):
        return sum(term.astype(f32) for term in terms)

    def line_swap(line):
        return [line[0]] + [lax.ppermute(line[k], "fsdp", along[k]) for k in (1, 2, 3)]

    def rounded(*terms):
        return added(terms).astype(bf16)

    if fast:
        ff_near, ff_far_a, ff_far_b = ff_grads[:3]
        came_a, came_b, came = (lax.ppermute(ff_grads[3 + n], "fsdp", swap) for n in (1, 2, 0))
        a_far, b_far, d_conv = bar((ff_far_a + came_a, ff_far_b + came_b, d_conv))
        a_came = lax.ppermute(a_far, "dp", across[1])
        b_came = lax.ppermute(b_far, "dp", across[2])
        conv_keep, conv_send = conv_grad(lengths, place, masked_across, d_conv, blocks, body)
        a_came, b_came, came, conv_keep, conv_send, d_conv = bar((a_came, b_came, came, conv_keep, conv_send, d_conv))
        conv_came = lax.ppermute(conv_send, "fsdp", swap)
        a_last = lax.ppermute(rounded(ff_near[2:4], came[2:4], a_came[2:]), "dp", across[2])
        b_last = lax.ppermute(rounded(ff_near[6:], came[6:], b_came[2:]), "dp", across[1])
        conv_chip = conv_keep + conv_came
        conv_chip, a_last, b_last, d_conv = bar((conv_chip, a_last, b_last, d_conv))
        conv_plane = lax.all_to_all(conv_chip.reshape(4, 4, body, width), "dp", 0, 0, tiled=True)
        line = [rounded(ff_near[k], came[k], a_came[k], a_last[k]) for k in (0, 1)]
        line += [rounded(ff_near[4 + k], came[4 + k], b_came[k], b_last[k]) for k in (0, 1)]
        ff_line = line_swap(line)
        d_tokens = token_grad(lengths, place, w_near, w_far, d_conv, d_hidden, keep)
        d_tokens, ff_line, conv_plane = bar((d_tokens, ff_line, conv_plane))
        conv_line = line_swap([added(conv_plane[r, k] for r in range(4)).astype(bf16) for k in range(4)])
        ff_share = added(ff_line)
        d_conv_w = added(conv_line)
        top = cols * inner_rows
        d_w_in = jnp.concatenate([ff_share[j * inner_rows : (j + 1) * inner_rows] for j in range(cols)], axis=1)
        d_w_out = ff_share[top + extra :]
        seat = dp * n_fsdp + fsdp
        own = lax.dynamic_slice(ff_share[top : top + 6], (0, seat * n), (6, n))
        vector_grads = list(own)
        vector_grads.append(lax.dynamic_slice(ff_share[top + 6], (fsdp * few,), (few,)))
    else:
        conv_pair = conv_grad(lengths, place, masked_across, d_conv, blocks, body)
        d_tokens = token_grad(lengths, place, w_near, w_far, d_conv, d_hidden, keep)
        ff_share = jnp.concatenate(ff_grads, axis=0)
        scatter = functools.partial(lax.psum_scatter, axis_name=AXES, scatter_dimension=0, tiled=True)
        d_in_full = jnp.concatenate(
            [ff_share[:, j * inner_rows : (j + 1) * inner_rows].reshape(-1, width) for j in range(cols)], axis=1
        )
        d_w_in = scatter(d_in_full.astype(f32))
        d_w_out = scatter(ff_share[:, cols * inner_rows + extra :].reshape(-1, width).astype(f32))
        d_conv_w = scatter(jnp.concatenate(conv_pair, axis=0).reshape(-1, width).astype(f32))
        vector_grads = [scatter(line) for line in sums[:6]] + [scatter(sums[6 : 6 + cols].reshape(-1))]
    d_conv_b, d_gain_one, d_shift_one, d_b_out, d_gain_two, d_shift_two, d_b_in = vector_grads
    return (
        mixed, d_tokens, d_conv_w, d_conv_b, d_gain_one, d_shift_one, d_w_in, d_b_in, d_w_out, d_b_out, d_gain_two, d_shift_two
    )


def solution(mesh):
    both = P(AXES)
    flat = P(AXES, None)
    in_specs = (flat, both, flat, flat, both, both, both, flat, both, flat, both, both, both, flat)
    out_specs = (flat, flat, flat, both, both, both, flat, both, flat, both, both, both)
    return jax.shard_map(
        functools.partial(on_device, mesh.shape["dp"], mesh.shape["fsdp"]),
        mesh=mesh,
        in_specs=in_specs,
        out_specs=out_specs,
        check_vma=False,
    )
```

```python
import functools
import jax
import jax.numpy as jnp
from jax import lax
from jax.experimental import pallas as pl
from jax.experimental.pallas import tpu as pltpu
from jax.sharding import PartitionSpec as P

TAPS = 9
STEP = 8
REACH = (TAPS // 2) * STEP
EPSILON = 1e-05
SLAB = 512
QUARTERS = 4
AXES = ("dp", "fsdp")
f32 = jnp.float32
bf16 = jnp.bfloat16
ANY = pl.BlockSpec(memory_space=pl.ANY)
SMEM = pl.BlockSpec(memory_space=pltpu.SMEM)


def dot(a, b):
    return jnp.dot(a, b, preferred_element_type=f32)


def dot_t(a, b):
    return lax.dot_general(a, b, (((1,), (1,)), ((), ())), preferred_element_type=f32)


def dot_rows(a, b):
    return lax.dot_general(a, b, (((0,), (0,)), ((), ())), preferred_element_type=f32)


def gelu_pair(v):
    phi = 0.5 + 0.5 * lax.erf(v * 0.7071067811865476)
    return v * phi, phi + v * (0.3989422804014327 * jnp.exp2(v * v * -0.7213475204444817))


def mean(v):
    return jnp.sum(v, axis=-1, keepdims=True) * (1.0 / v.shape[-1])


def fold(v):
    return sum(v[r : r + 8] for r in range(0, v.shape[0], 8))


def slabs(total, size):
    return [pl.ds(r, size) for r in range(0, total, size)]


def colsum(v):
    return jnp.sum(v, axis=0, keepdims=True)


def vmem(mib):
    return pltpu.CompilerParams(vmem_limit_bytes=mib << 20)


def cost(macs, nbytes):
    return pl.CostEstimate(flops=macs // 32, bytes_accessed=nbytes // 32, transcendentals=0)


def whole(shape):
    return pl.BlockSpec(shape, lambda *_: (0,) * len(shape), pipeline_mode=pl.Buffered(1))


def rows_of(tile, width):
    return pl.BlockSpec((tile, width), lambda i: (i, 0))


def window_reach(len_ref, position, wins, total):
    first = jnp.zeros_like(position)
    last = jnp.full_like(position, total - 1)
    edge = jnp.int32(0)
    edges = []
    for w in range(wins - 1):
        edge = edge + len_ref[0, w]
        edges.append(edge)
    for edge in edges:
        first = jnp.where(position >= edge, edge, first)
    for edge in reversed(edges):
        last = jnp.where(position < edge, edge - 1, last)
    return position - first, last - position


def within(block, reach, tap):
    shift = (tap - TAPS // 2) * STEP
    if shift == 0:
        return block
    before, after = reach
    valid = (before >= -shift) if shift < 0 else (after >= shift)
    return block * wide(jnp.where(valid, 1.0, 0.0).astype(bf16), block.shape[1])


def wide(mask, width):
    return jnp.concatenate([mask] * (width // 128), axis=1)


def prep_kernel(tokens_ref, present_ref, masked_ref, across_ref, keep_ref):
    tile, width = tokens_ref.shape
    for r in range(0, tile, 128):
        line = jnp.broadcast_to((present_ref[0, r // 128 : r // 128 + 1] > 0).astype(f32), (128, 128))
        kept = line.T
        keep_ref[r : r + 128] = kept
        masked_ref[r : r + 128] = tokens_ref[r : r + 128] * wide(kept.astype(bf16), width)
    across_ref[...] = masked_ref[...].T


def prep(tokens, present):
    rows, width = tokens.shape
    tile = 512
    return pl.pallas_call(
        prep_kernel,
        grid=(rows // tile,),
        in_specs=[rows_of(tile, width), pl.BlockSpec((1, tile // 128, 128), lambda i: (i, 0, 0))],
        out_specs=[rows_of(tile, width), pl.BlockSpec((width, tile), lambda i: (0, i)), rows_of(tile, 128)],
        out_shape=[
            jax.ShapeDtypeStruct((rows, width), bf16),
            jax.ShapeDtypeStruct((width, rows), bf16),
            jax.ShapeDtypeStruct((rows, 128), f32),
        ],
        compiler_params=vmem(63),
        cost_estimate=cost(0, 24 * rows * width),
        name="prep",
    )(tokens, present.reshape(rows // tile, tile // 128, 128))


def conv_sites(pieces, first, place, fast, body):
    if not fast:
        return [(piece.at[0], first, 0) for piece in pieces]
    core, z, _ = place
    sites = []
    per = len(pieces) // 2
    for n, piece in enumerate(pieces):
        which = core if n < per else 1 - core
        kind = first + n % per
        for hop in range(piece.shape[0]):
            row = (((z - hop - (2 if kind == 4 else 0)) & 3) * 2 + which) * body
            sites.append((piece.at[hop], min(kind, 3), row))
    return sites


def conv_copies(sites, base, store, sems):
    copies = []
    for n, (source, kind, row) in enumerate(sites):
        start = pl.multiple_of(base(kind) + row, 16)
        copies.append(pltpu.make_async_copy(source, store.at[pl.ds(start, source.shape[0])], sems.at[n]))
    return copies


def conv_kernel(len_ref, place_ref, *refs, count, fast, body, wins):
    pieces = refs[:count]
    masked_ref, conv_ref, far_ref, near_ref, store, stack, even, odd, sems, out_sem = refs[count:]
    step = pl.program_id(0)
    rows, width = masked_ref.shape
    tile = conv_ref.shape[0]
    depth = store.shape[0] // (QUARTERS - 1)
    back = pltpu.make_async_copy(store, near_ref, out_sem)
    sites = conv_sites(pieces, 0, tuple(place_ref[i] for i in range(3)), fast, body)
    copies = conv_copies(sites, lambda kind: kind * depth, store, sems)

    @pl.when(step == 0)
    def _():
        for copy in copies:
            copy.start()
        lay_shifted(masked_ref, even, odd, 256)

    start = pl.multiple_of(step * tile, tile)
    position = lax.broadcasted_iota(jnp.int32, (tile, 128), 0) + start
    reach = window_reach(len_ref, position, wins, rows)
    per = depth // 128
    for tap in range(TAPS):
        offset = pl.multiple_of(start + tap // 2 * 2 * STEP, 2 * STEP)
        block = within((odd if tap % 2 else even)[pl.ds(offset, tile)], reach, tap)
        for lane in range(0, width, 128):
            chunk = (tap * width + lane) // 128
            seat = ((chunk // per) ^ place_ref[2]) * per + chunk % per
            stack[:, pl.ds(pl.multiple_of(seat * 128, 128), 128)] = block[:, lane : lane + 128]

    @pl.when(step == 0)
    def _():
        for copy in copies:
            copy.wait()
        back.start()

    far_ref[...] = stack[:, store.shape[0] :]
    conv_ref[...] = dot(stack[:, : store.shape[0]], store[...])

    @pl.when(step == pl.num_programs(0) - 1)
    def _():
        back.wait()


def conv_forward(lengths, place, pieces, masked, fast, body):
    rows, width = masked.shape
    depth = TAPS * width // QUARTERS
    tile = 512
    return pl.pallas_call(
        functools.partial(conv_kernel, count=len(pieces), fast=fast, body=body, wins=lengths.shape[1]),
        grid=(rows // tile,),
        in_specs=[SMEM, SMEM] + [ANY] * len(pieces) + [whole((rows, width))],
        out_specs=[rows_of(tile, width), rows_of(tile, depth), ANY],
        out_shape=[
            jax.ShapeDtypeStruct((rows, width), f32),
            jax.ShapeDtypeStruct((rows, depth), bf16),
            jax.ShapeDtypeStruct(((QUARTERS - 1) * depth, width), bf16),
        ],
        scratch_shapes=[
            pltpu.VMEM(((QUARTERS - 1) * depth, width), bf16),
            pltpu.VMEM((tile, QUARTERS * depth), bf16),
            pltpu.VMEM((rows + 2 * REACH, width), bf16),
            pltpu.VMEM((rows + 2 * REACH, width), bf16),
            pltpu.SemaphoreType.DMA((sum(piece.shape[0] for piece in pieces),)),
            pltpu.SemaphoreType.DMA,
        ],
        compiler_params=vmem(63),
        cost_estimate=cost(3 * depth * rows * width, 24 * rows * width),
        name="conv_forward",
    )(lengths, place, *pieces, masked)


def ff_copies(pieces, place, fast, store, sems):
    if not fast:
        return [pltpu.make_async_copy(pieces[0], store, sems.at[0])]
    core, own_z, dp = place
    per = len(pieces) // 2
    copies = []
    for n, piece in enumerate(pieces):
        which = core if n < per else 1 - core
        kind = n % per
        for hop in range(piece.shape[0]):
            z = (own_z - hop - (2 if kind == 4 else 0)) & 3
            block = ((dp ^ min(kind, 3)) * 4 + z) * 2 + which
            copies.append(pltpu.make_async_copy(piece.at[hop], store.at[block], sems.at[len(copies)]))
    return copies


def relay_seat(r, k):
    if k < 2:
        return (1, r // 2 * 2 + k) if r % 2 else (0, r // 2 * 2 + k)
    return (2, r % 2 * 2 + k - 2) if r // 2 else (0, 4 + r * 2 + k - 2)


def feed_kernel(place_ref, *refs, far, count, outs, tiles, chunk, inner_rows, outer_rows, extra, fast, body):
    far_pieces, ff_pieces = refs[:far], refs[far : far + count]
    refs = refs[far + count :]
    stacked_ref, partial_ref, tokens_ref, cot_ref = refs[:4]
    mixed_ref, d_hidden_ref, d_conv_ref, sums_ref, far_ref = refs[4:9]
    targets = refs[9 : 9 + outs]
    refs = refs[9 + outs :]
    packed, w_in, w_far, small_ref, bend, slope_ref, normed_ref, hiddens, actives, d_outers, d_inners = refs[:11]
    tallies, ff_sems, far_sems, grad_sems, out_sem = refs[11:]
    slab = SLAB
    store = packed
    step = pl.program_id(0)
    tile, width = tokens_ref.shape
    total = w_in.shape[1]
    blocks = packed.shape[0]
    cols = total // width
    place = tuple(place_ref[i] for i in range(3))
    core = place[0]
    depth = w_far.shape[0]
    top = cols * inner_rows
    back = pltpu.make_async_copy(w_far, far_ref, out_sem)

    @pl.when(step == 0)
    def _():
        copies = ff_copies(ff_pieces, place, fast, packed, ff_sems)
        far_sites = conv_sites(far_pieces, QUARTERS - 1, place, fast, body)
        copies += conv_copies(far_sites, lambda kind: 0, w_far, far_sems)
        for copy in copies:
            copy.start()
        tallies[...] = jnp.zeros_like(tallies)
        for copy in copies:
            copy.wait()
        back.start()
        for j in range(cols):
            part = packed[:, j * inner_rows : (j + 1) * inner_rows].reshape(blocks * inner_rows, width)
            w_in[:, j * width : (j + 1) * width] = part
        small_ref[...] = jnp.sum(packed[:, top : top + extra].astype(f32), axis=0)

    base = pl.multiple_of(jnp.minimum(step, tiles - 1) * tile, tile)

    def at(part):
        return pl.ds(pl.multiple_of(base + part.start, part.size), part.size)

    def add_tally(row, col, term):
        tallies[8 * row : 8 * row + 8, col : col + term.shape[1]] += fold(term)

    def out_rows(j):
        if outer_rows > chunk:
            per = outer_rows // chunk
            first = top + extra + j % per * chunk
            return packed[j // per, first : first + chunk]
        count = chunk // outer_rows
        return packed[j * count : (j + 1) * count, top + extra :].reshape(chunk, width)

    in_rows = step < tiles

    @pl.when(in_rows)
    def _():
        for part in slabs(tile, slab):
            conv = partial_ref[part] + dot(stacked_ref[part], w_far[...]) + small_ref[0:1]
            bent, slope = gelu_pair(conv)
            shifted = bent - mean(bent)
            root = lax.rsqrt(mean(shifted * shifted) + EPSILON)
            normed = shifted * root
            normed_ref[part] = normed
            slope_ref[part] = slope * root
            hiddens[at(part)] = (
                tokens_ref[part].astype(f32) + normed * small_ref[1:2] + small_ref[2:3]
            ).astype(bf16)

    for j in range(total // chunk):
        cut = slice(j * chunk, (j + 1) * chunk)

        @pl.when(in_rows)
        def _(j=j, cut=cut):
            for part in slabs(tile, slab):
                inner = dot(hiddens[at(part)], w_in[:, cut]) + small_ref[6 + j : 7 + j]
                act, slope = gelu_pair(inner)
                actives[at(part), cut] = act.astype(bf16)
                bend[part, cut] = slope

    @pl.when(in_rows)
    def _():
        gain_two = small_ref[4:5]
        for part in slabs(tile, slab):
            full = packed[:, top + extra :].reshape(blocks * outer_rows, width)
            outer = dot(actives[at(part)], full) + small_ref[3:4]
            shifted = outer - mean(outer)
            root = lax.rsqrt(mean(shifted * shifted) + EPSILON)
            normal = shifted * root
            mixed_ref[part] = (hiddens[at(part)].astype(f32) + normal * gain_two + small_ref[5:6]).astype(bf16)
            cot = cot_ref[part].astype(f32)
            q = cot * gain_two
            d_outer_full = root * (q - mean(q) - normal * mean(q * normal))
            d_outers[at(part)] = d_outer_full.astype(bf16)
            add_tally(3, 0, d_outer_full)
            add_tally(4, 0, cot * normal)
            add_tally(5, 0, cot)

    for j in range(total // chunk):
        cut = slice(j * chunk, (j + 1) * chunk)

        @pl.when(in_rows)
        def _(j=j, cut=cut):
            for part in slabs(tile, slab):
                d_inner = dot_t(d_outers[at(part)], out_rows(j)) * bend[part, cut]
                d_inners[at(part), cut] = d_inner.astype(bf16)
                add_tally(6 + j, 0, d_inner)

    @pl.when(in_rows)
    def _():
        for part in slabs(tile, slab):
            d_hidden = dot_t(d_inners[at(part)], w_in[...]) + cot_ref[part].astype(f32)
            d_hidden_ref[part] = d_hidden
            first = normed_ref[part]
            p = d_hidden * small_ref[1:2]
            d_conv = slope_ref[part] * (p - mean(p) - first * mean(p * first))
            d_conv_ref[part] = d_conv.astype(bf16)
            add_tally(0, 0, d_conv)
            add_tally(1, 0, d_hidden * first)
            add_tally(2, 0, d_hidden)

    def put_blocks(dp):
        for r in range(4):

            @pl.when((dp ^ place[2]) == r)
            def _(r=r):
                for n, which in enumerate((core, 1 - core)):
                    for k in range(4):
                        array, seat = relay_seat(r, k)
                        target = targets[3 * n + array].at[seat]
                        block = (dp * 4 + ((place[1] + k) & 3)) * 2 + which
                        pltpu.make_async_copy(store.at[block], target, grad_sems.at[dp * 8 + 4 * n + k]).start()

    @pl.when(step == tiles)
    def _():
        for row in range(sums_ref.shape[0]):
            sums_ref[row : row + 1] = colsum(tallies[8 * row : 8 * row + 8])
        if fast:
            head = sums_ref[:6].astype(bf16)
            rest = jnp.zeros((extra - 7, width), bf16)
            for dp in range(blocks // 8):
                line = jnp.concatenate([head, sums_ref[6 + dp : 7 + dp].astype(bf16), rest])
                store[8 * dp : 8 * dp + 8, top : top + extra] = jnp.broadcast_to(line, (8, extra, width))

    for j in range(cols):
        part = slice(j * width, (j + 1) * width)

        @pl.when(step == tiles)
        def _(j=j, part=part):
            d_in = dot_rows(hiddens[...], d_inners[:, part]).astype(bf16)
            store[:, j * inner_rows : (j + 1) * inner_rows] = d_in.reshape(blocks, inner_rows, width)

    for j in range(cols):
        part = slice(j * width, (j + 1) * width)

        @pl.when(step == tiles)
        def _(j=j, part=part):
            d_out = dot_rows(actives[:, part], d_outers[...]).astype(bf16)
            first = top + extra
            if fast:
                many = width // outer_rows
                store[j * many : (j + 1) * many, first : first + outer_rows] = d_out.reshape(many, outer_rows, width)
                put_blocks(j)
            else:
                per = outer_rows // width
                start = first + j % per * width
                store[j // per, start : start + width] = d_out

    @pl.when(step == pl.num_programs(0) - 1)
    def _():
        back.wait()
        if fast:
            for n in range(blocks):
                pltpu.make_async_copy(store.at[n], targets[0].at[0], grad_sems.at[n]).wait()
        else:
            copies = [
                pltpu.make_async_copy(store.at[pl.ds(n, 1)], target, grad_sems.at[n]) for n, target in enumerate(targets)
            ]
            for copy in copies:
                copy.start()
            for copy in copies:
                copy.wait()


def feed(place, far, pieces, stacked, partial, tokens, cotangent, inner_rows, outer_rows, extra, total, fast, body):
    rows, width = tokens.shape
    blocks = width // inner_rows
    tile = 512
    tiles, cols = rows // tile, total // width
    share = cols * inner_rows + extra + outer_rows
    depth = stacked.shape[1]
    seats = (8, 4, 4) * 2 if fast else (1, 1)
    tall = pl.BlockSpec((tile, width), lambda i: (jnp.minimum(i, tiles - 1), 0))
    last = pl.BlockSpec((tile, depth), lambda i: (jnp.minimum(i, tiles - 1), 0))
    return pl.pallas_call(
        functools.partial(
            feed_kernel, far=len(far), count=len(pieces), outs=len(seats), tiles=tiles, chunk=512, inner_rows=inner_rows,
            outer_rows=outer_rows, extra=extra, fast=fast, body=body,
        ),
        grid=(tiles + 1,),
        in_specs=[SMEM] + [ANY] * (len(far) + len(pieces)) + [last, tall, tall, tall],
        out_specs=[tall, tall, tall, pl.BlockSpec((16, width), lambda i: (0, 0)), ANY] + [ANY] * len(seats),
        out_shape=[
            jax.ShapeDtypeStruct((rows, width), bf16),
            jax.ShapeDtypeStruct((rows, width), f32),
            jax.ShapeDtypeStruct((rows, width), bf16),
            jax.ShapeDtypeStruct((16, width), f32),
            jax.ShapeDtypeStruct((depth, width), bf16),
        ] + [jax.ShapeDtypeStruct((count, share, width), bf16) for count in seats],
        scratch_shapes=[
            pltpu.VMEM((blocks, share, width), bf16),
            pltpu.VMEM((width, total), bf16),
            pltpu.VMEM((depth, width), bf16),
            pltpu.VMEM((extra, width), f32),
            pltpu.VMEM((tile, total), f32),
            pltpu.VMEM((tile, width), f32),
            pltpu.VMEM((tile, width), f32),
            pltpu.VMEM((rows, width), bf16),
            pltpu.VMEM((rows, total), bf16),
            pltpu.VMEM((rows, width), bf16),
            pltpu.VMEM((rows, total), bf16),
            pltpu.VMEM((8 * extra, width), f32),
            pltpu.SemaphoreType.DMA((sum(piece.shape[0] for piece in pieces),)),
            pltpu.SemaphoreType.DMA((sum(piece.shape[0] for piece in far),)),
            pltpu.SemaphoreType.DMA((blocks,)),
            pltpu.SemaphoreType.DMA,
        ],
        compiler_params=vmem(63),
        cost_estimate=cost(6 * rows * width * total, 40 * rows * width),
        name="feed",
    )(place, *far, *pieces, stacked, partial, tokens, cotangent)


def lay_shifted(values_ref, even, odd, tile):
    rows, width = values_ref.shape
    zeros = jnp.zeros((REACH, width), bf16)
    even[:REACH] = zeros
    even[rows + REACH :] = zeros
    odd[:REACH] = zeros
    odd[rows:] = jnp.zeros((2 * REACH, width), bf16)
    for r in range(0, rows, tile):
        block = values_ref[r : r + tile]
        even[REACH + r : REACH + r + tile] = block
        odd[REACH - STEP + r : REACH - STEP + r + tile] = block


def tap_products(len_ref, place, masked_ref, even, odd, part, targets, store, sems, *, wins, blocks, body, turn):
    channels, rows = masked_ref.shape
    width = part.stop - part.start
    core = place[0]
    position = lax.broadcasted_iota(jnp.int32, (rows, 128), 0)
    reach = window_reach(len_ref, position, wins, rows)
    copies = []
    for tap in range(TAPS):
        mirror = TAPS - 1 - tap
        source = (odd if mirror % 2 else even)[mirror // 2 * 2 * STEP : mirror // 2 * 2 * STEP + rows, part]
        store[tap * channels : (tap + 1) * channels] = dot(masked_ref[...], within(source, reach, mirror)).astype(bf16)
        while len(copies) // 2 < blocks and (len(copies) // 2 + 1) * 2 * body <= (tap + 1) * channels:
            block = len(copies) // 2
            seat = ((block // 4) ^ turn) * 4 + ((block % 4 - place[1]) & 3) if blocks == 16 else block
            for n, (target, which) in enumerate(zip(targets, (core, 1 - core))):
                start = pl.multiple_of((2 * block + which) * body, 16)
                copies.append(pltpu.make_async_copy(store.at[pl.ds(start, body)], target.at[seat], sems.at[n, block]))
                copies[-1].start()
    for copy in copies:
        copy.wait()


def conv_grad_kernel(len_ref, place_ref, masked_ref, d_conv_ref, keep_ref, send_ref, even, odd, store, sems, *, wins, blocks, body):
    lay_shifted(d_conv_ref, even, odd, 256)
    tap_products(
        len_ref, tuple(place_ref[i] for i in range(3)), masked_ref, even, odd, slice(0, d_conv_ref.shape[1]),
        (keep_ref, send_ref), store, sems, wins=wins, blocks=blocks, body=body, turn=0,
    )


def conv_grad(lengths, place, masked, d_conv, blocks, body):
    channels, rows = masked.shape
    width = d_conv.shape[1]
    return pl.pallas_call(
        functools.partial(conv_grad_kernel, wins=lengths.shape[1], blocks=blocks, body=body),
        grid=(1,),
        in_specs=[SMEM, SMEM, whole(masked.shape), whole((rows, width))],
        out_specs=[ANY, ANY],
        out_shape=[jax.ShapeDtypeStruct((blocks, body, width), bf16)] * 2,
        scratch_shapes=[
            pltpu.VMEM((rows + 2 * REACH, width), bf16),
            pltpu.VMEM((rows + 2 * REACH, width), bf16),
            pltpu.VMEM((TAPS * channels, width), bf16),
            pltpu.SemaphoreType.DMA((2, blocks)),
        ],
        compiler_params=vmem(63),
        cost_estimate=cost(TAPS * rows * width * channels, 12 * rows * width),
        name="conv_grad",
    )(lengths, place, masked, d_conv)


def token_grad_kernel(
    len_ref, place_ref, near_ref, far_ref, d_conv_ref, d_hidden_ref, keep_ref, d_tokens_ref, even, odd, store, sems, *, wins, tile
):
    step = pl.program_id(0)
    rows, width = d_conv_ref.shape
    depth = far_ref.shape[0]

    @pl.when(step == 0)
    def _():
        copies = []
        for kind in range(QUARTERS):
            source = far_ref if kind == QUARTERS - 1 else near_ref.at[pl.ds(kind * depth, depth)]
            start = pl.multiple_of((place_ref[2] ^ kind) * depth, 128)
            copies.append(pltpu.make_async_copy(source, store.at[pl.ds(start, depth)], sems.at[kind]))
        for copy in copies:
            copy.start()
        lay_shifted(d_conv_ref, even, odd, 256)
        for copy in copies:
            copy.wait()

    start = pl.multiple_of(step * tile, tile)
    position = lax.broadcasted_iota(jnp.int32, (tile, 128), 0) + start
    reach = window_reach(len_ref, position, wins, rows)
    total = None
    for tap in range(TAPS):
        mirror = TAPS - 1 - tap
        offset = pl.multiple_of(start + mirror // 2 * 2 * STEP, 2 * STEP)
        block = within((odd if mirror % 2 else even)[pl.ds(offset, tile)], reach, mirror)
        term = dot_t(block, store[tap * width : (tap + 1) * width])
        total = term if total is None else total + term
    d_tokens_ref[...] = d_hidden_ref[...] + total * wide(keep_ref[...], width)


def token_grad(lengths, place, near, far, d_conv, d_hidden, keep):
    rows, width = d_conv.shape
    tile = 512
    return pl.pallas_call(
        functools.partial(token_grad_kernel, wins=lengths.shape[1], tile=tile),
        grid=(rows // tile,),
        in_specs=[SMEM, SMEM, ANY, ANY, whole((rows, width)), rows_of(tile, width), rows_of(tile, 128)],
        out_specs=rows_of(tile, width),
        out_shape=jax.ShapeDtypeStruct((rows, width), f32),
        scratch_shapes=[
            pltpu.VMEM((rows + 2 * REACH, width), bf16),
            pltpu.VMEM((rows + 2 * REACH, width), bf16),
            pltpu.VMEM((TAPS * width, width), bf16),
            pltpu.SemaphoreType.DMA((QUARTERS,)),
        ],
        compiler_params=vmem(63),
        cost_estimate=cost(TAPS * rows * width * width, 12 * rows * width),
        name="token_grad",
    )(lengths, place, near, far, d_conv, d_hidden, keep)


def on_device(
    n_dp, n_fsdp, tokens, present, lengths, conv_w, conv_b, gain_one, shift_one, w_in, b_in, w_out, b_out, gain_two, shift_two, cotangent
):
    rows, width = tokens.shape
    total = w_in.shape[1]
    cols = total // width
    devices = n_dp * n_fsdp
    fast = n_dp == 4 and n_fsdp == 8 and conv_w.shape[0] % 16 == 0 and w_in.shape[0] % 16 == 0
    bar = lax.optimization_barrier
    extra = 16
    n = width // devices
    swap = [(i, i ^ 1) for i in range(n_fsdp)]
    across = {r: [(i, i ^ r) for i in range(n_dp)] for r in (1, 2, 3)}
    along = {k: [(i, (i + 2 * k) % n_fsdp) for i in range(n_fsdp)] for k in (1, 2, 3)}
    vectors = (conv_b, gain_one, shift_one, b_out, gain_two, shift_two)
    if fast:
        fsdp = lax.axis_index("fsdp").astype(jnp.int32)
        dp = lax.axis_index("dp").astype(jnp.int32)
        place = jnp.stack([fsdp & 1, fsdp >> 1, dp])
        body = conv_w.shape[0]
        inner_rows, outer_rows = w_in.shape[0], w_out.shape[0]
        blocks = devices // 2

        def from_column(shard):
            return [shard] + [lax.ppermute(shard, "fsdp", along[k]) for k in (1, 2, 3)]

        column = jnp.stack(from_column(conv_w))
        seat = dp * n_fsdp + fsdp
        lane = jnp.arange(width, dtype=jnp.int32)
        line = jnp.arange(extra, dtype=jnp.int32)[:, None]
        lines = jnp.concatenate(
            [jnp.tile(jnp.stack(vectors), (1, devices))]
            + [jnp.tile(b_in, width // b_in.shape[0])[None]] * cols
            + [jnp.zeros((extra - 6 - cols, width), bf16)]
        )
        few = b_in.shape[0]
        own_line = ((line < 6) & (lane // n == seat)) | ((line == 6 + dp) & (lane // few == fsdp))
        lines = jnp.where(own_line, lines, 0)
        ff_own = jnp.concatenate([w_in[:, j * width : (j + 1) * width] for j in range(cols)] + [lines, w_out], axis=0)
        masked, masked_across, keep = prep(tokens, present)
        column, ff_own, masked, masked_across, keep = bar((column, ff_own, masked, masked_across, keep))
        beside_x = lax.ppermute(column, "dp", across[1])
        beside_y = lax.ppermute(column, "dp", across[2])
        ff_rest = from_column(ff_own)
        column, beside_x, beside_y, ff_rest = bar((column, beside_x, beside_y, ff_rest))
        ff_column = jnp.stack(ff_rest)
        near = (column, beside_x, beside_y)
        near = near + tuple(lax.ppermute(piece, "fsdp", swap) for piece in near)
        far = (
            lax.ppermute(beside_x[:2], "dp", across[2]),
            lax.ppermute(beside_y[2:], "dp", across[1]),
        )
        ff = (ff_column, lax.ppermute(ff_column, "dp", across[1]), lax.ppermute(ff_column, "dp", across[2]))
    else:
        place = jnp.zeros((3,), jnp.int32)
        gather = functools.partial(lax.all_gather, axis_name=AXES, axis=0, tiled=True)
        full = gather(conv_w)
        body = full.shape[0] // 2
        depth = full.shape[0] // QUARTERS * (QUARTERS - 1)
        near, far = (full[None, :depth],), (full[None, depth:],)
        lines = [gather(vector) for vector in vectors] + list(gather(b_in).reshape(cols, width))
        lines = jnp.stack(lines + [jnp.zeros_like(lines[0])] * (extra - len(lines)))
        full_in, full_out = gather(w_in), gather(w_out)
        inner_rows, outer_rows = full_in.shape[0] // 2, full_out.shape[0] // 2
        blocks = 1
        ff = [full_in[:, j * width : (j + 1) * width].reshape(2, inner_rows, width) for j in range(cols)]
        ff.append(jnp.stack([lines, jnp.zeros_like(lines)]))
        ff = (jnp.concatenate(ff + [full_out.reshape(2, outer_rows, width)], axis=1),)
        masked, masked_across, keep = prep(tokens, present)

    partial, stacked, w_near = conv_forward(lengths, place, near, masked, fast, body)
    if fast:
        far, ff, partial = bar((far, ff, partial))
        ff = ff + (
            lax.ppermute(ff[1][:2], "dp", across[2]),
            lax.ppermute(ff[2][2:], "dp", across[1]),
        )
        far = far + tuple(lax.ppermute(piece, "fsdp", swap) for piece in far)
        ff = ff + tuple(lax.ppermute(piece, "fsdp", swap) for piece in ff)
    mixed, d_hidden, d_conv, sums, w_far, *ff_grads = feed(
        place, far, ff, stacked, partial, tokens, cotangent, inner_rows, outer_rows, extra, total, fast, body
    )
    def added(terms):
        return sum(term.astype(f32) for term in terms)

    def line_swap(line):
        return [line[0]] + [lax.ppermute(line[k], "fsdp", along[k]) for k in (1, 2, 3)]

    def rounded(*terms):
        return added(terms).astype(bf16)

    if fast:
        ff_near, ff_far_a, ff_far_b = ff_grads[:3]
        came_a, came_b, came = (lax.ppermute(ff_grads[3 + n], "fsdp", swap) for n in (1, 2, 0))
        a_far, b_far, d_conv = bar((ff_far_a + came_a, ff_far_b + came_b, d_conv))
        a_came = lax.ppermute(a_far, "dp", across[1])
        b_came = lax.ppermute(b_far, "dp", across[2])
        conv_keep, conv_send = conv_grad(lengths, place, masked_across, d_conv, blocks, body)
        a_came, b_came, came, conv_keep, conv_send, d_conv = bar((a_came, b_came, came, conv_keep, conv_send, d_conv))
        conv_came = lax.ppermute(conv_send, "fsdp", swap)
        a_last = lax.ppermute(rounded(ff_near[2:4], came[2:4], a_came[2:]), "dp", across[2])
        b_last = lax.ppermute(rounded(ff_near[6:], came[6:], b_came[2:]), "dp", across[1])
        conv_chip = conv_keep + conv_came
        conv_chip, a_last, b_last, d_conv = bar((conv_chip, a_last, b_last, d_conv))
        conv_plane = lax.all_to_all(conv_chip.reshape(4, 4, body, width), "dp", 0, 0, tiled=True)
        line = [rounded(ff_near[k], came[k], a_came[k], a_last[k]) for k in (0, 1)]
        line += [rounded(ff_near[4 + k], came[4 + k], b_came[k], b_last[k]) for k in (0, 1)]
        ff_line = line_swap(line)
        d_tokens = token_grad(lengths, place, w_near, w_far, d_conv, d_hidden, keep)
        d_tokens, ff_line, conv_plane = bar((d_tokens, ff_line, conv_plane))
        conv_line = line_swap([added(conv_plane[r, k] for r in range(4)).astype(bf16) for k in range(4)])
        ff_share = added(ff_line)
        d_conv_w = added(conv_line)
        top = cols * inner_rows
        d_w_in = jnp.concatenate([ff_share[j * inner_rows : (j + 1) * inner_rows] for j in range(cols)], axis=1)
        d_w_out = ff_share[top + extra :]
        seat = dp * n_fsdp + fsdp
        own = lax.dynamic_slice(ff_share[top : top + 6], (0, seat * n), (6, n))
        vector_grads = list(own)
        vector_grads.append(lax.dynamic_slice(ff_share[top + 6], (fsdp * few,), (few,)))
    else:
        conv_pair = conv_grad(lengths, place, masked_across, d_conv, blocks, body)
        d_tokens = token_grad(lengths, place, w_near, w_far, d_conv, d_hidden, keep)
        ff_share = jnp.concatenate(ff_grads, axis=0)
        scatter = functools.partial(lax.psum_scatter, axis_name=AXES, scatter_dimension=0, tiled=True)
        d_in_full = jnp.concatenate(
            [ff_share[:, j * inner_rows : (j + 1) * inner_rows].reshape(-1, width) for j in range(cols)], axis=1
        )
        d_w_in = scatter(d_in_full.astype(f32))
        d_w_out = scatter(ff_share[:, cols * inner_rows + extra :].reshape(-1, width).astype(f32))
        d_conv_w = scatter(jnp.concatenate(conv_pair, axis=0).reshape(-1, width).astype(f32))
        vector_grads = [scatter(line) for line in sums[:6]] + [scatter(sums[6 : 6 + cols].reshape(-1))]
    d_conv_b, d_gain_one, d_shift_one, d_b_out, d_gain_two, d_shift_two, d_b_in = vector_grads
    return (
        mixed, d_tokens, d_conv_w, d_conv_b, d_gain_one, d_shift_one, d_w_in, d_b_in, d_w_out, d_b_out, d_gain_two, d_shift_two
    )


def solution(mesh):
    both = P(AXES)
    flat = P(AXES, None)
    in_specs = (flat, both, flat, flat, both, both, both, flat, both, flat, both, both, both, flat)
    out_specs = (flat, flat, flat, both, both, both, flat, both, flat, both, both, both)
    return jax.shard_map(
        functools.partial(on_device, mesh.shape["dp"], mesh.shape["fsdp"]),
        mesh=mesh,
        in_specs=in_specs,
        out_specs=out_specs,
        check_vma=False,
    )
```

```python
import functools
import jax
import jax.numpy as jnp
from jax import lax
from jax.experimental import pallas as pl
from jax.experimental.pallas import tpu as pltpu
from jax.sharding import PartitionSpec as P

TAPS = 9
STEP = 8
REACH = (TAPS // 2) * STEP
EPSILON = 1e-05
SLAB = 512
QUARTERS = 4
AXES = ("dp", "fsdp")
f32 = jnp.float32
bf16 = jnp.bfloat16
ANY = pl.BlockSpec(memory_space=pl.ANY)
SMEM = pl.BlockSpec(memory_space=pltpu.SMEM)


def dot(a, b):
    return jnp.dot(a, b, preferred_element_type=f32)


def dot_t(a, b):
    return lax.dot_general(a, b, (((1,), (1,)), ((), ())), preferred_element_type=f32)


def dot_rows(a, b):
    return lax.dot_general(a, b, (((0,), (0,)), ((), ())), preferred_element_type=f32)


def gelu_pair(v):
    phi = 0.5 + 0.5 * lax.erf(v * 0.7071067811865476)
    return v * phi, phi + v * (0.3989422804014327 * jnp.exp2(v * v * -0.7213475204444817))


def mean(v):
    return jnp.sum(v, axis=-1, keepdims=True) * (1.0 / v.shape[-1])


def fold(v):
    return sum(v[r : r + 8] for r in range(0, v.shape[0], 8))


def slabs(total, size):
    return [pl.ds(r, size) for r in range(0, total, size)]


def colsum(v):
    return jnp.sum(v, axis=0, keepdims=True)


def vmem(mib):
    return pltpu.CompilerParams(vmem_limit_bytes=mib << 20)


def cost(macs, nbytes):
    return pl.CostEstimate(flops=macs // 32, bytes_accessed=nbytes // 32, transcendentals=0)


def whole(shape):
    return pl.BlockSpec(shape, lambda *_: (0,) * len(shape), pipeline_mode=pl.Buffered(1))


def rows_of(tile, width):
    return pl.BlockSpec((tile, width), lambda i: (i, 0))


def window_reach(len_ref, position, wins, total):
    first = jnp.zeros_like(position)
    last = jnp.full_like(position, total - 1)
    edge = jnp.int32(0)
    edges = []
    for w in range(wins - 1):
        edge = edge + len_ref[0, w]
        edges.append(edge)
    for edge in edges:
        first = jnp.where(position >= edge, edge, first)
    for edge in reversed(edges):
        last = jnp.where(position < edge, edge - 1, last)
    return position - first, last - position


def within(block, reach, tap):
    shift = (tap - TAPS // 2) * STEP
    if shift == 0:
        return block
    before, after = reach
    valid = (before >= -shift) if shift < 0 else (after >= shift)
    return block * wide(jnp.where(valid, 1.0, 0.0).astype(bf16), block.shape[1])


def wide(mask, width):
    return jnp.concatenate([mask] * (width // 128), axis=1)


def prep_kernel(tokens_ref, present_ref, masked_ref, across_ref, keep_ref):
    tile, width = tokens_ref.shape
    for r in range(0, tile, 128):
        line = jnp.broadcast_to((present_ref[0, r // 128 : r // 128 + 1] > 0).astype(f32), (128, 128))
        kept = line.T
        keep_ref[r : r + 128] = kept
        masked_ref[r : r + 128] = tokens_ref[r : r + 128] * wide(kept.astype(bf16), width)
    across_ref[...] = masked_ref[...].T


def prep(tokens, present):
    rows, width = tokens.shape
    tile = 512
    return pl.pallas_call(
        prep_kernel,
        grid=(rows // tile,),
        in_specs=[rows_of(tile, width), pl.BlockSpec((1, tile // 128, 128), lambda i: (i, 0, 0))],
        out_specs=[rows_of(tile, width), pl.BlockSpec((width, tile), lambda i: (0, i)), rows_of(tile, 128)],
        out_shape=[
            jax.ShapeDtypeStruct((rows, width), bf16),
            jax.ShapeDtypeStruct((width, rows), bf16),
            jax.ShapeDtypeStruct((rows, 128), f32),
        ],
        compiler_params=vmem(63),
        cost_estimate=cost(0, 24 * rows * width),
        name="prep",
    )(tokens, present.reshape(rows // tile, tile // 128, 128))


def conv_sites(pieces, first, place, fast, body):
    if not fast:
        return [(piece.at[0], first, 0) for piece in pieces]
    core, z, _ = place
    sites = []
    per = len(pieces) // 2
    for n, piece in enumerate(pieces):
        which = core if n < per else 1 - core
        kind = first + n % per
        for hop in range(piece.shape[0]):
            row = (((z - hop - (2 if kind == 4 else 0)) & 3) * 2 + which) * body
            sites.append((piece.at[hop], min(kind, 3), row))
    return sites


def conv_copies(sites, base, store, sems):
    copies = []
    for n, (source, kind, row) in enumerate(sites):
        start = pl.multiple_of(base(kind) + row, 16)
        copies.append(pltpu.make_async_copy(source, store.at[pl.ds(start, source.shape[0])], sems.at[n]))
    return copies


def conv_kernel(len_ref, place_ref, *refs, count, fast, body, wins):
    pieces = refs[:count]
    masked_ref, conv_ref, far_ref, near_ref, store, stack, even, odd, sems, out_sem = refs[count:]
    step = pl.program_id(0)
    rows, width = masked_ref.shape
    tile = conv_ref.shape[0]
    depth = store.shape[0] // (QUARTERS - 1)
    back = pltpu.make_async_copy(store, near_ref, out_sem)
    sites = conv_sites(pieces, 0, tuple(place_ref[i] for i in range(3)), fast, body)
    copies = conv_copies(sites, lambda kind: kind * depth, store, sems)

    @pl.when(step == 0)
    def _():
        for copy in copies:
            copy.start()
        lay_shifted(masked_ref, even, odd, 256)

    start = pl.multiple_of(step * tile, tile)
    position = lax.broadcasted_iota(jnp.int32, (tile, 128), 0) + start
    reach = window_reach(len_ref, position, wins, rows)
    per = depth // 128
    for tap in range(TAPS):
        offset = pl.multiple_of(start + tap // 2 * 2 * STEP, 2 * STEP)
        block = within((odd if tap % 2 else even)[pl.ds(offset, tile)], reach, tap)
        for lane in range(0, width, 128):
            chunk = (tap * width + lane) // 128
            seat = ((chunk // per) ^ place_ref[2]) * per + chunk % per
            stack[:, pl.ds(pl.multiple_of(seat * 128, 128), 128)] = block[:, lane : lane + 128]

    @pl.when(step == 0)
    def _():
        for copy in copies:
            copy.wait()
        back.start()

    far_ref[...] = stack[:, store.shape[0] :]
    conv_ref[...] = dot(stack[:, : store.shape[0]], store[...])

    @pl.when(step == pl.num_programs(0) - 1)
    def _():
        back.wait()


def conv_forward(lengths, place, pieces, masked, fast, body):
    rows, width = masked.shape
    depth = TAPS * width // QUARTERS
    tile = 512
    return pl.pallas_call(
        functools.partial(conv_kernel, count=len(pieces), fast=fast, body=body, wins=lengths.shape[1]),
        grid=(rows // tile,),
        in_specs=[SMEM, SMEM] + [ANY] * len(pieces) + [whole((rows, width))],
        out_specs=[rows_of(tile, width), rows_of(tile, depth), ANY],
        out_shape=[
            jax.ShapeDtypeStruct((rows, width), f32),
            jax.ShapeDtypeStruct((rows, depth), bf16),
            jax.ShapeDtypeStruct(((QUARTERS - 1) * depth, width), bf16),
        ],
        scratch_shapes=[
            pltpu.VMEM(((QUARTERS - 1) * depth, width), bf16),
            pltpu.VMEM((tile, QUARTERS * depth), bf16),
            pltpu.VMEM((rows + 2 * REACH, width), bf16),
            pltpu.VMEM((rows + 2 * REACH, width), bf16),
            pltpu.SemaphoreType.DMA((sum(piece.shape[0] for piece in pieces),)),
            pltpu.SemaphoreType.DMA,
        ],
        compiler_params=vmem(63),
        cost_estimate=cost(3 * depth * rows * width, 24 * rows * width),
        name="conv_forward",
    )(lengths, place, *pieces, masked)


def ff_copies(pieces, place, fast, store, sems):
    if not fast:
        return [pltpu.make_async_copy(pieces[0], store, sems.at[0])]
    core, own_z, dp = place
    per = len(pieces) // 2
    copies = []
    for n, piece in enumerate(pieces):
        which = core if n < per else 1 - core
        kind = n % per
        for hop in range(piece.shape[0]):
            z = (own_z - hop - (2 if kind == 4 else 0)) & 3
            block = ((dp ^ min(kind, 3)) * 4 + z) * 2 + which
            copies.append(pltpu.make_async_copy(piece.at[hop], store.at[block], sems.at[len(copies)]))
    return copies


def relay_seat(r, k):
    if k < 2:
        return (1, r // 2 * 2 + k) if r % 2 else (0, r // 2 * 2 + k)
    return (2, r % 2 * 2 + k - 2) if r // 2 else (0, 4 + r * 2 + k - 2)


def feed_kernel(place_ref, *refs, far, count, outs, tiles, chunk, inner_rows, outer_rows, extra, fast, body):
    far_pieces, ff_pieces = refs[:far], refs[far : far + count]
    refs = refs[far + count :]
    stacked_ref, partial_ref, tokens_ref, cot_ref = refs[:4]
    mixed_ref, d_hidden_ref, d_conv_ref, sums_ref, far_ref = refs[4:9]
    targets = refs[9 : 9 + outs]
    refs = refs[9 + outs :]
    packed, w_in, w_far, small_ref, bend, slope_ref, normed_ref, hiddens, actives, d_outers, d_inners = refs[:11]
    tallies, ff_sems, far_sems, grad_sems, out_sem = refs[11:]
    slab = SLAB
    store = packed
    step = pl.program_id(0)
    tile, width = tokens_ref.shape
    total = w_in.shape[1]
    blocks = packed.shape[0]
    cols = total // width
    place = tuple(place_ref[i] for i in range(3))
    core = place[0]
    depth = w_far.shape[0]
    top = cols * inner_rows
    back = pltpu.make_async_copy(w_far, far_ref, out_sem)

    @pl.when(step == 0)
    def _():
        copies = ff_copies(ff_pieces, place, fast, packed, ff_sems)
        far_sites = conv_sites(far_pieces, QUARTERS - 1, place, fast, body)
        copies += conv_copies(far_sites, lambda kind: 0, w_far, far_sems)
        for copy in copies:
            copy.start()
        tallies[...] = jnp.zeros_like(tallies)
        for copy in copies:
            copy.wait()
        back.start()
        for j in range(cols):
            part = packed[:, j * inner_rows : (j + 1) * inner_rows].reshape(blocks * inner_rows, width)
            w_in[:, j * width : (j + 1) * width] = part
        small_ref[...] = jnp.sum(packed[:, top : top + extra].astype(f32), axis=0)

    base = pl.multiple_of(jnp.minimum(step, tiles - 1) * tile, tile)

    def at(part):
        return pl.ds(pl.multiple_of(base + part.start, part.size), part.size)

    def add_tally(row, col, term):
        tallies[8 * row : 8 * row + 8, col : col + term.shape[1]] += fold(term)

    def out_rows(j):
        if outer_rows > chunk:
            per = outer_rows // chunk
            first = top + extra + j % per * chunk
            return packed[j // per, first : first + chunk]
        count = chunk // outer_rows
        return packed[j * count : (j + 1) * count, top + extra :].reshape(chunk, width)

    in_rows = step < tiles

    @pl.when(in_rows)
    def _():
        for part in slabs(tile, slab):
            conv = partial_ref[part] + dot(stacked_ref[part], w_far[...]) + small_ref[0:1]
            bent, slope = gelu_pair(conv)
            shifted = bent - mean(bent)
            root = lax.rsqrt(mean(shifted * shifted) + EPSILON)
            normed = shifted * root
            normed_ref[part] = normed
            slope_ref[part] = slope * root
            hiddens[at(part)] = (
                tokens_ref[part].astype(f32) + normed * small_ref[1:2] + small_ref[2:3]
            ).astype(bf16)

    for j in range(total // chunk):
        cut = slice(j * chunk, (j + 1) * chunk)

        @pl.when(in_rows)
        def _(j=j, cut=cut):
            for part in slabs(tile, slab):
                inner = dot(hiddens[at(part)], w_in[:, cut]) + small_ref[6 + j : 7 + j]
                act, slope = gelu_pair(inner)
                actives[at(part), cut] = act.astype(bf16)
                bend[part, cut] = slope

    @pl.when(in_rows)
    def _():
        gain_two = small_ref[4:5]
        for part in slabs(tile, slab):
            full = packed[:, top + extra :].reshape(blocks * outer_rows, width)
            outer = dot(actives[at(part)], full) + small_ref[3:4]
            shifted = outer - mean(outer)
            root = lax.rsqrt(mean(shifted * shifted) + EPSILON)
            normal = shifted * root
            mixed_ref[part] = (hiddens[at(part)].astype(f32) + normal * gain_two + small_ref[5:6]).astype(bf16)
            cot = cot_ref[part].astype(f32)
            q = cot * gain_two
            d_outer_full = root * (q - mean(q) - normal * mean(q * normal))
            d_outers[at(part)] = d_outer_full.astype(bf16)
            add_tally(3, 0, d_outer_full)
            add_tally(4, 0, cot * normal)
            add_tally(5, 0, cot)

    for j in range(total // chunk):
        cut = slice(j * chunk, (j + 1) * chunk)

        @pl.when(in_rows)
        def _(j=j, cut=cut):
            for part in slabs(tile, slab):
                d_inner = dot_t(d_outers[at(part)], out_rows(j)) * bend[part, cut]
                d_inners[at(part), cut] = d_inner.astype(bf16)
                add_tally(6 + j, 0, d_inner)

    @pl.when(in_rows)
    def _():
        for part in slabs(tile, slab):
            d_hidden = dot_t(d_inners[at(part)], w_in[...]) + cot_ref[part].astype(f32)
            d_hidden_ref[part] = d_hidden
            first = normed_ref[part]
            p = d_hidden * small_ref[1:2]
            d_conv = slope_ref[part] * (p - mean(p) - first * mean(p * first))
            d_conv_ref[part] = d_conv.astype(bf16)
            add_tally(0, 0, d_conv)
            add_tally(1, 0, d_hidden * first)
            add_tally(2, 0, d_hidden)

    def put_blocks(dp):
        for r in range(4):

            @pl.when((dp ^ place[2]) == r)
            def _(r=r):
                for n, which in enumerate((core, 1 - core)):
                    for k in range(4):
                        array, seat = relay_seat(r, k)
                        target = targets[3 * n + array].at[seat]
                        block = (dp * 4 + ((place[1] + k) & 3)) * 2 + which
                        pltpu.make_async_copy(store.at[block], target, grad_sems.at[dp * 8 + 4 * n + k]).start()

    @pl.when(step == tiles)
    def _():
        for row in range(sums_ref.shape[0]):
            sums_ref[row : row + 1] = colsum(tallies[8 * row : 8 * row + 8])
        if fast:
            head = sums_ref[:6].astype(bf16)
            rest = jnp.zeros((extra - 7, width), bf16)
            for dp in range(blocks // 8):
                line = jnp.concatenate([head, sums_ref[6 + dp : 7 + dp].astype(bf16), rest])
                store[8 * dp : 8 * dp + 8, top : top + extra] = jnp.broadcast_to(line, (8, extra, width))

    for j in range(cols):
        part = slice(j * width, (j + 1) * width)

        @pl.when(step == tiles)
        def _(j=j, part=part):
            d_in = dot_rows(hiddens[...], d_inners[:, part]).astype(bf16)
            store[:, j * inner_rows : (j + 1) * inner_rows] = d_in.reshape(blocks, inner_rows, width)

    for j in range(cols):
        part = slice(j * width, (j + 1) * width)

        @pl.when(step == tiles)
        def _(j=j, part=part):
            d_out = dot_rows(actives[:, part], d_outers[...]).astype(bf16)
            first = top + extra
            if fast:
                many = width // outer_rows
                store[j * many : (j + 1) * many, first : first + outer_rows] = d_out.reshape(many, outer_rows, width)
                put_blocks(j)
            else:
                per = outer_rows // width
                start = first + j % per * width
                store[j // per, start : start + width] = d_out

    @pl.when(step == pl.num_programs(0) - 1)
    def _():
        back.wait()
        if fast:
            for n in range(blocks):
                pltpu.make_async_copy(store.at[n], targets[0].at[0], grad_sems.at[n]).wait()
        else:
            copies = [
                pltpu.make_async_copy(store.at[pl.ds(n, 1)], target, grad_sems.at[n]) for n, target in enumerate(targets)
            ]
            for copy in copies:
                copy.start()
            for copy in copies:
                copy.wait()


def feed(place, far, pieces, stacked, partial, tokens, cotangent, inner_rows, outer_rows, extra, total, fast, body):
    rows, width = tokens.shape
    blocks = width // inner_rows
    tile = 512
    tiles, cols = rows // tile, total // width
    share = cols * inner_rows + extra + outer_rows
    depth = stacked.shape[1]
    seats = (8, 4, 4) * 2 if fast else (1, 1)
    tall = pl.BlockSpec((tile, width), lambda i: (jnp.minimum(i, tiles - 1), 0))
    last = pl.BlockSpec((tile, depth), lambda i: (jnp.minimum(i, tiles - 1), 0))
    return pl.pallas_call(
        functools.partial(
            feed_kernel, far=len(far), count=len(pieces), outs=len(seats), tiles=tiles, chunk=512, inner_rows=inner_rows,
            outer_rows=outer_rows, extra=extra, fast=fast, body=body,
        ),
        grid=(tiles + 1,),
        in_specs=[SMEM] + [ANY] * (len(far) + len(pieces)) + [last, tall, tall, tall],
        out_specs=[tall, tall, tall, pl.BlockSpec((16, width), lambda i: (0, 0)), ANY] + [ANY] * len(seats),
        out_shape=[
            jax.ShapeDtypeStruct((rows, width), bf16),
            jax.ShapeDtypeStruct((rows, width), f32),
            jax.ShapeDtypeStruct((rows, width), bf16),
            jax.ShapeDtypeStruct((16, width), f32),
            jax.ShapeDtypeStruct((depth, width), bf16),
        ] + [jax.ShapeDtypeStruct((count, share, width), bf16) for count in seats],
        scratch_shapes=[
            pltpu.VMEM((blocks, share, width), bf16),
            pltpu.VMEM((width, total), bf16),
            pltpu.VMEM((depth, width), bf16),
            pltpu.VMEM((extra, width), f32),
            pltpu.VMEM((tile, total), f32),
            pltpu.VMEM((tile, width), f32),
            pltpu.VMEM((tile, width), f32),
            pltpu.VMEM((rows, width), bf16),
            pltpu.VMEM((rows, total), bf16),
            pltpu.VMEM((rows, width), bf16),
            pltpu.VMEM((rows, total), bf16),
            pltpu.VMEM((8 * extra, width), f32),
            pltpu.SemaphoreType.DMA((sum(piece.shape[0] for piece in pieces),)),
            pltpu.SemaphoreType.DMA((sum(piece.shape[0] for piece in far),)),
            pltpu.SemaphoreType.DMA((blocks,)),
            pltpu.SemaphoreType.DMA,
        ],
        compiler_params=vmem(63),
        cost_estimate=cost(6 * rows * width * total, 40 * rows * width),
        name="feed",
    )(place, *far, *pieces, stacked, partial, tokens, cotangent)


def lay_shifted(values_ref, even, odd, tile):
    rows, width = values_ref.shape
    zeros = jnp.zeros((REACH, width), bf16)
    even[:REACH] = zeros
    even[rows + REACH :] = zeros
    odd[:REACH] = zeros
    odd[rows:] = jnp.zeros((2 * REACH, width), bf16)
    for r in range(0, rows, tile):
        block = values_ref[r : r + tile]
        even[REACH + r : REACH + r + tile] = block
        odd[REACH - STEP + r : REACH - STEP + r + tile] = block


def tap_products(len_ref, place, masked_ref, even, odd, part, targets, store, sems, *, wins, blocks, body, turn):
    channels, rows = masked_ref.shape
    width = part.stop - part.start
    core = place[0]
    position = lax.broadcasted_iota(jnp.int32, (rows, 128), 0)
    reach = window_reach(len_ref, position, wins, rows)
    copies = []
    for tap in range(TAPS):
        mirror = TAPS - 1 - tap
        source = (odd if mirror % 2 else even)[mirror // 2 * 2 * STEP : mirror // 2 * 2 * STEP + rows, part]
        store[tap * channels : (tap + 1) * channels] = dot(masked_ref[...], within(source, reach, mirror)).astype(bf16)
        while len(copies) // 2 < blocks and (len(copies) // 2 + 1) * 2 * body <= (tap + 1) * channels:
            block = len(copies) // 2
            seat = ((block // 4) ^ turn) * 4 + ((block % 4 - place[1]) & 3) if blocks == 16 else block
            for n, (target, which) in enumerate(zip(targets, (core, 1 - core))):
                start = pl.multiple_of((2 * block + which) * body, 16)
                copies.append(pltpu.make_async_copy(store.at[pl.ds(start, body)], target.at[seat], sems.at[n, block]))
                copies[-1].start()
    for copy in copies:
        copy.wait()


def conv_grad_kernel(len_ref, place_ref, masked_ref, d_conv_ref, keep_ref, send_ref, even, odd, store, sems, *, wins, blocks, body):
    lay_shifted(d_conv_ref, even, odd, 256)
    tap_products(
        len_ref, tuple(place_ref[i] for i in range(3)), masked_ref, even, odd, slice(0, d_conv_ref.shape[1]),
        (keep_ref, send_ref), store, sems, wins=wins, blocks=blocks, body=body, turn=0,
    )


def conv_grad(lengths, place, masked, d_conv, blocks, body):
    channels, rows = masked.shape
    width = d_conv.shape[1]
    return pl.pallas_call(
        functools.partial(conv_grad_kernel, wins=lengths.shape[1], blocks=blocks, body=body),
        grid=(1,),
        in_specs=[SMEM, SMEM, whole(masked.shape), whole((rows, width))],
        out_specs=[ANY, ANY],
        out_shape=[jax.ShapeDtypeStruct((blocks, body, width), bf16)] * 2,
        scratch_shapes=[
            pltpu.VMEM((rows + 2 * REACH, width), bf16),
            pltpu.VMEM((rows + 2 * REACH, width), bf16),
            pltpu.VMEM((TAPS * channels, width), bf16),
            pltpu.SemaphoreType.DMA((2, blocks)),
        ],
        compiler_params=vmem(63),
        cost_estimate=cost(TAPS * rows * width * channels, 12 * rows * width),
        name="conv_grad",
    )(lengths, place, masked, d_conv)


def token_grad_kernel(
    len_ref, place_ref, near_ref, far_ref, d_conv_ref, d_hidden_ref, keep_ref, d_tokens_ref, even, odd, store, sems, *, wins, tile
):
    step = pl.program_id(0)
    rows, width = d_conv_ref.shape
    depth = far_ref.shape[0]

    @pl.when(step == 0)
    def _():
        copies = []
        for kind in range(QUARTERS):
            source = far_ref if kind == QUARTERS - 1 else near_ref.at[pl.ds(kind * depth, depth)]
            start = pl.multiple_of((place_ref[2] ^ kind) * depth, 128)
            copies.append(pltpu.make_async_copy(source, store.at[pl.ds(start, depth)], sems.at[kind]))
        for copy in copies:
            copy.start()
        lay_shifted(d_conv_ref, even, odd, 256)
        for copy in copies:
            copy.wait()

    start = pl.multiple_of(step * tile, tile)
    position = lax.broadcasted_iota(jnp.int32, (tile, 128), 0) + start
    reach = window_reach(len_ref, position, wins, rows)
    total = None
    for tap in range(TAPS):
        mirror = TAPS - 1 - tap
        offset = pl.multiple_of(start + mirror // 2 * 2 * STEP, 2 * STEP)
        block = within((odd if mirror % 2 else even)[pl.ds(offset, tile)], reach, mirror)
        term = dot_t(block, store[tap * width : (tap + 1) * width])
        total = term if total is None else total + term
    d_tokens_ref[...] = d_hidden_ref[...] + total * wide(keep_ref[...], width)


def token_grad(lengths, place, near, far, d_conv, d_hidden, keep):
    rows, width = d_conv.shape
    tile = 512
    return pl.pallas_call(
        functools.partial(token_grad_kernel, wins=lengths.shape[1], tile=tile),
        grid=(rows // tile,),
        in_specs=[SMEM, SMEM, ANY, ANY, whole((rows, width)), rows_of(tile, width), rows_of(tile, 128)],
        out_specs=rows_of(tile, width),
        out_shape=jax.ShapeDtypeStruct((rows, width), f32),
        scratch_shapes=[
            pltpu.VMEM((rows + 2 * REACH, width), bf16),
            pltpu.VMEM((rows + 2 * REACH, width), bf16),
            pltpu.VMEM((TAPS * width, width), bf16),
            pltpu.SemaphoreType.DMA((QUARTERS,)),
        ],
        compiler_params=vmem(63),
        cost_estimate=cost(TAPS * rows * width * width, 12 * rows * width),
        name="token_grad",
    )(lengths, place, near, far, d_conv, d_hidden, keep)


def on_device(
    n_dp, n_fsdp, tokens, present, lengths, conv_w, conv_b, gain_one, shift_one, w_in, b_in, w_out, b_out, gain_two, shift_two, cotangent
):
    rows, width = tokens.shape
    total = w_in.shape[1]
    cols = total // width
    devices = n_dp * n_fsdp
    fast = n_dp == 4 and n_fsdp == 8 and conv_w.shape[0] % 16 == 0 and w_in.shape[0] % 16 == 0
    bar = lax.optimization_barrier
    extra = 16
    n = width // devices
    swap = [(i, i ^ 1) for i in range(n_fsdp)]
    across = {r: [(i, i ^ r) for i in range(n_dp)] for r in (1, 2, 3)}
    along = {k: [(i, (i + 2 * k) % n_fsdp) for i in range(n_fsdp)] for k in (1, 2, 3)}
    vectors = (conv_b, gain_one, shift_one, b_out, gain_two, shift_two)
    if fast:
        fsdp = lax.axis_index("fsdp").astype(jnp.int32)
        dp = lax.axis_index("dp").astype(jnp.int32)
        place = jnp.stack([fsdp & 1, fsdp >> 1, dp])
        body = conv_w.shape[0]
        inner_rows, outer_rows = w_in.shape[0], w_out.shape[0]
        blocks = devices // 2

        def from_column(shard):
            return [shard] + [lax.ppermute(shard, "fsdp", along[k]) for k in (1, 2, 3)]

        column = jnp.stack(from_column(conv_w))
        seat = dp * n_fsdp + fsdp
        lane = jnp.arange(width, dtype=jnp.int32)
        line = jnp.arange(extra, dtype=jnp.int32)[:, None]
        lines = jnp.concatenate(
            [jnp.tile(jnp.stack(vectors), (1, devices))]
            + [jnp.tile(b_in, width // b_in.shape[0])[None]] * cols
            + [jnp.zeros((extra - 6 - cols, width), bf16)]
        )
        few = b_in.shape[0]
        own_line = ((line < 6) & (lane // n == seat)) | ((line == 6 + dp) & (lane // few == fsdp))
        lines = jnp.where(own_line, lines, 0)
        ff_own = jnp.concatenate([w_in[:, j * width : (j + 1) * width] for j in range(cols)] + [lines, w_out], axis=0)
        masked, masked_across, keep = prep(tokens, present)
        column, ff_own, masked, masked_across, keep, place = bar((column, ff_own, masked, masked_across, keep, place))
        beside_x = lax.ppermute(column, "dp", across[1])
        beside_y = lax.ppermute(column, "dp", across[2])
        ff_rest = from_column(ff_own)
        ff_column = jnp.stack(ff_rest)
        column, beside_x, beside_y, ff_column = bar((column, beside_x, beside_y, ff_column))
        near = (column, beside_x, beside_y)
        near = near + tuple(lax.ppermute(piece, "fsdp", swap) for piece in near)
        far = (
            lax.ppermute(beside_x[:2], "dp", across[2]),
            lax.ppermute(beside_y[2:], "dp", across[1]),
        )
        ff = (ff_column, lax.ppermute(ff_column, "dp", across[1]), lax.ppermute(ff_column, "dp", across[2]))
    else:
        place = jnp.zeros((3,), jnp.int32)
        gather = functools.partial(lax.all_gather, axis_name=AXES, axis=0, tiled=True)
        full = gather(conv_w)
        body = full.shape[0] // 2
        depth = full.shape[0] // QUARTERS * (QUARTERS - 1)
        near, far = (full[None, :depth],), (full[None, depth:],)
        lines = [gather(vector) for vector in vectors] + list(gather(b_in).reshape(cols, width))
        lines = jnp.stack(lines + [jnp.zeros_like(lines[0])] * (extra - len(lines)))
        full_in, full_out = gather(w_in), gather(w_out)
        inner_rows, outer_rows = full_in.shape[0] // 2, full_out.shape[0] // 2
        blocks = 1
        ff = [full_in[:, j * width : (j + 1) * width].reshape(2, inner_rows, width) for j in range(cols)]
        ff.append(jnp.stack([lines, jnp.zeros_like(lines)]))
        ff = (jnp.concatenate(ff + [full_out.reshape(2, outer_rows, width)], axis=1),)
        masked, masked_across, keep = prep(tokens, present)

    partial, stacked, w_near = conv_forward(lengths, place, near, masked, fast, body)
    if fast:
        far, ff, partial = bar((far, ff, partial))
        ff = ff + (
            lax.ppermute(ff[1][:2], "dp", across[2]),
            lax.ppermute(ff[2][2:], "dp", across[1]),
        )
        far = far + tuple(lax.ppermute(piece, "fsdp", swap) for piece in far)
        ff = ff + tuple(lax.ppermute(piece, "fsdp", swap) for piece in ff)
    mixed, d_hidden, d_conv, sums, w_far, *ff_grads = feed(
        place, far, ff, stacked, partial, tokens, cotangent, inner_rows, outer_rows, extra, total, fast, body
    )
    def added(terms):
        return sum(term.astype(f32) for term in terms)

    def line_swap(line):
        return [line[0]] + [lax.ppermute(line[k], "fsdp", along[k]) for k in (1, 2, 3)]

    def rounded(*terms):
        return added(terms).astype(bf16)

    if fast:
        ff_near, ff_far_a, ff_far_b = ff_grads[:3]
        came_a, came_b, came = (lax.ppermute(ff_grads[3 + n], "fsdp", swap) for n in (1, 2, 0))
        a_far, b_far, d_conv = bar((ff_far_a + came_a, ff_far_b + came_b, d_conv))
        a_came = lax.ppermute(a_far, "dp", across[1])
        b_came = lax.ppermute(b_far, "dp", across[2])
        conv_keep, conv_send = conv_grad(lengths, place, masked_across, d_conv, blocks, body)
        a_came, b_came, came, conv_keep, conv_send, d_conv = bar((a_came, b_came, came, conv_keep, conv_send, d_conv))
        conv_came = lax.ppermute(conv_send, "fsdp", swap)
        a_last = lax.ppermute(rounded(ff_near[2:4], came[2:4], a_came[2:]), "dp", across[2])
        b_last = lax.ppermute(rounded(ff_near[6:], came[6:], b_came[2:]), "dp", across[1])
        conv_chip = conv_keep + conv_came
        conv_chip, a_last, b_last, d_conv = bar((conv_chip, a_last, b_last, d_conv))
        conv_plane = lax.all_to_all(conv_chip.reshape(4, 4, body, width), "dp", 0, 0, tiled=True)
        line = [rounded(ff_near[k], came[k], a_came[k], a_last[k]) for k in (0, 1)]
        line += [rounded(ff_near[4 + k], came[4 + k], b_came[k], b_last[k]) for k in (0, 1)]
        ff_line = line_swap(line)
        d_tokens = token_grad(lengths, place, w_near, w_far, d_conv, d_hidden, keep)
        d_tokens, ff_line, conv_plane = bar((d_tokens, ff_line, conv_plane))
        conv_line = line_swap([added(conv_plane[r, k] for r in range(4)).astype(bf16) for k in range(4)])
        ff_share = added(ff_line)
        d_conv_w = added(conv_line)
        top = cols * inner_rows
        d_w_in = jnp.concatenate([ff_share[j * inner_rows : (j + 1) * inner_rows] for j in range(cols)], axis=1)
        d_w_out = ff_share[top + extra :]
        seat = dp * n_fsdp + fsdp
        own = lax.dynamic_slice(ff_share[top : top + 6], (0, seat * n), (6, n))
        vector_grads = list(own)
        vector_grads.append(lax.dynamic_slice(ff_share[top + 6], (fsdp * few,), (few,)))
    else:
        conv_pair = conv_grad(lengths, place, masked_across, d_conv, blocks, body)
        d_tokens = token_grad(lengths, place, w_near, w_far, d_conv, d_hidden, keep)
        ff_share = jnp.concatenate(ff_grads, axis=0)
        scatter = functools.partial(lax.psum_scatter, axis_name=AXES, scatter_dimension=0, tiled=True)
        d_in_full = jnp.concatenate(
            [ff_share[:, j * inner_rows : (j + 1) * inner_rows].reshape(-1, width) for j in range(cols)], axis=1
        )
        d_w_in = scatter(d_in_full.astype(f32))
        d_w_out = scatter(ff_share[:, cols * inner_rows + extra :].reshape(-1, width).astype(f32))
        d_conv_w = scatter(jnp.concatenate(conv_pair, axis=0).reshape(-1, width).astype(f32))
        vector_grads = [scatter(line) for line in sums[:6]] + [scatter(sums[6 : 6 + cols].reshape(-1))]
    d_conv_b, d_gain_one, d_shift_one, d_b_out, d_gain_two, d_shift_two, d_b_in = vector_grads
    return (
        mixed, d_tokens, d_conv_w, d_conv_b, d_gain_one, d_shift_one, d_w_in, d_b_in, d_w_out, d_b_out, d_gain_two, d_shift_two
    )


def solution(mesh):
    both = P(AXES)
    flat = P(AXES, None)
    in_specs = (flat, both, flat, flat, both, both, both, flat, both, flat, both, both, both, flat)
    out_specs = (flat, flat, flat, both, both, both, flat, both, flat, both, both, both)
    return jax.shard_map(
        functools.partial(on_device, mesh.shape["dp"], mesh.shape["fsdp"]),
        mesh=mesh,
        in_specs=in_specs,
        out_specs=out_specs,
        check_vma=False,
    )
```

```python
import functools
import jax
import jax.numpy as jnp
from jax import lax
from jax.experimental import pallas as pl
from jax.experimental.pallas import tpu as pltpu
from jax.sharding import PartitionSpec as P

TAPS = 9
STEP = 8
REACH = (TAPS // 2) * STEP
EPSILON = 1e-05
SLAB = 512
QUARTERS = 4
AXES = ("dp", "fsdp")
f32 = jnp.float32
bf16 = jnp.bfloat16
ANY = pl.BlockSpec(memory_space=pl.ANY)
SMEM = pl.BlockSpec(memory_space=pltpu.SMEM)


def dot(a, b):
    return jnp.dot(a, b, preferred_element_type=f32)


def dot_t(a, b):
    return lax.dot_general(a, b, (((1,), (1,)), ((), ())), preferred_element_type=f32)


def dot_rows(a, b):
    return lax.dot_general(a, b, (((0,), (0,)), ((), ())), preferred_element_type=f32)


def gelu_pair(v):
    phi = 0.5 + 0.5 * lax.erf(v * 0.7071067811865476)
    return v * phi, phi + v * (0.3989422804014327 * jnp.exp2(v * v * -0.7213475204444817))


def mean(v):
    return jnp.sum(v, axis=-1, keepdims=True) * (1.0 / v.shape[-1])


def fold(v):
    return sum(v[r : r + 8] for r in range(0, v.shape[0], 8))


def slabs(total, size):
    return [pl.ds(r, size) for r in range(0, total, size)]


def colsum(v):
    return jnp.sum(v, axis=0, keepdims=True)


def vmem(mib):
    return pltpu.CompilerParams(vmem_limit_bytes=mib << 20)


def cost(macs, nbytes):
    return pl.CostEstimate(flops=macs // 32, bytes_accessed=nbytes // 32, transcendentals=0)


def whole(shape):
    return pl.BlockSpec(shape, lambda *_: (0,) * len(shape), pipeline_mode=pl.Buffered(1))


def rows_of(tile, width):
    return pl.BlockSpec((tile, width), lambda i: (i, 0))


def window_reach(len_ref, position, wins, total):
    first = jnp.zeros_like(position)
    last = jnp.full_like(position, total - 1)
    edge = jnp.int32(0)
    edges = []
    for w in range(wins - 1):
        edge = edge + len_ref[0, w]
        edges.append(edge)
    for edge in edges:
        first = jnp.where(position >= edge, edge, first)
    for edge in reversed(edges):
        last = jnp.where(position < edge, edge - 1, last)
    return position - first, last - position


def within(block, reach, tap):
    shift = (tap - TAPS // 2) * STEP
    if shift == 0:
        return block
    before, after = reach
    valid = (before >= -shift) if shift < 0 else (after >= shift)
    return block * wide(jnp.where(valid, 1.0, 0.0).astype(bf16), block.shape[1])


def wide(mask, width):
    return jnp.concatenate([mask] * (width // 128), axis=1)


def prep_kernel(tokens_ref, present_ref, masked_ref, across_ref, keep_ref):
    tile, width = tokens_ref.shape
    for r in range(0, tile, 128):
        line = jnp.broadcast_to((present_ref[0, r // 128 : r // 128 + 1] > 0).astype(f32), (128, 128))
        kept = line.T
        keep_ref[r : r + 128] = kept
        masked_ref[r : r + 128] = tokens_ref[r : r + 128] * wide(kept.astype(bf16), width)
    across_ref[...] = masked_ref[...].T


def prep(tokens, present):
    rows, width = tokens.shape
    tile = 512
    return pl.pallas_call(
        prep_kernel,
        grid=(rows // tile,),
        in_specs=[rows_of(tile, width), pl.BlockSpec((1, tile // 128, 128), lambda i: (i, 0, 0))],
        out_specs=[rows_of(tile, width), pl.BlockSpec((width, tile), lambda i: (0, i)), rows_of(tile, 128)],
        out_shape=[
            jax.ShapeDtypeStruct((rows, width), bf16),
            jax.ShapeDtypeStruct((width, rows), bf16),
            jax.ShapeDtypeStruct((rows, 128), f32),
        ],
        compiler_params=vmem(63),
        cost_estimate=cost(0, 24 * rows * width),
        name="prep",
    )(tokens, present.reshape(rows // tile, tile // 128, 128))


def conv_sites(pieces, first, place, fast, body):
    if not fast:
        return [(piece.at[0], first, 0) for piece in pieces]
    core, z, _ = place
    sites = []
    per = len(pieces) // 2
    for n, piece in enumerate(pieces):
        which = core if n < per else 1 - core
        kind = first + n % per
        for hop in range(piece.shape[0]):
            row = (((z - hop - (2 if kind == 4 else 0)) & 3) * 2 + which) * body
            sites.append((piece.at[hop], min(kind, 3), row))
    return sites


def conv_copies(sites, base, store, sems):
    copies = []
    for n, (source, kind, row) in enumerate(sites):
        start = pl.multiple_of(base(kind) + row, 16)
        copies.append(pltpu.make_async_copy(source, store.at[pl.ds(start, source.shape[0])], sems.at[n]))
    return copies


def conv_kernel(len_ref, place_ref, *refs, count, fast, body, wins):
    pieces = refs[:count]
    masked_ref, conv_ref, far_ref, near_ref, store, stack, even, odd, sems, out_sem = refs[count:]
    step = pl.program_id(0)
    rows, width = masked_ref.shape
    tile = conv_ref.shape[0]
    depth = store.shape[0] // (QUARTERS - 1)
    back = pltpu.make_async_copy(store, near_ref, out_sem)
    sites = conv_sites(pieces, 0, tuple(place_ref[i] for i in range(3)), fast, body)
    copies = conv_copies(sites, lambda kind: kind * depth, store, sems)

    @pl.when(step == 0)
    def _():
        for copy in copies:
            copy.start()
        lay_shifted(masked_ref, even, odd, 256)

    start = pl.multiple_of(step * tile, tile)
    position = lax.broadcasted_iota(jnp.int32, (tile, 128), 0) + start
    reach = window_reach(len_ref, position, wins, rows)
    per = depth // 128
    for tap in range(TAPS):
        offset = pl.multiple_of(start + tap // 2 * 2 * STEP, 2 * STEP)
        block = within((odd if tap % 2 else even)[pl.ds(offset, tile)], reach, tap)
        for lane in range(0, width, 128):
            chunk = (tap * width + lane) // 128
            seat = ((chunk // per) ^ place_ref[2]) * per + chunk % per
            stack[:, pl.ds(pl.multiple_of(seat * 128, 128), 128)] = block[:, lane : lane + 128]

    @pl.when(step == 0)
    def _():
        for copy in copies:
            copy.wait()
        back.start()

    far_ref[...] = stack[:, store.shape[0] :]
    conv_ref[...] = dot(stack[:, : store.shape[0]], store[...])

    @pl.when(step == pl.num_programs(0) - 1)
    def _():
        back.wait()


def conv_forward(lengths, place, pieces, masked, fast, body):
    rows, width = masked.shape
    depth = TAPS * width // QUARTERS
    tile = 512
    return pl.pallas_call(
        functools.partial(conv_kernel, count=len(pieces), fast=fast, body=body, wins=lengths.shape[1]),
        grid=(rows // tile,),
        in_specs=[SMEM, SMEM] + [ANY] * len(pieces) + [whole((rows, width))],
        out_specs=[rows_of(tile, width), rows_of(tile, depth), ANY],
        out_shape=[
            jax.ShapeDtypeStruct((rows, width), f32),
            jax.ShapeDtypeStruct((rows, depth), bf16),
            jax.ShapeDtypeStruct(((QUARTERS - 1) * depth, width), bf16),
        ],
        scratch_shapes=[
            pltpu.VMEM(((QUARTERS - 1) * depth, width), bf16),
            pltpu.VMEM((tile, QUARTERS * depth), bf16),
            pltpu.VMEM((rows + 2 * REACH, width), bf16),
            pltpu.VMEM((rows + 2 * REACH, width), bf16),
            pltpu.SemaphoreType.DMA((sum(piece.shape[0] for piece in pieces),)),
            pltpu.SemaphoreType.DMA,
        ],
        compiler_params=vmem(63),
        cost_estimate=cost(3 * depth * rows * width, 24 * rows * width),
        name="conv_forward",
    )(lengths, place, *pieces, masked)


def ff_copies(pieces, place, fast, store, sems):
    if not fast:
        return [pltpu.make_async_copy(pieces[0], store, sems.at[0])]
    core, own_z, dp = place
    per = len(pieces) // 2
    copies = []
    for n, piece in enumerate(pieces):
        which = core if n < per else 1 - core
        kind = n % per
        for hop in range(piece.shape[0]):
            z = (own_z - hop - (2 if kind == 4 else 0)) & 3
            block = ((dp ^ min(kind, 3)) * 4 + z) * 2 + which
            copies.append(pltpu.make_async_copy(piece.at[hop], store.at[block], sems.at[len(copies)]))
    return copies


def relay_seat(r, k):
    if k < 2:
        return (1, r // 2 * 2 + k) if r % 2 else (0, r // 2 * 2 + k)
    return (2, r % 2 * 2 + k - 2) if r // 2 else (0, 4 + r * 2 + k - 2)


def feed_kernel(place_ref, *refs, far, count, outs, tiles, chunk, inner_rows, outer_rows, extra, fast, body):
    far_pieces, ff_pieces = refs[:far], refs[far : far + count]
    refs = refs[far + count :]
    stacked_ref, partial_ref, tokens_ref, cot_ref = refs[:4]
    mixed_ref, d_hidden_ref, d_conv_ref, sums_ref, far_ref = refs[4:9]
    targets = refs[9 : 9 + outs]
    refs = refs[9 + outs :]
    packed, w_in, w_far, small_ref, bend, slope_ref, normed_ref, hiddens, actives, d_outers, d_inners = refs[:11]
    tallies, ff_sems, far_sems, grad_sems, out_sem = refs[11:]
    slab = SLAB
    store = packed
    step = pl.program_id(0)
    tile, width = tokens_ref.shape
    total = w_in.shape[1]
    blocks = packed.shape[0]
    cols = total // width
    place = tuple(place_ref[i] for i in range(3))
    core = place[0]
    depth = w_far.shape[0]
    top = cols * inner_rows
    back = pltpu.make_async_copy(w_far, far_ref, out_sem)

    @pl.when(step == 0)
    def _():
        copies = ff_copies(ff_pieces, place, fast, packed, ff_sems)
        far_sites = conv_sites(far_pieces, QUARTERS - 1, place, fast, body)
        copies += conv_copies(far_sites, lambda kind: 0, w_far, far_sems)
        for copy in copies:
            copy.start()
        tallies[...] = jnp.zeros_like(tallies)
        for copy in copies:
            copy.wait()
        back.start()
        for j in range(cols):
            part = packed[:, j * inner_rows : (j + 1) * inner_rows].reshape(blocks * inner_rows, width)
            w_in[:, j * width : (j + 1) * width] = part
        small_ref[...] = jnp.sum(packed[:, top : top + extra].astype(f32), axis=0)

    base = pl.multiple_of(jnp.minimum(step, tiles - 1) * tile, tile)

    def at(part):
        return pl.ds(pl.multiple_of(base + part.start, part.size), part.size)

    def add_tally(row, col, term):
        tallies[8 * row : 8 * row + 8, col : col + term.shape[1]] += fold(term)

    def out_rows(j):
        if outer_rows > chunk:
            per = outer_rows // chunk
            first = top + extra + j % per * chunk
            return packed[j // per, first : first + chunk]
        count = chunk // outer_rows
        return packed[j * count : (j + 1) * count, top + extra :].reshape(chunk, width)

    in_rows = step < tiles

    @pl.when(in_rows)
    def _():
        for part in slabs(tile, slab):
            conv = partial_ref[part] + dot(stacked_ref[part], w_far[...]) + small_ref[0:1]
            bent, slope = gelu_pair(conv)
            shifted = bent - mean(bent)
            root = lax.rsqrt(mean(shifted * shifted) + EPSILON)
            normed = shifted * root
            normed_ref[part] = normed
            slope_ref[part] = slope * root
            hiddens[at(part)] = (
                tokens_ref[part].astype(f32) + normed * small_ref[1:2] + small_ref[2:3]
            ).astype(bf16)

    for j in range(total // chunk):
        cut = slice(j * chunk, (j + 1) * chunk)

        @pl.when(in_rows)
        def _(j=j, cut=cut):
            for part in slabs(tile, slab):
                inner = dot(hiddens[at(part)], w_in[:, cut]) + small_ref[6 + j : 7 + j]
                act, slope = gelu_pair(inner)
                actives[at(part), cut] = act.astype(bf16)
                bend[part, cut] = slope

    @pl.when(in_rows)
    def _():
        gain_two = small_ref[4:5]
        for part in slabs(tile, slab // 2):
            full = packed[:, top + extra :].reshape(blocks * outer_rows, width)
            outer = dot(actives[at(part)], full) + small_ref[3:4]
            shifted = outer - mean(outer)
            root = lax.rsqrt(mean(shifted * shifted) + EPSILON)
            normal = shifted * root
            mixed_ref[part] = (hiddens[at(part)].astype(f32) + normal * gain_two + small_ref[5:6]).astype(bf16)
            cot = cot_ref[part].astype(f32)
            q = cot * gain_two
            d_outer_full = root * (q - mean(q) - normal * mean(q * normal))
            d_outers[at(part)] = d_outer_full.astype(bf16)
            add_tally(3, 0, d_outer_full)
            add_tally(4, 0, cot * normal)
            add_tally(5, 0, cot)

    for j in range(total // chunk):
        cut = slice(j * chunk, (j + 1) * chunk)

        @pl.when(in_rows)
        def _(j=j, cut=cut):
            for part in slabs(tile, slab):
                d_inner = dot_t(d_outers[at(part)], out_rows(j)) * bend[part, cut]
                d_inners[at(part), cut] = d_inner.astype(bf16)
                add_tally(6 + j, 0, d_inner)

    @pl.when(in_rows)
    def _():
        for part in slabs(tile, slab):
            d_hidden = dot_t(d_inners[at(part)], w_in[...]) + cot_ref[part].astype(f32)
            d_hidden_ref[part] = d_hidden
            first = normed_ref[part]
            p = d_hidden * small_ref[1:2]
            d_conv = slope_ref[part] * (p - mean(p) - first * mean(p * first))
            d_conv_ref[part] = d_conv.astype(bf16)
            add_tally(0, 0, d_conv)
            add_tally(1, 0, d_hidden * first)
            add_tally(2, 0, d_hidden)

    def put_blocks(dp):
        for r in range(4):

            @pl.when((dp ^ place[2]) == r)
            def _(r=r):
                for n, which in enumerate((core, 1 - core)):
                    for k in range(4):
                        array, seat = relay_seat(r, k)
                        target = targets[3 * n + array].at[seat]
                        block = (dp * 4 + ((place[1] + k) & 3)) * 2 + which
                        pltpu.make_async_copy(store.at[block], target, grad_sems.at[dp * 8 + 4 * n + k]).start()

    @pl.when(step == tiles)
    def _():
        for row in range(sums_ref.shape[0]):
            sums_ref[row : row + 1] = colsum(tallies[8 * row : 8 * row + 8])
        if fast:
            head = sums_ref[:6].astype(bf16)
            rest = jnp.zeros((extra - 7, width), bf16)
            for dp in range(blocks // 8):
                line = jnp.concatenate([head, sums_ref[6 + dp : 7 + dp].astype(bf16), rest])
                store[8 * dp : 8 * dp + 8, top : top + extra] = jnp.broadcast_to(line, (8, extra, width))

    for j in range(cols):
        part = slice(j * width, (j + 1) * width)

        @pl.when(step == tiles)
        def _(j=j, part=part):
            d_in = dot_rows(hiddens[...], d_inners[:, part]).astype(bf16)
            store[:, j * inner_rows : (j + 1) * inner_rows] = d_in.reshape(blocks, inner_rows, width)

    for j in range(cols):
        part = slice(j * width, (j + 1) * width)

        @pl.when(step == tiles)
        def _(j=j, part=part):
            d_out = dot_rows(actives[:, part], d_outers[...]).astype(bf16)
            first = top + extra
            if fast:
                many = width // outer_rows
                store[j * many : (j + 1) * many, first : first + outer_rows] = d_out.reshape(many, outer_rows, width)
                put_blocks(j)
            else:
                per = outer_rows // width
                start = first + j % per * width
                store[j // per, start : start + width] = d_out

    @pl.when(step == pl.num_programs(0) - 1)
    def _():
        back.wait()
        if fast:
            for n in range(blocks):
                pltpu.make_async_copy(store.at[n], targets[0].at[0], grad_sems.at[n]).wait()
        else:
            copies = [
                pltpu.make_async_copy(store.at[pl.ds(n, 1)], target, grad_sems.at[n]) for n, target in enumerate(targets)
            ]
            for copy in copies:
                copy.start()
            for copy in copies:
                copy.wait()


def feed(place, far, pieces, stacked, partial, tokens, cotangent, inner_rows, outer_rows, extra, total, fast, body):
    rows, width = tokens.shape
    blocks = width // inner_rows
    tile = 512
    tiles, cols = rows // tile, total // width
    share = cols * inner_rows + extra + outer_rows
    depth = stacked.shape[1]
    seats = (8, 4, 4) * 2 if fast else (1, 1)
    tall = pl.BlockSpec((tile, width), lambda i: (jnp.minimum(i, tiles - 1), 0))
    last = pl.BlockSpec((tile, depth), lambda i: (jnp.minimum(i, tiles - 1), 0))
    return pl.pallas_call(
        functools.partial(
            feed_kernel, far=len(far), count=len(pieces), outs=len(seats), tiles=tiles, chunk=512, inner_rows=inner_rows,
            outer_rows=outer_rows, extra=extra, fast=fast, body=body,
        ),
        grid=(tiles + 1,),
        in_specs=[SMEM] + [ANY] * (len(far) + len(pieces)) + [last, tall, tall, tall],
        out_specs=[tall, tall, tall, pl.BlockSpec((16, width), lambda i: (0, 0)), ANY] + [ANY] * len(seats),
        out_shape=[
            jax.ShapeDtypeStruct((rows, width), bf16),
            jax.ShapeDtypeStruct((rows, width), f32),
            jax.ShapeDtypeStruct((rows, width), bf16),
            jax.ShapeDtypeStruct((16, width), f32),
            jax.ShapeDtypeStruct((depth, width), bf16),
        ] + [jax.ShapeDtypeStruct((count, share, width), bf16) for count in seats],
        scratch_shapes=[
            pltpu.VMEM((blocks, share, width), bf16),
            pltpu.VMEM((width, total), bf16),
            pltpu.VMEM((depth, width), bf16),
            pltpu.VMEM((extra, width), f32),
            pltpu.VMEM((tile, total), f32),
            pltpu.VMEM((tile, width), f32),
            pltpu.VMEM((tile, width), f32),
            pltpu.VMEM((rows, width), bf16),
            pltpu.VMEM((rows, total), bf16),
            pltpu.VMEM((rows, width), bf16),
            pltpu.VMEM((rows, total), bf16),
            pltpu.VMEM((8 * extra, width), f32),
            pltpu.SemaphoreType.DMA((sum(piece.shape[0] for piece in pieces),)),
            pltpu.SemaphoreType.DMA((sum(piece.shape[0] for piece in far),)),
            pltpu.SemaphoreType.DMA((blocks,)),
            pltpu.SemaphoreType.DMA,
        ],
        compiler_params=vmem(63),
        cost_estimate=cost(6 * rows * width * total, 40 * rows * width),
        name="feed",
    )(place, *far, *pieces, stacked, partial, tokens, cotangent)


def lay_shifted(values_ref, even, odd, tile):
    rows, width = values_ref.shape
    zeros = jnp.zeros((REACH, width), bf16)
    even[:REACH] = zeros
    even[rows + REACH :] = zeros
    odd[:REACH] = zeros
    odd[rows:] = jnp.zeros((2 * REACH, width), bf16)
    for r in range(0, rows, tile):
        block = values_ref[r : r + tile]
        even[REACH + r : REACH + r + tile] = block
        odd[REACH - STEP + r : REACH - STEP + r + tile] = block


def tap_products(len_ref, place, masked_ref, even, odd, part, targets, store, sems, *, wins, blocks, body, turn):
    channels, rows = masked_ref.shape
    width = part.stop - part.start
    core = place[0]
    position = lax.broadcasted_iota(jnp.int32, (rows, 128), 0)
    reach = window_reach(len_ref, position, wins, rows)
    copies = []
    for tap in range(TAPS):
        mirror = TAPS - 1 - tap
        source = (odd if mirror % 2 else even)[mirror // 2 * 2 * STEP : mirror // 2 * 2 * STEP + rows, part]
        store[tap * channels : (tap + 1) * channels] = dot(masked_ref[...], within(source, reach, mirror)).astype(bf16)
        while len(copies) // 2 < blocks and (len(copies) // 2 + 1) * 2 * body <= (tap + 1) * channels:
            block = len(copies) // 2
            seat = ((block // 4) ^ turn) * 4 + ((block % 4 - place[1]) & 3) if blocks == 16 else block
            for n, (target, which) in enumerate(zip(targets, (core, 1 - core))):
                start = pl.multiple_of((2 * block + which) * body, 16)
                copies.append(pltpu.make_async_copy(store.at[pl.ds(start, body)], target.at[seat], sems.at[n, block]))
                copies[-1].start()
    for copy in copies:
        copy.wait()


def conv_grad_kernel(len_ref, place_ref, masked_ref, d_conv_ref, keep_ref, send_ref, even, odd, store, sems, *, wins, blocks, body):
    lay_shifted(d_conv_ref, even, odd, 256)
    tap_products(
        len_ref, tuple(place_ref[i] for i in range(3)), masked_ref, even, odd, slice(0, d_conv_ref.shape[1]),
        (keep_ref, send_ref), store, sems, wins=wins, blocks=blocks, body=body, turn=0,
    )


def conv_grad(lengths, place, masked, d_conv, blocks, body):
    channels, rows = masked.shape
    width = d_conv.shape[1]
    return pl.pallas_call(
        functools.partial(conv_grad_kernel, wins=lengths.shape[1], blocks=blocks, body=body),
        grid=(1,),
        in_specs=[SMEM, SMEM, whole(masked.shape), whole((rows, width))],
        out_specs=[ANY, ANY],
        out_shape=[jax.ShapeDtypeStruct((blocks, body, width), bf16)] * 2,
        scratch_shapes=[
            pltpu.VMEM((rows + 2 * REACH, width), bf16),
            pltpu.VMEM((rows + 2 * REACH, width), bf16),
            pltpu.VMEM((TAPS * channels, width), bf16),
            pltpu.SemaphoreType.DMA((2, blocks)),
        ],
        compiler_params=vmem(63),
        cost_estimate=cost(TAPS * rows * width * channels, 12 * rows * width),
        name="conv_grad",
    )(lengths, place, masked, d_conv)


def token_grad_kernel(
    len_ref, place_ref, near_ref, far_ref, d_conv_ref, d_hidden_ref, keep_ref, d_tokens_ref, even, odd, store, sems, *, wins, tile
):
    step = pl.program_id(0)
    rows, width = d_conv_ref.shape
    depth = far_ref.shape[0]

    @pl.when(step == 0)
    def _():
        copies = []
        for kind in range(QUARTERS):
            source = far_ref if kind == QUARTERS - 1 else near_ref.at[pl.ds(kind * depth, depth)]
            start = pl.multiple_of((place_ref[2] ^ kind) * depth, 128)
            copies.append(pltpu.make_async_copy(source, store.at[pl.ds(start, depth)], sems.at[kind]))
        for copy in copies:
            copy.start()
        lay_shifted(d_conv_ref, even, odd, 256)
        for copy in copies:
            copy.wait()

    start = pl.multiple_of(step * tile, tile)
    position = lax.broadcasted_iota(jnp.int32, (tile, 128), 0) + start
    reach = window_reach(len_ref, position, wins, rows)
    total = None
    for tap in range(TAPS):
        mirror = TAPS - 1 - tap
        offset = pl.multiple_of(start + mirror // 2 * 2 * STEP, 2 * STEP)
        block = within((odd if mirror % 2 else even)[pl.ds(offset, tile)], reach, mirror)
        term = dot_t(block, store[tap * width : (tap + 1) * width])
        total = term if total is None else total + term
    d_tokens_ref[...] = d_hidden_ref[...] + total * wide(keep_ref[...], width)


def token_grad(lengths, place, near, far, d_conv, d_hidden, keep):
    rows, width = d_conv.shape
    tile = 512
    return pl.pallas_call(
        functools.partial(token_grad_kernel, wins=lengths.shape[1], tile=tile),
        grid=(rows // tile,),
        in_specs=[SMEM, SMEM, ANY, ANY, whole((rows, width)), rows_of(tile, width), rows_of(tile, 128)],
        out_specs=rows_of(tile, width),
        out_shape=jax.ShapeDtypeStruct((rows, width), f32),
        scratch_shapes=[
            pltpu.VMEM((rows + 2 * REACH, width), bf16),
            pltpu.VMEM((rows + 2 * REACH, width), bf16),
            pltpu.VMEM((TAPS * width, width), bf16),
            pltpu.SemaphoreType.DMA((QUARTERS,)),
        ],
        compiler_params=vmem(63),
        cost_estimate=cost(TAPS * rows * width * width, 12 * rows * width),
        name="token_grad",
    )(lengths, place, near, far, d_conv, d_hidden, keep)


def on_device(
    n_dp, n_fsdp, tokens, present, lengths, conv_w, conv_b, gain_one, shift_one, w_in, b_in, w_out, b_out, gain_two, shift_two, cotangent
):
    rows, width = tokens.shape
    total = w_in.shape[1]
    cols = total // width
    devices = n_dp * n_fsdp
    fast = n_dp == 4 and n_fsdp == 8 and conv_w.shape[0] % 16 == 0 and w_in.shape[0] % 16 == 0
    bar = lax.optimization_barrier
    extra = 16
    n = width // devices
    swap = [(i, i ^ 1) for i in range(n_fsdp)]
    across = {r: [(i, i ^ r) for i in range(n_dp)] for r in (1, 2, 3)}
    along = {k: [(i, (i + 2 * k) % n_fsdp) for i in range(n_fsdp)] for k in (1, 2, 3)}
    vectors = (conv_b, gain_one, shift_one, b_out, gain_two, shift_two)
    if fast:
        fsdp = lax.axis_index("fsdp").astype(jnp.int32)
        dp = lax.axis_index("dp").astype(jnp.int32)
        place = jnp.stack([fsdp & 1, fsdp >> 1, dp])
        body = conv_w.shape[0]
        inner_rows, outer_rows = w_in.shape[0], w_out.shape[0]
        blocks = devices // 2

        def from_column(shard):
            return [shard] + [lax.ppermute(shard, "fsdp", along[k]) for k in (1, 2, 3)]

        column = jnp.stack(from_column(conv_w))
        seat = dp * n_fsdp + fsdp
        lane = jnp.arange(width, dtype=jnp.int32)
        line = jnp.arange(extra, dtype=jnp.int32)[:, None]
        lines = jnp.concatenate(
            [jnp.tile(jnp.stack(vectors), (1, devices))]
            + [jnp.tile(b_in, width // b_in.shape[0])[None]] * cols
            + [jnp.zeros((extra - 6 - cols, width), bf16)]
        )
        few = b_in.shape[0]
        own_line = ((line < 6) & (lane // n == seat)) | ((line == 6 + dp) & (lane // few == fsdp))
        lines = jnp.where(own_line, lines, 0)
        ff_own = jnp.concatenate([w_in[:, j * width : (j + 1) * width] for j in range(cols)] + [lines, w_out], axis=0)
        masked, masked_across, keep = prep(tokens, present)
        column, ff_own, masked, masked_across, keep, place = bar((column, ff_own, masked, masked_across, keep, place))
        beside_x = lax.ppermute(column, "dp", across[1])
        beside_y = lax.ppermute(column, "dp", across[2])
        ff_rest = from_column(ff_own)
        ff_column = jnp.stack(ff_rest)
        column, beside_x, beside_y, ff_column = bar((column, beside_x, beside_y, ff_column))
        near = (column, beside_x, beside_y)
        near = near + tuple(lax.ppermute(piece, "fsdp", swap) for piece in near)
        far = (
            lax.ppermute(beside_x[:2], "dp", across[2]),
            lax.ppermute(beside_y[2:], "dp", across[1]),
        )
        ff = (ff_column, lax.ppermute(ff_column, "dp", across[1]), lax.ppermute(ff_column, "dp", across[2]))
    else:
        place = jnp.zeros((3,), jnp.int32)
        gather = functools.partial(lax.all_gather, axis_name=AXES, axis=0, tiled=True)
        full = gather(conv_w)
        body = full.shape[0] // 2
        depth = full.shape[0] // QUARTERS * (QUARTERS - 1)
        near, far = (full[None, :depth],), (full[None, depth:],)
        lines = [gather(vector) for vector in vectors] + list(gather(b_in).reshape(cols, width))
        lines = jnp.stack(lines + [jnp.zeros_like(lines[0])] * (extra - len(lines)))
        full_in, full_out = gather(w_in), gather(w_out)
        inner_rows, outer_rows = full_in.shape[0] // 2, full_out.shape[0] // 2
        blocks = 1
        ff = [full_in[:, j * width : (j + 1) * width].reshape(2, inner_rows, width) for j in range(cols)]
        ff.append(jnp.stack([lines, jnp.zeros_like(lines)]))
        ff = (jnp.concatenate(ff + [full_out.reshape(2, outer_rows, width)], axis=1),)
        masked, masked_across, keep = prep(tokens, present)

    partial, stacked, w_near = conv_forward(lengths, place, near, masked, fast, body)
    if fast:
        far, ff, partial = bar((far, ff, partial))
        ff = ff + (
            lax.ppermute(ff[1][:2], "dp", across[2]),
            lax.ppermute(ff[2][2:], "dp", across[1]),
        )
        far = far + tuple(lax.ppermute(piece, "fsdp", swap) for piece in far)
        ff = ff + tuple(lax.ppermute(piece, "fsdp", swap) for piece in ff)
    mixed, d_hidden, d_conv, sums, w_far, *ff_grads = feed(
        place, far, ff, stacked, partial, tokens, cotangent, inner_rows, outer_rows, extra, total, fast, body
    )
    def added(terms):
        return sum(term.astype(f32) for term in terms)

    def line_swap(line):
        return [line[0]] + [lax.ppermute(line[k], "fsdp", along[k]) for k in (1, 2, 3)]

    def rounded(*terms):
        return added(terms).astype(bf16)

    if fast:
        ff_near, ff_far_a, ff_far_b = ff_grads[:3]
        came_a, came_b, came = (lax.ppermute(ff_grads[3 + n], "fsdp", swap) for n in (1, 2, 0))
        a_far, b_far, d_conv = bar((ff_far_a + came_a, ff_far_b + came_b, d_conv))
        a_came = lax.ppermute(a_far, "dp", across[1])
        b_came = lax.ppermute(b_far, "dp", across[2])
        conv_keep, conv_send = conv_grad(lengths, place, masked_across, d_conv, blocks, body)
        a_came, b_came, came, conv_keep, conv_send, d_conv = bar((a_came, b_came, came, conv_keep, conv_send, d_conv))
        conv_came = lax.ppermute(conv_send, "fsdp", swap)
        a_last = lax.ppermute(rounded(ff_near[2:4], came[2:4], a_came[2:]), "dp", across[2])
        b_last = lax.ppermute(rounded(ff_near[6:], came[6:], b_came[2:]), "dp", across[1])
        conv_chip = conv_keep + conv_came
        conv_chip, a_last, b_last, d_conv = bar((conv_chip, a_last, b_last, d_conv))
        conv_plane = lax.all_to_all(conv_chip.reshape(4, 4, body, width), "dp", 0, 0, tiled=True)
        line = [rounded(ff_near[k], came[k], a_came[k], a_last[k]) for k in (0, 1)]
        line += [rounded(ff_near[4 + k], came[4 + k], b_came[k], b_last[k]) for k in (0, 1)]
        ff_line = line_swap(line)
        d_tokens = token_grad(lengths, place, w_near, w_far, d_conv, d_hidden, keep)
        d_tokens, ff_line, conv_plane = bar((d_tokens, ff_line, conv_plane))
        conv_line = line_swap([added(conv_plane[r, k] for r in range(4)).astype(bf16) for k in range(4)])
        ff_share = added(ff_line)
        d_conv_w = added(conv_line)
        top = cols * inner_rows
        d_w_in = jnp.concatenate([ff_share[j * inner_rows : (j + 1) * inner_rows] for j in range(cols)], axis=1)
        d_w_out = ff_share[top + extra :]
        seat = dp * n_fsdp + fsdp
        own = lax.dynamic_slice(ff_share[top : top + 6], (0, seat * n), (6, n))
        vector_grads = list(own)
        vector_grads.append(lax.dynamic_slice(ff_share[top + 6], (fsdp * few,), (few,)))
    else:
        conv_pair = conv_grad(lengths, place, masked_across, d_conv, blocks, body)
        d_tokens = token_grad(lengths, place, w_near, w_far, d_conv, d_hidden, keep)
        ff_share = jnp.concatenate(ff_grads, axis=0)
        scatter = functools.partial(lax.psum_scatter, axis_name=AXES, scatter_dimension=0, tiled=True)
        d_in_full = jnp.concatenate(
            [ff_share[:, j * inner_rows : (j + 1) * inner_rows].reshape(-1, width) for j in range(cols)], axis=1
        )
        d_w_in = scatter(d_in_full.astype(f32))
        d_w_out = scatter(ff_share[:, cols * inner_rows + extra :].reshape(-1, width).astype(f32))
        d_conv_w = scatter(jnp.concatenate(conv_pair, axis=0).reshape(-1, width).astype(f32))
        vector_grads = [scatter(line) for line in sums[:6]] + [scatter(sums[6 : 6 + cols].reshape(-1))]
    d_conv_b, d_gain_one, d_shift_one, d_b_out, d_gain_two, d_shift_two, d_b_in = vector_grads
    return (
        mixed, d_tokens, d_conv_w, d_conv_b, d_gain_one, d_shift_one, d_w_in, d_b_in, d_w_out, d_b_out, d_gain_two, d_shift_two
    )


def solution(mesh):
    both = P(AXES)
    flat = P(AXES, None)
    in_specs = (flat, both, flat, flat, both, both, both, flat, both, flat, both, both, both, flat)
    out_specs = (flat, flat, flat, both, both, both, flat, both, flat, both, both, both)
    return jax.shard_map(
        functools.partial(on_device, mesh.shape["dp"], mesh.shape["fsdp"]),
        mesh=mesh,
        in_specs=in_specs,
        out_specs=out_specs,
        check_vma=False,
    )
```
